32 devices in a mesh: dp: 16 (over z, x, core), blk: 2 (over y).
Axes of the slice: x: 2, y: 2, z: 4, core: 2. Of those that a mesh axis runs over, the one named last changes fastest.
Arguments:
- hidden_in: bfloat16 [32, 512, 768], P('dp', 'blk'), may hold values from -6 to 6
- page_lengths: int32 [32], P('dp'), may hold values from 40 to 512, as said below
- pad_mask: int32 [32, 512], P('dp', 'blk'), may hold values from 0 to 1, as said below
- query_weight: bfloat16 [768, 768], P(('dp', 'blk')), may hold values from -0.21875 to 0.21875
- query_bias: bfloat16 [768], P(('dp', 'blk')), may hold values from -1.1953125 to 1.1953125
- key_weight: bfloat16 [768, 768], P(('dp', 'blk')), may hold values from -0.21875 to 0.21875
- value_weight: bfloat16 [768, 768], P(('dp', 'blk')), may hold values from -0.21875 to 0.21875
- value_bias: bfloat16 [768], P(('dp', 'blk')), may hold values from -3 to 3
- output_weight: bfloat16 [768, 768], P(('dp', 'blk')), may hold values from -1.25 to 1.25
- output_bias: bfloat16 [768], P(('dp', 'blk')), may hold values from -3 to 3
- first_gain: bfloat16 [768], P(('dp', 'blk')), may hold values from 0.5 to 1.5
- first_shift: bfloat16 [768], P(('dp', 'blk')), may hold values from -3 to 3
- inner_weight: bfloat16 [768, 3072], P(('dp', 'blk')), may hold values from -0.21875 to 0.21875
- inner_bias: bfloat16 [3072], P(('dp', 'blk')), may hold values from -3 to 3
- outer_weight: bfloat16 [3072, 768], P(('dp', 'blk')), may hold values from -0.109375 to 0.109375
- outer_bias: bfloat16 [768], P(('dp', 'blk')), may hold values from -3 to 3
- second_gain: bfloat16 [768], P(('dp', 'blk')), may hold values from 0.5 to 1.5
- second_shift: bfloat16 [768], P(('dp', 'blk')), may hold values from -3 to 3
- out_grad: bfloat16 [32, 512, 768], P('dp', 'blk'), may hold values from -6 to 6
Outputs:
- output: bfloat16 [32, 512, 768], P('dp', 'blk')
- input_grad: bfloat16 [32, 512, 768], P('dp', 'blk')
- query_weight_grad: float32 [768, 768], P(('dp', 'blk'))
- query_bias_grad: float32 [768], P(('dp', 'blk'))
- key_weight_grad: float32 [768, 768], P(('dp', 'blk'))
- value_weight_grad: float32 [768, 768], P(('dp', 'blk'))
- value_bias_grad: float32 [768], P(('dp', 'blk'))
- output_weight_grad: float32 [768, 768], P(('dp', 'blk'))
- output_bias_grad: float32 [768], P(('dp', 'blk'))
- first_gain_grad: float32 [768], P(('dp', 'blk'))
- first_shift_grad: float32 [768], P(('dp', 'blk'))
- inner_weight_grad: float32 [768, 3072], P(('dp', 'blk'))
- inner_bias_grad: float32 [3072], P(('dp', 'blk'))
- outer_weight_grad: float32 [3072, 768], P(('dp', 'blk'))
- outer_bias_grad: float32 [768], P(('dp', 'blk'))
- second_gain_grad: float32 [768], P(('dp', 'blk'))
- second_shift_grad: float32 [768], P(('dp', 'blk'))
The draws below stay inside these ranges and needn't reach their ends.
Inputs may be any that keep to these rules, and one draw needn't show every extreme that they name: `page_lengths`: among the 2 pages of each index of dp, at least one has exactly 512 real tokens. `pad_mask`: position 0 of every page is 1.
All inputs are finite; a program needn't handle non-finite values.
Results may differ from the reference program's by a relative error of at most 0.014.
Values may be sent and summed in bfloat16 or wider, within the bound.
A program may use at most 192 MiB of HBM per device.

```python
import math
import jax
import jax.numpy as jnp
from jax import lax

D = 768
HEADS = 12
HEAD_DIM = 64
FF = 3072
SEQ = 512
PAGES_DEV = 2
MIN_LEN = 40
PAGES = 32
N_DP = 16


def draw_page_lengths(key, part):
    key = jax.random.fold_in(key, 11)
    first_key, second_key = jax.random.split(key)
    lengths = jax.random.randint(first_key, (N_DP, PAGES_DEV), MIN_LEN, SEQ + 1)
    chosen = jax.random.randint(second_key, (N_DP, 1), 0, PAGES_DEV)
    column = jnp.arange(PAGES_DEV, dtype=jnp.int32)[None, :]
    lengths = jnp.where(column == chosen, SEQ, lengths)
    return lengths.reshape(PAGES).astype(jnp.int32)


def draw_pad_mask(key, part):
    key = jax.random.fold_in(key, 23)
    levels = jax.random.randint(key, (PAGES, SEQ), 0, 8)
    marks = (levels > 0).astype(jnp.int32)
    column = jnp.arange(SEQ, dtype=jnp.int32)[None, :]
    return jnp.where(column == 0, 1, marks).astype(jnp.int32)


def shard_levels(key, dims, cuts, least, high):
    def one(position, shards_of):
        steps = jax.random.uniform(jax.random.fold_in(jax.random.fold_in(key, 6), position), (shards_of,), jnp.float32, least / len(cuts), high / len(cuts))
        return jnp.repeat(jnp.exp(steps), dims[position] // shards_of).reshape((-1,) + (1,) * (len(dims) - position - 1))

    loudness = one(*cuts[0])
    for cut in cuts[1:]:
        loudness = loudness * one(*cut)
    return loudness


def gaussian(own_key, extent, spread, reach, cuts=(), kind=jnp.bfloat16):
    values = spread * jax.random.normal(own_key, extent, jnp.float32)
    if cuts:
        values = values * shard_levels(own_key, extent, cuts, -0.22, 0.18)
    return jnp.clip(values, -reach, reach).astype(kind)


def setup_inputs(seed: int = 0) -> dict:
    streams_of = jax.random.split(jax.random.key(seed), 20)
    return {
        "hidden_in": gaussian(streams_of[0], (PAGES, SEQ, D), 1.0, 6.0, ((0, 16), (1, 2))),
        "page_lengths": draw_page_lengths(jax.random.fold_in(streams_of[19], 71), 0),
        "pad_mask": draw_pad_mask(jax.random.fold_in(streams_of[19], 71), 0),
        "query_weight": gaussian(streams_of[3], (D, D), D ** -0.5, 0.21875, ((0, 32),)),
        "query_bias": gaussian(streams_of[4], (D,), 0.2, 1.1953125, ((0, 32),)),
        "key_weight": gaussian(streams_of[5], (D, D), D ** -0.5, 0.21875, ((0, 32),)),
        "value_weight": gaussian(streams_of[6], (D, D), D ** -0.5, 0.21875, ((0, 32),)),
        "value_bias": gaussian(streams_of[7], (D,), 0.5, 3.0, ((0, 32),)),
        "output_weight": gaussian(streams_of[8], (D, D), (D // 32) ** -0.5, 1.25, ((0, 32),)),
        "output_bias": gaussian(streams_of[9], (D,), 0.5, 3.0, ((0, 32),)),
        "first_gain": jnp.clip(1.0 + 0.1 * jax.random.normal(streams_of[10], (D,), jnp.float32), 0.5, 1.5).astype(jnp.bfloat16),
        "first_shift": gaussian(streams_of[11], (D,), 0.5, 3.0, ((0, 32),)),
        "inner_weight": gaussian(streams_of[12], (D, FF), D ** -0.5, 0.21875, ((0, 32),)),
        "inner_bias": gaussian(streams_of[13], (FF,), 0.5, 3.0, ((0, 32),)),
        "outer_weight": gaussian(streams_of[14], (FF, D), FF ** -0.5, 0.109375, ((0, 32),)),
        "outer_bias": gaussian(streams_of[15], (D,), 0.5, 3.0, ((0, 32),)),
        "second_gain": jnp.clip(1.0 + 0.1 * jax.random.normal(streams_of[16], (D,), jnp.float32), 0.5, 1.5).astype(jnp.bfloat16),
        "second_shift": gaussian(streams_of[17], (D,), 0.5, 3.0, ((0, 32),)),
        "out_grad": gaussian(streams_of[18], (PAGES, SEQ, D), 1.0, 6.0, ((0, 16), (1, 2))),
    }


@jax.custom_vjp
def low(v):
    return lax.optimization_barrier(v.astype(jnp.bfloat16)).astype(jnp.float32)

@jax.custom_vjp
def low_back(v):
    return v

def low_keep(v):
    return (low(v), None)

def low_pass(kept, grad):
    return (grad,)

def back_keep(v):
    return (v, None)

def back_low(kept, grad):
    return (low(grad),)
low.defvjp(low_keep, low_pass)
low_back.defvjp(back_keep, back_low)
NEG_FILL = -1000000000.0
EPSILON = 1e-05

def dense(left, right):
    return jnp.dot(left, right, precision=lax.Precision.HIGHEST, preferred_element_type=jnp.float32)

def layer_norm(values, gain, shift):
    center = values - lax.optimization_barrier(jnp.mean(values, axis=-1, keepdims=True))
    inverse = lax.rsqrt(lax.optimization_barrier(jnp.mean(center * center, axis=-1, keepdims=True)) + EPSILON)
    return center * inverse * gain + shift

def layer(values, live, query_weight, query_bias, key_weight, value_weight, value_bias, output_weight, output_bias, first_gain, first_shift, inner_weight, inner_bias, outer_weight, outer_bias, second_gain, second_shift):
    pages = values.shape[0]
    flat = values.reshape(pages * SEQ, D)
    shape4 = (pages, SEQ, HEADS, HEAD_DIM)
    queries = low(low_back(dense(flat, query_weight) + query_bias)).reshape(shape4)
    keys = low(low_back(dense(flat, key_weight))).reshape(shape4)
    vals = low(low_back(dense(flat, value_weight) + value_bias)).reshape(shape4)
    scores = jnp.einsum('gqhd,gkhd->ghqk', queries, keys, precision=lax.Precision.HIGHEST) * HEAD_DIM ** (-0.5)
    scores = jnp.where(live[:, None, None, :], scores, NEG_FILL)
    scores = low_back(scores)
    top = lax.optimization_barrier(jnp.max(scores, axis=-1, keepdims=True))
    expos = jnp.exp(scores - top)
    probs = low(expos / lax.optimization_barrier(jnp.sum(expos, axis=-1, keepdims=True)))
    context = jnp.einsum('ghqk,gkhd->gqhd', probs, vals, precision=lax.Precision.HIGHEST)
    context = low(low_back(context)).reshape(pages * SEQ, D)
    attended = low_back(dense(context, output_weight) + output_bias)
    hidden = low(layer_norm(flat + attended, first_gain, first_shift))
    inner = low_back(dense(hidden, inner_weight) + inner_bias)
    activated = low(jax.nn.gelu(inner, approximate=False))
    outer = low_back(dense(activated, outer_weight) + outer_bias)
    return layer_norm(hidden + outer, second_gain, second_shift).reshape(pages, SEQ, D)

def reference(hidden_in, page_lengths, pad_mask, query_weight, query_bias, key_weight, value_weight, value_bias, output_weight, output_bias, first_gain, first_shift, inner_weight, inner_bias, outer_weight, outer_bias, second_gain, second_shift, out_grad):
    params = tuple((weight.astype(jnp.float32) for weight in (query_weight, query_bias, key_weight, value_weight, value_bias, output_weight, output_bias, first_gain, first_shift, inner_weight, inner_bias, outer_weight, outer_bias, second_gain, second_shift)))
    positions = jnp.arange(SEQ, dtype=jnp.int32)
    live = (positions[None, :] < page_lengths[:, None]) & (pad_mask == 1)
    group = math.gcd(PAGES, 8)
    count = PAGES // group
    inputs = hidden_in.astype(jnp.float32).reshape(count, group, SEQ, D)
    cotans = out_grad.astype(jnp.float32).reshape(count, group, SEQ, D)
    lives = live.reshape(count, group, SEQ)

    def one_group(carry, items):
        block_in, block_live, block_cot = items

        def forward(values, *weights):
            return layer(values, block_live, *weights)
        result, pullback = jax.vjp(forward, block_in, *params)
        grads = pullback(block_cot)
        carry = tuple((summed + fresh for summed, fresh in zip(carry, grads[1:])))
        return (carry, (result, grads[0]))
    start = tuple((jnp.zeros_like(weight) for weight in params))
    totals, (results, input_grads) = lax.scan(one_group, start, (inputs, lives, cotans))
    return (results.reshape(PAGES, SEQ, D).astype(jnp.bfloat16), input_grads.reshape(PAGES, SEQ, D).astype(jnp.bfloat16), totals[0], totals[1], totals[2], totals[3], totals[4], totals[5], totals[6], totals[7], totals[8], totals[9], totals[10], totals[11], totals[12], totals[13], totals[14])
```

```python
from functools import partial

import jax
import jax.numpy as jnp
from jax import lax
from jax.experimental import pallas as pl
from jax.experimental.pallas import tpu as pltpu
from jax.sharding import PartitionSpec as P

HEADS = 12
NEG_FILL = -1000000000.0
EPSILON = 1e-05

NZ, NX, NC, NY = 4, 2, 2, 2
GROUP = NZ * NX * NC
CHUNKS = 6
ROWS, COLS = 96, 384
CUT = 64
WIDTH = 768
BF, F32 = jnp.bfloat16, jnp.float32


def rem(a, b):
    return lax.rem(a, b)


class Place:
    def __init__(self, stride):
        dp = lax.axis_index("dp")
        self.y = lax.axis_index("blk")
        index = dp // stride
        self.low = dp - index * stride
        self.stride = stride
        self.z = index // (NX * NC)
        self.x = (index // NC) % NX
        self.c = index % NC
        self.ox, self.oy, self.oc = 1 - self.x, 1 - self.y, 1 - self.c

    def dev(self, z, x, c, y):
        return ((z * (NX * NC) + x * NC + c) * self.stride + self.low, y)

    def above(self, k):
        return rem(self.z + k, NZ)

    def below(self, k):
        return rem(self.z + NZ - k, NZ)

    def to_z(self, k):
        return self.dev(self.above(k), self.x, self.c, self.y)

    @property
    def to_x(self):
        return self.dev(self.z, self.ox, self.c, self.y)

    @property
    def to_y(self):
        return self.dev(self.z, self.x, self.c, self.oy)

    @property
    def to_c(self):
        return self.dev(self.z, self.x, self.oc, self.y)

    def greet(self):
        barrier = pltpu.get_barrier_semaphore()
        partners = [self.to_z(k) for k in range(1, NZ)] + [self.to_x, self.to_y, self.to_c]
        for who in partners:
            pl.semaphore_signal(barrier, inc=1, device_id=who, device_id_type=pl.DeviceIdType.MESH)
        pl.semaphore_wait(barrier, len(partners))


def remote(src, dst, sems, index, who):
    send, recv = sems
    return pltpu.make_async_remote_copy(
        src_ref=src,
        dst_ref=dst,
        send_sem=send.at[index],
        recv_sem=recv.at[index],
        device_id=who,
        device_id_type=pl.DeviceIdType.MESH,
    )


def loop(count, body):
    def step(i, carry):
        body(i)
        return carry

    lax.fori_loop(0, count, step, 0)


class Gather:
    def __init__(self, at, blocks, zs, p1, p2, cs):
        self.at, self.g = at, blocks
        self.zs, self.p1, self.p2, self.cs = zs, p1, p2, cs

    def z_copy(self, ch, k, mine=True):
        at = self.at
        z = at.z if mine else at.below(k)
        ref = self.g.at[ch, z, at.x, at.c, at.y]
        return remote(ref, ref, self.zs, (ch, k - 1), at.to_z(k))

    def p1_copies(self, ch, k, mine=True):
        at = self.at
        z = at.below(k)
        x, y = (at.x, at.y) if mine else (at.ox, at.oy)
        over_x = self.g.at[ch, z, x, at.c, at.y]
        over_y = self.g.at[ch, z, at.x, at.c, y]
        return (
            remote(over_x, over_x, self.p1, (ch, k, 0), at.to_x),
            remote(over_y, over_y, self.p1, (ch, k, 1), at.to_y),
        )

    def p2_copies(self, ch, k, mine=True):
        at = self.at
        z = at.below(k)
        head, tail = pl.ds(0, CUT), pl.ds(CUT, ROWS - CUT)
        if mine:
            over_x = self.g.at[ch, z, at.x, at.c, at.oy, head]
            over_y = self.g.at[ch, z, at.ox, at.c, at.y, tail]
        else:
            over_x = self.g.at[ch, z, at.ox, at.c, at.oy, head]
            over_y = self.g.at[ch, z, at.ox, at.c, at.oy, tail]
        return (
            remote(over_x, over_x, self.p2, (ch, k, 0), at.to_x),
            remote(over_y, over_y, self.p2, (ch, k, 1), at.to_y),
        )

    def c_copy(self, ch, mine=True):
        at = self.at
        ref = self.g.at[ch, :, :, at.c if mine else at.oc]
        return remote(ref, ref, self.cs, (ch,), at.to_c)

    def start_z(self, ch):
        for k in range(1, NZ):
            self.z_copy(ch, k).start()

    def start_own(self, ch):
        for copy in self.p1_copies(ch, 0):
            copy.start()

    def plane(self, ch):
        for k in range(1, NZ):
            self.z_copy(ch, k, False).wait_recv()
            for copy in self.p1_copies(ch, k):
                copy.start()

    def diagonal(self, ch):
        def one(k):
            from_x, from_y = self.p1_copies(ch, k, False)
            over_x, over_y = self.p2_copies(ch, k)
            from_y.wait_recv()
            over_x.start()
            from_x.wait_recv()
            over_y.start()

        loop(NZ, one)

    def cross(self, ch):
        def one(k):
            for copy in self.p2_copies(ch, k, False):
                copy.wait_recv()

        loop(NZ, one)
        self.c_copy(ch).start()

    def arrive(self, ch):
        self.c_copy(ch, False).wait_recv()

    def drain(self, ch):
        for k in range(1, NZ):
            self.z_copy(ch, k).wait_send()

        def one(k):
            for copy in self.p1_copies(ch, k) + self.p2_copies(ch, k):
                copy.wait_send()

        loop(NZ, one)
        self.c_copy(ch).wait_send()


def fold(wide):
    return jnp.concatenate([wide[:, :COLS], wide[:, COLS:]], axis=0)


def pack_weights(refs, put):
    q, k, v, o, inner, outer = refs
    units = [r[...].astype(F32) for r in (q, k, v, o)]
    wide = inner[...].astype(F32)
    units += [wide[:, WIDTH * i : WIDTH * (i + 1)] for i in range(4)]
    for ch in range(4):
        put(ch, jnp.concatenate([fold(units[2 * ch]), fold(units[2 * ch + 1])], axis=0).astype(BF))
    tall = outer[...]
    put(4, tall[:, :COLS])
    put(5, tall[:, COLS:])


def unpack_weights(g, ch, w):
    def one(pair):
        z, x, c = pair // (NX * NC), (pair // NC) % NX, pair % NC
        a = g[ch, z, x, c, 0].astype(F32)
        b = g[ch, z, x, c, 1].astype(F32)
        for unit in range(2):
            base = 48 * unit
            left = jnp.concatenate([a[base : base + 24], b[base : base + 24]], axis=0)
            right = jnp.concatenate([a[base + 24 : base + 48], b[base + 24 : base + 48]], axis=0)
            at = WIDTH * (2 * ch + unit)
            rows = pl.ds(pl.multiple_of(48 * pair, 48), 48)
            w[rows, at : at + COLS] = left.astype(BF)
            w[rows, at + COLS : at + WIDTH] = right.astype(BF)

    loop(GROUP, one)


def spread(gv, vec, ib):
    flat = gv[...].reshape(GROUP * NY * 16, 128)
    row = lax.broadcasted_iota(jnp.int32, (GROUP * NY * 16, WIDTH), 0)
    col = lax.broadcasted_iota(jnp.int32, (GROUP * NY * 16, WIDTH), 1)
    lane = lax.broadcasted_iota(jnp.int32, (128, WIDTH), 0)
    across = lax.broadcasted_iota(jnp.int32, (128, WIDTH), 1)
    first = (row // 16) * 24
    pick = (rem(across, 24) == lane).astype(F32).astype(BF)
    wide = jnp.dot(flat, pick, preferred_element_type=F32)
    wide = jnp.where((col >= first) & (col < first + 24), wide, 0.0)
    vec[...] = jnp.sum(wide.reshape(GROUP * NY, 16, WIDTH), axis=0)
    first = (row // 16) * 96
    for i in range(4):
        pick = (rem(across + WIDTH * i, 96) == lane).astype(F32).astype(BF)
        wide = jnp.dot(flat, pick, preferred_element_type=F32)
        at = col + WIDTH * i
        wide = jnp.where((at >= first) & (at < first + 96) & (rem(row, 16) == 8), wide, 0.0)
        total = jnp.sum(wide, axis=0, keepdims=True)
        ib[:, WIDTH * i : WIDTH * (i + 1)] = jnp.broadcast_to(total, (8, WIDTH))


def gather_kernel(
    stride,
    q, k, v, o, inner, outer, small, hidden, grad, mask,
    w, wu, vec, ib, page, cot, dead,
    g, gv, zs, zr, p1s, p1r, p2s, p2r, cs, cr, vs, vr, es, er,
):
    at = Place(stride)
    gather = Gather(at, g, (zs, zr), (p1s, p1r), (p2s, p2r), (cs, cr))

    def put(ch, value):
        g[ch, at.z, at.x, at.c, at.y] = value

    pack_weights((q, k, v, o, inner, outer), put)
    gv[at.z, at.x, at.c, at.y] = small[...]
    own = pl.ds(pl.multiple_of(at.y * 256, 256), 256)
    at.greet()
    ve = (vs, vr)
    ee = (es, er)
    swaps = [
        remote(hidden.at[at.oy], page.at[own], ee, 0, at.to_y),
        remote(mask.at[at.oy], dead.at[at.y], ee, 1, at.to_y),
        remote(grad.at[at.oy], cot.at[own], ee, 2, at.to_y),
    ]
    mine = gv.at[at.z, at.x, at.c, at.y]
    vz = [remote(mine, mine, ve, kk - 1, at.to_z(kk)) for kk in range(1, NZ)]
    for copy in vz:
        copy.start()
    swaps[0].start()
    swaps[1].start()
    gather.start_z(0)
    gather.start_own(0)
    gather.start_z(1)
    gather.start_own(1)
    for copy in vz:
        copy.wait_recv()
    column = gv.at[:, at.x, at.c, at.y]
    vx = remote(column, column, ve, 3, at.to_x)
    vx.start()
    loop(CHUNKS - 2, lambda i: gather.start_z(i + 2))
    page[own] = hidden[at.y]
    cot[own] = grad[at.y]
    dead[at.y] = mask[at.y]
    vx.wait_recv()
    pairs = gv.at[:, :, at.c, at.y]
    vy = remote(pairs, pairs, ve, 4, at.to_y)
    vy.start()
    gather.plane(0)
    vy.wait_recv()
    core = gv.at[:, :, at.c]
    vc = remote(core, core, ve, 5, at.to_c)
    vc.start()

    def step(ch):
        @pl.when(ch < CHUNKS - 2)
        def _():
            gather.start_own(ch + 2)

        @pl.when(ch < CHUNKS - 1)
        def _():
            gather.plane(ch + 1)

        @pl.when(ch == CHUNKS - 2)
        def _():
            swaps[2].start()

        gather.diagonal(ch)

        @pl.when(ch > 0)
        def _():
            gather.cross(ch - 1)

    loop(CHUNKS, step)
    gather.cross(CHUNKS - 1)
    vc.wait_recv()
    spread(gv, vec, ib)
    for ch in range(CHUNKS):
        gather.arrive(ch)
        if ch < 4:
            unpack_weights(g, ch, w)
        else:
            wu[ch - 4] = g[ch].reshape(GROUP * NY * ROWS, COLS)
    for copy in swaps:
        copy.wait_recv()
    loop(CHUNKS, gather.drain)
    for copy in vz + [vx, vy, vc] + swaps:
        copy.wait_send()


def gather_call(stride, args):
    vmem = pl.BlockSpec(memory_space=pltpu.VMEM)
    dma = pltpu.SemaphoreType.DMA
    shapes = (
        ((WIDTH, 8 * WIDTH), BF),
        ((2, GROUP * NY * ROWS, COLS), BF),
        ((16, WIDTH), F32),
        ((8, 4 * WIDTH), F32),
        ((512, WIDTH), BF),
        ((512, WIDTH), BF),
        ((2, 8, 256), F32),
    )
    return pl.pallas_call(
        partial(gather_kernel, stride),
        out_shape=tuple(jax.ShapeDtypeStruct(s, t) for s, t in shapes),
        in_specs=[vmem] * len(args),
        out_specs=tuple([vmem] * len(shapes)),
        scratch_shapes=[
            pltpu.VMEM((CHUNKS, NZ, NX, NC, NY, ROWS, COLS), BF),
            pltpu.VMEM((NZ, NX, NC, NY, 16, 128), BF),
            dma((CHUNKS, NZ - 1)), dma((CHUNKS, NZ - 1)),
            dma((CHUNKS, NZ, 2)), dma((CHUNKS, NZ, 2)),
            dma((CHUNKS, NZ, 2)), dma((CHUNKS, NZ, 2)),
            dma((CHUNKS,)), dma((CHUNKS,)),
            dma((6,)), dma((6,)),
            dma((3,)), dma((3,)),
        ],
        compiler_params=pltpu.CompilerParams(
            collective_id=0, has_side_effects=True, vmem_limit_bytes=56 * 2**20
        ),
        name="gather",
    )(*args)


class Scatter:
    def __init__(self, at, s, r1, rd0, rd1, rx, ry, rz, cs, p2, p1, zs):
        self.at, self.s = at, s
        self.r1, self.rd0, self.rd1, self.rx, self.ry, self.rz = r1, rd0, rd1, rx, ry, rz
        self.cs, self.p2, self.p1, self.zs = cs, p2, p1, zs

    def c_copy(self, ch):
        at = self.at
        return remote(self.s.at[ch, :, :, at.oc], self.r1.at[ch], self.cs, (ch,), at.to_c)

    def p2_copies(self, ch):
        at = self.at
        head, tail = pl.ds(0, CUT), pl.ds(CUT, ROWS - CUT)
        return (
            remote(self.s.at[ch, :, at.ox, at.c, at.oy, head], self.rd0.at[ch], self.p2, (ch, 0), at.to_x),
            remote(self.s.at[ch, :, at.ox, at.c, at.oy, tail], self.rd1.at[ch], self.p2, (ch, 1), at.to_y),
        )

    def p1_copies(self, ch):
        at = self.at
        return (
            remote(self.s.at[ch, :, at.ox, at.c, at.y], self.rx.at[ch], self.p1, (ch, 0), at.to_x),
            remote(self.s.at[ch, :, at.x, at.c, at.oy], self.ry.at[ch], self.p1, (ch, 1), at.to_y),
        )

    def z_copies(self, ch):
        at = self.at
        return [
            remote(self.s.at[ch, at.above(k), at.x, at.c, at.y], self.rz.at[ch, k - 1], self.zs, (ch, k - 1), at.to_z(k))
            for k in range(1, NZ)
        ]

    def start(self, ch):
        self.c_copy(ch).start()

    def add_core(self, ch, x, y):
        def one(z):
            total = self.s[ch, z, x, self.at.c, y].astype(F32) + self.r1[ch, z, x, y].astype(F32)
            self.s[ch, z, x, self.at.c, y] = total.astype(BF)

        loop(NZ, one)

    def core(self, ch):
        at = self.at
        self.c_copy(ch).wait_recv()
        self.add_core(ch, at.ox, at.oy)
        for copy in self.p2_copies(ch):
            copy.start()
        self.add_core(ch, at.ox, at.y)
        self.add_core(ch, at.x, at.oy)
        self.add_core(ch, at.x, at.y)

    def diagonal(self, ch):
        at = self.at
        over_x, over_y = self.p2_copies(ch)
        to_x, to_y = self.p1_copies(ch)
        head, tail = pl.ds(0, CUT), pl.ds(CUT, ROWS - CUT)
        over_x.wait_recv()

        def first(z):
            total = self.s[ch, z, at.x, at.c, at.oy, head].astype(F32) + self.rd0[ch, z].astype(F32)
            self.s[ch, z, at.x, at.c, at.oy, head] = total.astype(BF)

        loop(NZ, first)
        to_y.start()
        over_y.wait_recv()

        def second(z):
            total = self.s[ch, z, at.ox, at.c, at.y, tail].astype(F32) + self.rd1[ch, z].astype(F32)
            self.s[ch, z, at.ox, at.c, at.y, tail] = total.astype(BF)

        loop(NZ, second)
        to_x.start()

    def plane(self, ch):
        at = self.at
        for copy in self.p1_copies(ch):
            copy.wait_recv()

        def one(z):
            total = self.s[ch, z, at.x, at.c, at.y].astype(F32) + self.rx[ch, z].astype(F32)
            total = total + self.ry[ch, z].astype(F32)
            self.s[ch, z, at.x, at.c, at.y] = total.astype(BF)

        loop(NZ, one)
        for copy in self.z_copies(ch):
            copy.start()

    def finish(self, ch):
        at = self.at
        for copy in self.z_copies(ch):
            copy.wait_recv()
        total = self.s[ch, at.z, at.x, at.c, at.y].astype(F32)
        for k in range(NZ - 1):
            total = total + self.rz[ch, k].astype(F32)
        return total

    def drain(self, ch):
        for copy in (self.c_copy(ch), *self.p2_copies(ch), *self.p1_copies(ch), *self.z_copies(ch)):
            copy.wait_send()


def unfold(total, unit):
    base = 48 * unit
    return jnp.concatenate([total[base : base + 24], total[base + 24 : base + 48]], axis=1)


def pack_grad(src, dst, ch, unit):
    def one(device):
        z, x = device // (NX * NC * NY), (device // (NC * NY)) % NX
        c, y = (device // NY) % NC, device % NY
        rows = pl.ds(pl.multiple_of(24 * device, 24), 24)
        dst[ch, z, x, c, y, 48 * unit : 48 * unit + 48] = fold(src[rows, :]).astype(BF)

    loop(GROUP * NY, one)


class VectorScatter:
    def __init__(self, at, s, rc, rx, ry, rz, sems):
        self.at, self.s = at, s
        self.rc, self.rx, self.ry, self.rz, self.sems = rc, rx, ry, rz, sems
        at = self.at
        self.cc = remote(s.at[:, :, at.oc], rc, sems, 0, at.to_c)
        self.xx = remote(s.at[:, at.ox, at.c], rx, sems, 1, at.to_x)
        self.yy = remote(s.at[:, at.x, at.c, at.oy], ry, sems, 2, at.to_y)
        self.zz = [
            remote(s.at[at.above(k), at.x, at.c, at.y], rz.at[k - 1], sems, 2 + k, at.to_z(k)) for k in range(1, NZ)
        ]

    def start(self):
        self.cc.start()

    def core(self):
        self.cc.wait_recv()
        self.s[:, :, self.at.c] = self.s[:, :, self.at.c] + self.rc[...]
        self.xx.start()

    def over_x(self):
        at = self.at
        self.xx.wait_recv()
        self.s[:, at.x, at.c] = self.s[:, at.x, at.c] + self.rx[...]
        self.yy.start()

    def over_y(self):
        at = self.at
        self.yy.wait_recv()
        self.s[:, at.x, at.c, at.y] = self.s[:, at.x, at.c, at.y] + self.ry[...]
        for copy in self.zz:
            copy.start()

    def finish(self):
        at = self.at
        for copy in self.zz:
            copy.wait_recv()
        return self.s[at.z, at.x, at.c, at.y] + self.rz[0] + self.rz[1] + self.rz[2]

    def drain(self):
        for copy in [self.cc, self.xx, self.yy] + self.zz:
            copy.wait_send()


def scatter_kernel(
    stride,
    s_in, sv_in,
    q, k, v, o, inner, outer, small,
    s, sv, r1, rd0, rd1, rx, ry, rz, vc, vx, vy, vz,
    css, csr, p2s, p2r, p1s, p1r, zss, zsr, vs, vr, loads,
):
    at = Place(stride)
    scatter = Scatter(
        at, s, r1, rd0, rd1, rx, ry, rz, (css, csr), (p2s, p2r), (p1s, p1r), (zss, zsr)
    )
    vector = VectorScatter(at, sv, vc, vx, vy, vz, (vs, vr))
    load = pltpu.make_async_copy(s_in, s, loads.at[0])
    load.start()
    sv[...] = sv_in[...]
    at.greet()
    load.wait()
    vector.start()
    loop(CHUNKS, scatter.start)
    vector.core()

    def step(t):
        @pl.when(t < CHUNKS)
        def _():
            scatter.core(t)

        @pl.when((t >= 1) & (t < CHUNKS + 1))
        def _():
            scatter.diagonal(t - 1)

        @pl.when(t == 0)
        def _():
            vector.over_x()

        @pl.when(t == 1)
        def _():
            vector.over_y()

        @pl.when(t >= 2)
        def _():
            scatter.plane(t - 2)

    loop(CHUNKS + 2, step)
    small[...] = vector.finish()
    outs = (q, k, v, o)
    for ch in range(CHUNKS):
        total = scatter.finish(ch)
        if ch < 4:
            for unit in range(2):
                index = 2 * ch + unit
                value = unfold(total, unit)
                if index < 4:
                    outs[index][...] = value
                else:
                    inner[:, WIDTH * (index - 4) : WIDTH * (index - 3)] = value
        else:
            outer[:, COLS * (ch - 4) : COLS * (ch - 3)] = total
    loop(CHUNKS, scatter.drain)
    vector.drain()


def scatter_call(stride, s, sv):
    vmem = pl.BlockSpec(memory_space=pltpu.VMEM)
    dma = pltpu.SemaphoreType.DMA
    shapes = [(24, WIDTH)] * 4 + [(24, 4 * WIDTH), (96, WIDTH), (16, 128)]
    return pl.pallas_call(
        partial(scatter_kernel, stride),
        out_shape=tuple(jax.ShapeDtypeStruct(shape, F32) for shape in shapes),
        in_specs=[pl.BlockSpec(memory_space=pl.ANY), vmem],
        out_specs=tuple([vmem] * len(shapes)),
        scratch_shapes=[
            pltpu.VMEM((CHUNKS, NZ, NX, NC, NY, ROWS, COLS), BF),
            pltpu.VMEM((NZ, NX, NC, NY, 16, 128), F32),
            pltpu.VMEM((CHUNKS, NZ, NX, NY, ROWS, COLS), BF),
            pltpu.VMEM((CHUNKS, NZ, CUT, COLS), BF),
            pltpu.VMEM((CHUNKS, NZ, ROWS - CUT, COLS), BF),
            pltpu.VMEM((CHUNKS, NZ, ROWS, COLS), BF),
            pltpu.VMEM((CHUNKS, NZ, ROWS, COLS), BF),
            pltpu.VMEM((CHUNKS, NZ - 1, ROWS, COLS), BF),
            pltpu.VMEM((NZ, NX, NY, 16, 128), F32),
            pltpu.VMEM((NZ, NY, 16, 128), F32),
            pltpu.VMEM((NZ, 16, 128), F32),
            pltpu.VMEM((NZ - 1, 16, 128), F32),
            dma((CHUNKS,)), dma((CHUNKS,)),
            dma((CHUNKS, 2)), dma((CHUNKS, 2)),
            dma((CHUNKS, 2)), dma((CHUNKS, 2)),
            dma((CHUNKS, NZ - 1)), dma((CHUNKS, NZ - 1)),
            dma((6,)), dma((6,)),
            dma((1,)),
        ],
        compiler_params=pltpu.CompilerParams(
            collective_id=1, has_side_effects=True, vmem_limit_bytes=56 * 2**20
        ),
        name="scatter",
    )(s, sv)


def product(left, right):
    return jnp.dot(left, right, preferred_element_type=F32)


def product_left(left, right):
    return lax.dot_general(left, right, (((0,), (0,)), ((), ())), preferred_element_type=F32)


def product_right(left, right):
    return lax.dot_general(left, right, (((1,), (1,)), ((), ())), preferred_element_type=F32)


def layer_norm(values, gain, shift):
    center = values - jnp.mean(values, axis=-1, keepdims=True)
    inverse = lax.rsqrt(jnp.mean(center * center, axis=-1, keepdims=True) + EPSILON)
    normed = center * inverse
    return (normed * gain + shift, normed, inverse)


def norm_back(upstream, normed, inverse, gain):
    scaled = upstream * gain
    return inverse * (
        scaled
        - jnp.mean(scaled, axis=-1, keepdims=True)
        - normed * jnp.mean(scaled * normed, axis=-1, keepdims=True)
    )


def column_sum(values):
    return jnp.sum(values.astype(F32), axis=0)


def own_part(value, groups, stride):
    if stride == 1:
        return value
    whole = lax.all_gather(value, ("dp", "blk"), axis=0, tiled=True)
    rows = whole.shape[0] // (GROUP * NY)
    index = (lax.axis_index("dp") // stride) * NY + lax.axis_index("blk")
    return lax.dynamic_slice_in_dim(whole, index * rows, rows, axis=0)


def fine_part(value, groups, stride):
    if stride == 1:
        return value
    index = (lax.axis_index("dp") // stride) * NY + lax.axis_index("blk")
    rows = value.shape[0]
    whole = jnp.zeros((rows * GROUP * NY,) + value.shape[1:], value.dtype)
    whole = lax.dynamic_update_slice_in_dim(whole, value, index * rows, axis=0)
    return lax.psum_scatter(whole, ("dp", "blk"), scatter_dimension=0, tiled=True)


def body(
    stride,
    hidden_in,
    page_lengths,
    pad_mask,
    query_weight,
    query_bias,
    key_weight,
    value_weight,
    value_bias,
    output_weight,
    output_bias,
    first_gain,
    first_shift,
    inner_weight,
    inner_bias,
    outer_weight,
    outer_bias,
    second_gain,
    second_shift,
    out_grad,
):
    coarse = partial(own_part, groups=None, stride=stride)
    fine = partial(fine_part, groups=None, stride=stride)
    place = lax.axis_index("blk")
    segment, width = hidden_in.shape[1:]
    tokens = 2 * segment
    positions = place * segment + jnp.arange(segment, dtype=jnp.int32)
    live = (positions[None, :] < page_lengths[:, None]) & (pad_mask == 1)
    mask = jnp.where(live, 0.0, NEG_FILL).astype(F32)
    mask = jnp.broadcast_to(mask[:, None, :], (2, 8, segment))
    vectors = (
        query_bias, value_bias, output_bias, first_gain, first_shift, outer_bias, second_gain, second_shift,
    )
    small = jnp.stack([coarse(v) for v in vectors])
    small = jnp.concatenate(
        [
            jnp.pad(small, ((0, 0), (0, 104))),
            jnp.pad(coarse(inner_bias)[None, :], ((0, 7), (0, 32))),
        ]
    )
    weights = [
        coarse(v) for v in (query_weight, key_weight, value_weight, output_weight, inner_weight, outer_weight)
    ]
    w, wu, vec, ib, page, cot, dead = gather_call(
        stride, (*weights, small, hidden_in, out_grad, mask)
    )
    heads = HEADS
    size = width // heads
    wq, wk, wv, wo = (w[:, width * i : width * (i + 1)] for i in range(4))
    wi = w[:, 4 * width :]
    wout = jnp.concatenate([wu[0], wu[1]], axis=1)
    qb, vb, ob, g1, s1, ub, g2, s2 = (vec[i] for i in range(8))
    bias = dead[:, 0, :].reshape(tokens)

    def split_heads(values):
        return values.reshape(tokens, heads, size)

    factor = size**-0.5
    queries = split_heads((product(page, wq) + qb).astype(BF))
    keys = split_heads(product(page, wk).astype(BF))
    vals = split_heads((product(page, wv) + vb).astype(BF))
    scores = jnp.einsum("qhd,khd->hqk", queries, keys, preferred_element_type=F32) * factor
    scores = jnp.where(bias == 0.0, scores, NEG_FILL)
    probs = jax.nn.softmax(scores, axis=-1)
    low = probs.astype(BF)
    context = jnp.einsum("hqk,khd->qhd", low, vals, preferred_element_type=F32)
    context = context.astype(BF).reshape(tokens, width)
    joined = page.astype(F32) + product(context, wo) + ob
    first_out, first_normed, first_inverse = layer_norm(joined, g1, s1)
    hidden = first_out.astype(BF)
    inner = product(hidden, wi) + ib[0]
    activated = jax.nn.gelu(inner, approximate=False).astype(BF)
    second_in = hidden.astype(F32) + product(activated, wout) + ub
    result, second_normed, second_inverse = layer_norm(second_in, g2, s2)
    output = result.astype(BF)
    upstream = cot.astype(F32)
    second_gain_grad = jnp.sum(upstream * second_normed, axis=0)
    second_shift_grad = jnp.sum(upstream, axis=0)
    second_grad = norm_back(upstream, second_normed, second_inverse, g2)
    outer_low = second_grad.astype(BF)
    outer_weight_grad = product_left(activated, outer_low)
    outer_bias_grad = column_sum(outer_low)
    activated_grad = product_right(outer_low, wout)
    _, gelu_pull = jax.vjp(partial(jax.nn.gelu, approximate=False), inner)
    inner_low = gelu_pull(activated_grad)[0].astype(BF)
    inner_weight_grad = product_left(hidden, inner_low)
    inner_bias_grad = column_sum(inner_low)
    hidden_grad = second_grad + product_right(inner_low, wi)
    first_gain_grad = jnp.sum(hidden_grad * first_normed, axis=0)
    first_shift_grad = jnp.sum(hidden_grad, axis=0)
    first_grad = norm_back(hidden_grad, first_normed, first_inverse, g1)
    attended_low = first_grad.astype(BF)
    output_weight_grad = product_left(context, attended_low)
    output_bias_grad = column_sum(attended_low)
    context_grad = split_heads(product_right(attended_low, wo).astype(BF))
    prob_grad = jnp.einsum("qhd,khd->hqk", context_grad, vals, preferred_element_type=F32)
    delta = jnp.sum(probs * prob_grad, axis=-1, keepdims=True)
    score_grad = (probs * (prob_grad - delta)).astype(BF)
    query_grad = jnp.einsum("hqk,khd->qhd", score_grad, keys, preferred_element_type=F32) * factor
    key_grad = jnp.einsum("hqk,qhd->khd", score_grad, queries, preferred_element_type=F32) * factor
    value_grad = jnp.einsum("hqk,qhd->khd", low, context_grad, preferred_element_type=F32)
    query_grad, key_grad, value_grad = (
        v.astype(BF).reshape(tokens, width) for v in (query_grad, key_grad, value_grad)
    )
    input_grad = (
        first_grad
        + product_right(query_grad, wq)
        + product_right(key_grad, wk)
        + product_right(value_grad, wv)
    ).astype(BF)

    def owners(value):
        blocks = value.reshape(GROUP * NY, 24, -1, 2, COLS)
        return blocks.transpose(2, 0, 3, 1, 4).reshape(-1, GROUP * NY, 48, COLS).astype(BF)

    units = jnp.concatenate(
        [
            owners(v)
            for v in (
                product_left(page, query_grad),
                product_left(page, key_grad),
                product_left(page, value_grad),
                output_weight_grad,
                inner_weight_grad,
            )
        ]
    )
    chunks = units.reshape(4, 2, GROUP * NY, 48, COLS).transpose(0, 2, 1, 3, 4)
    chunks = chunks.reshape(4, GROUP * NY, ROWS, COLS)
    tall = outer_weight_grad.reshape(GROUP * NY, ROWS, 2, COLS).transpose(2, 0, 1, 3).astype(BF)
    s = jnp.concatenate([chunks, tall]).reshape(CHUNKS, NZ, NX, NC, NY, ROWS, COLS)
    grads = (
        column_sum(query_grad),
        column_sum(value_grad),
        output_bias_grad,
        first_gain_grad,
        first_shift_grad,
        outer_bias_grad,
        second_gain_grad,
        second_shift_grad,
    )
    sv = jnp.stack(grads).reshape(8, GROUP * NY, 24).transpose(1, 0, 2)
    sv = jnp.concatenate(
        [
            jnp.pad(sv, ((0, 0), (0, 0), (0, 104))),
            jnp.pad(inner_bias_grad.reshape(GROUP * NY, 1, 96), ((0, 0), (0, 7), (0, 32))),
        ],
        axis=1,
    ).reshape(NZ, NX, NC, NY, 16, 128)
    dq, dk, dv, do, di, du, dsmall = scatter_call(stride, s, sv)

    def halves(value):
        mine = value.reshape(2, segment, width)
        kept = lax.dynamic_index_in_dim(mine, place, 0, keepdims=False)
        sent = lax.dynamic_index_in_dim(mine, 1 - place, 0, keepdims=False)
        got = lax.ppermute(sent, "blk", [(0, 1), (1, 0)])
        return jnp.where(place == 0, jnp.stack([kept, got]), jnp.stack([got, kept]))

    output, input_grad = halves(output), halves(input_grad)
    small_grads = [fine(dsmall[i, :24]) for i in range(8)]
    qbg, vbg, obg, g1g, s1g, ubg, g2g, s2g = small_grads
    return (
        output,
        input_grad,
        fine(dq),
        qbg,
        fine(dk),
        fine(dv),
        vbg,
        fine(do),
        obg,
        g1g,
        s1g,
        fine(di),
        fine(dsmall[8, :96]),
        fine(du),
        ubg,
        g2g,
        s2g,
    )


def solution(mesh):
    stride = mesh.shape["dp"] // GROUP
    row = P(("dp", "blk"))
    mat = P(("dp", "blk"), None)
    tok = P("dp", "blk", None)
    in_specs = (
        tok, P("dp"), P("dp", "blk"), mat, row, mat, mat, row, mat, row, row, row, mat, row, mat, row, row, row, tok,
    )
    out_specs = (
        tok, tok, mat, row, mat, mat, row, mat, row, row, row, mat, row, mat, row, row, row,
    )
    return jax.shard_map(
        partial(body, stride), mesh=mesh, in_specs=in_specs, out_specs=out_specs, check_vma=False
    )
```

```python
from functools import partial

import jax
import jax.numpy as jnp
from jax import lax
from jax.experimental import pallas as pl
from jax.experimental.pallas import tpu as pltpu
from jax.sharding import PartitionSpec as P

HEADS = 12
NEG_FILL = -1000000000.0
EPSILON = 1e-05

NZ, NX, NC, NY = 4, 2, 2, 2
GROUP = NZ * NX * NC
CHUNKS = 6
ROWS, COLS = 96, 384
CUT = 64
WIDTH = 768
BF, F32 = jnp.bfloat16, jnp.float32
VMEM_LIMIT = 62 * 2**20


def rem(a, b):
    return lax.rem(a, b)


class Place:
    def __init__(self, stride):
        dp = lax.axis_index("dp")
        self.y = lax.axis_index("blk")
        index = dp // stride
        self.low = dp - index * stride
        self.stride = stride
        self.z = index // (NX * NC)
        self.x = (index // NC) % NX
        self.c = index % NC
        self.ox, self.oy, self.oc = 1 - self.x, 1 - self.y, 1 - self.c

    def dev(self, z, x, c, y):
        return ((z * (NX * NC) + x * NC + c) * self.stride + self.low, y)

    def above(self, k):
        return rem(self.z + k, NZ)

    def below(self, k):
        return rem(self.z + NZ - k, NZ)

    def to_z(self, k):
        return self.dev(self.above(k), self.x, self.c, self.y)

    @property
    def to_x(self):
        return self.dev(self.z, self.ox, self.c, self.y)

    @property
    def to_y(self):
        return self.dev(self.z, self.x, self.c, self.oy)

    @property
    def to_c(self):
        return self.dev(self.z, self.x, self.oc, self.y)

    def greet(self):
        barrier = pltpu.get_barrier_semaphore()
        partners = [self.to_z(k) for k in range(1, NZ)] + [self.to_x, self.to_y, self.to_c]
        for who in partners:
            pl.semaphore_signal(barrier, inc=1, device_id=who, device_id_type=pl.DeviceIdType.MESH)
        pl.semaphore_wait(barrier, len(partners))


def remote(src, dst, sems, index, who):
    send, recv = sems
    return pltpu.make_async_remote_copy(
        src_ref=src,
        dst_ref=dst,
        send_sem=send.at[index],
        recv_sem=recv.at[index],
        device_id=who,
        device_id_type=pl.DeviceIdType.MESH,
    )


def loop(count, body):
    def step(i, carry):
        body(i)
        return carry

    lax.fori_loop(0, count, step, 0)


class Gather:
    def __init__(self, at, blocks, zs, p1, p2, cs):
        self.at, self.g = at, blocks
        self.zs, self.p1, self.p2, self.cs = zs, p1, p2, cs

    def z_copy(self, ch, k, mine=True):
        at = self.at
        z = at.z if mine else at.below(k)
        ref = self.g.at[ch, z, at.x, at.c, at.y]
        return remote(ref, ref, self.zs, (ch, k - 1), at.to_z(k))

    def p1_copies(self, ch, k, mine=True):
        at = self.at
        z = at.below(k)
        x, y = (at.x, at.y) if mine else (at.ox, at.oy)
        over_x = self.g.at[ch, z, x, at.c, at.y]
        over_y = self.g.at[ch, z, at.x, at.c, y]
        return (
            remote(over_x, over_x, self.p1, (ch, k, 0), at.to_x),
            remote(over_y, over_y, self.p1, (ch, k, 1), at.to_y),
        )

    def p2_copies(self, ch, k, mine=True):
        at = self.at
        z = at.below(k)
        head, tail = pl.ds(0, CUT), pl.ds(CUT, ROWS - CUT)
        if mine:
            over_x = self.g.at[ch, z, at.x, at.c, at.oy, head]
            over_y = self.g.at[ch, z, at.ox, at.c, at.y, tail]
        else:
            over_x = self.g.at[ch, z, at.ox, at.c, at.oy, head]
            over_y = self.g.at[ch, z, at.ox, at.c, at.oy, tail]
        return (
            remote(over_x, over_x, self.p2, (ch, k, 0), at.to_x),
            remote(over_y, over_y, self.p2, (ch, k, 1), at.to_y),
        )

    def c_copy(self, ch, mine=True):
        at = self.at
        ref = self.g.at[ch, :, :, at.c if mine else at.oc]
        return remote(ref, ref, self.cs, (ch,), at.to_c)

    def start_z(self, ch):
        for k in range(1, NZ):
            self.z_copy(ch, k).start()

    def start_own(self, ch):
        for copy in self.p1_copies(ch, 0):
            copy.start()

    def plane(self, ch):
        for k in range(1, NZ):
            self.z_copy(ch, k, False).wait_recv()
            for copy in self.p1_copies(ch, k):
                copy.start()

    def diagonal(self, ch):
        def one(k):
            from_x, from_y = self.p1_copies(ch, k, False)
            over_x, over_y = self.p2_copies(ch, k)
            from_y.wait_recv()
            over_x.start()
            from_x.wait_recv()
            over_y.start()

        loop(NZ, one)

    def cross(self, ch):
        def one(k):
            for copy in self.p2_copies(ch, k, False):
                copy.wait_recv()

        loop(NZ, one)
        self.c_copy(ch).start()

    def arrive(self, ch):
        self.c_copy(ch, False).wait_recv()

    def drain(self, ch):
        for k in range(1, NZ):
            self.z_copy(ch, k).wait_send()

        def one(k):
            for copy in self.p1_copies(ch, k) + self.p2_copies(ch, k):
                copy.wait_send()

        loop(NZ, one)
        self.c_copy(ch).wait_send()


def fold(wide):
    return jnp.concatenate([wide[:, :COLS], wide[:, COLS:]], axis=0)


def pack_weights(refs, put):
    q, k, v, o, inner, outer = refs
    units = [r[...].astype(F32) for r in (q, k, v, o)]
    wide = inner[...].astype(F32)
    units += [wide[:, WIDTH * i : WIDTH * (i + 1)] for i in range(4)]
    for ch in range(4):
        put(ch, jnp.concatenate([fold(units[2 * ch]), fold(units[2 * ch + 1])], axis=0).astype(BF))
    tall = outer[...]
    put(4, tall[:, :COLS])
    put(5, tall[:, COLS:])


def unpack_weights(g, ch, w):
    def one(pair):
        z, x, c = pair // (NX * NC), (pair // NC) % NX, pair % NC
        a = g[ch, z, x, c, 0].astype(F32)
        b = g[ch, z, x, c, 1].astype(F32)
        for unit in range(2):
            base = 48 * unit
            left = jnp.concatenate([a[base : base + 24], b[base : base + 24]], axis=0)
            right = jnp.concatenate([a[base + 24 : base + 48], b[base + 24 : base + 48]], axis=0)
            at = WIDTH * (2 * ch + unit)
            rows = pl.ds(pl.multiple_of(48 * pair, 48), 48)
            w[rows, at : at + COLS] = left.astype(BF)
            w[rows, at + COLS : at + WIDTH] = right.astype(BF)

    loop(GROUP, one)


def spread(gv, vec, ib):
    flat = gv[...].reshape(GROUP * NY * 16, 128)
    row = lax.broadcasted_iota(jnp.int32, (GROUP * NY * 16, WIDTH), 0)
    col = lax.broadcasted_iota(jnp.int32, (GROUP * NY * 16, WIDTH), 1)
    lane = lax.broadcasted_iota(jnp.int32, (128, WIDTH), 0)
    across = lax.broadcasted_iota(jnp.int32, (128, WIDTH), 1)
    first = (row // 16) * 24
    pick = (rem(across, 24) == lane).astype(F32).astype(BF)
    wide = jnp.dot(flat, pick, preferred_element_type=F32)
    wide = jnp.where((col >= first) & (col < first + 24), wide, 0.0)
    vec[...] = jnp.sum(wide.reshape(GROUP * NY, 16, WIDTH), axis=0)
    first = (row // 16) * 96
    for i in range(4):
        pick = (rem(across + WIDTH * i, 96) == lane).astype(F32).astype(BF)
        wide = jnp.dot(flat, pick, preferred_element_type=F32)
        at = col + WIDTH * i
        wide = jnp.where((at >= first) & (at < first + 96) & (rem(row, 16) == 8), wide, 0.0)
        total = jnp.sum(wide, axis=0, keepdims=True)
        ib[:, WIDTH * i : WIDTH * (i + 1)] = jnp.broadcast_to(total, (8, WIDTH))


class Scatter:
    def __init__(self, at, s, r1, rd0, rd1, rx, ry, rz, cs, p2, p1, zs):
        self.at, self.s = at, s
        self.r1, self.rd0, self.rd1, self.rx, self.ry, self.rz = r1, rd0, rd1, rx, ry, rz
        self.cs, self.p2, self.p1, self.zs = cs, p2, p1, zs

    def c_copy(self, ch):
        at = self.at
        return remote(self.s.at[ch, :, :, at.oc], self.r1.at[ch], self.cs, (ch,), at.to_c)

    def p2_copies(self, ch):
        at = self.at
        head, tail = pl.ds(0, CUT), pl.ds(CUT, ROWS - CUT)
        return (
            remote(self.s.at[ch, :, at.ox, at.c, at.oy, head], self.rd0.at[ch], self.p2, (ch, 0), at.to_x),
            remote(self.s.at[ch, :, at.ox, at.c, at.oy, tail], self.rd1.at[ch], self.p2, (ch, 1), at.to_y),
        )

    def p1_copies(self, ch):
        at = self.at
        return (
            remote(self.s.at[ch, :, at.ox, at.c, at.y], self.rx.at[ch], self.p1, (ch, 0), at.to_x),
            remote(self.s.at[ch, :, at.x, at.c, at.oy], self.ry.at[ch], self.p1, (ch, 1), at.to_y),
        )

    def z_copies(self, ch):
        at = self.at
        return [
            remote(self.s.at[ch, at.above(k), at.x, at.c, at.y], self.rz.at[ch, k - 1], self.zs, (ch, k - 1), at.to_z(k))
            for k in range(1, NZ)
        ]

    def start(self, ch):
        self.c_copy(ch).start()

    def add_core(self, ch, x, y):
        def one(z):
            total = self.s[ch, z, x, self.at.c, y].astype(F32) + self.r1[ch, z, x, y].astype(F32)
            self.s[ch, z, x, self.at.c, y] = total.astype(BF)

        loop(NZ, one)

    def core(self, ch):
        at = self.at
        self.c_copy(ch).wait_recv()
        self.add_core(ch, at.ox, at.oy)
        for copy in self.p2_copies(ch):
            copy.start()
        self.add_core(ch, at.ox, at.y)
        self.add_core(ch, at.x, at.oy)
        self.add_core(ch, at.x, at.y)

    def diagonal(self, ch):
        at = self.at
        over_x, over_y = self.p2_copies(ch)
        to_x, to_y = self.p1_copies(ch)
        head, tail = pl.ds(0, CUT), pl.ds(CUT, ROWS - CUT)
        over_x.wait_recv()

        def first(z):
            total = self.s[ch, z, at.x, at.c, at.oy, head].astype(F32) + self.rd0[ch, z].astype(F32)
            self.s[ch, z, at.x, at.c, at.oy, head] = total.astype(BF)

        loop(NZ, first)
        to_y.start()
        over_y.wait_recv()

        def second(z):
            total = self.s[ch, z, at.ox, at.c, at.y, tail].astype(F32) + self.rd1[ch, z].astype(F32)
            self.s[ch, z, at.ox, at.c, at.y, tail] = total.astype(BF)

        loop(NZ, second)
        to_x.start()

    def plane(self, ch):
        at = self.at
        for copy in self.p1_copies(ch):
            copy.wait_recv()

        def one(z):
            total = self.s[ch, z, at.x, at.c, at.y].astype(F32) + self.rx[ch, z].astype(F32)
            total = total + self.ry[ch, z].astype(F32)
            self.s[ch, z, at.x, at.c, at.y] = total.astype(BF)

        loop(NZ, one)
        for copy in self.z_copies(ch):
            copy.start()

    def finish(self, ch):
        at = self.at
        for copy in self.z_copies(ch):
            copy.wait_recv()
        total = self.s[ch, at.z, at.x, at.c, at.y].astype(F32)
        for k in range(NZ - 1):
            total = total + self.rz[ch, k].astype(F32)
        return total

    def drain(self, ch):
        for copy in (self.c_copy(ch), *self.p2_copies(ch), *self.p1_copies(ch), *self.z_copies(ch)):
            copy.wait_send()


def unfold(total, unit):
    base = 48 * unit
    return jnp.concatenate([total[base : base + 24], total[base + 24 : base + 48]], axis=1)


class VectorScatter:
    def __init__(self, at, s, rc, rx, ry, rz, sems):
        self.at, self.s = at, s
        self.rc, self.rx, self.ry, self.rz, self.sems = rc, rx, ry, rz, sems
        at = self.at
        self.cc = remote(s.at[:, :, at.oc], rc, sems, 0, at.to_c)
        self.xx = remote(s.at[:, at.ox, at.c], rx, sems, 1, at.to_x)
        self.yy = remote(s.at[:, at.x, at.c, at.oy], ry, sems, 2, at.to_y)
        self.zz = [
            remote(s.at[at.above(k), at.x, at.c, at.y], rz.at[k - 1], sems, 2 + k, at.to_z(k)) for k in range(1, NZ)
        ]

    def start(self):
        self.cc.start()

    def core(self):
        self.cc.wait_recv()
        self.s[:, :, self.at.c] = self.s[:, :, self.at.c] + self.rc[...]
        self.xx.start()

    def over_x(self):
        at = self.at
        self.xx.wait_recv()
        self.s[:, at.x, at.c] = self.s[:, at.x, at.c] + self.rx[...]
        self.yy.start()

    def over_y(self):
        at = self.at
        self.yy.wait_recv()
        self.s[:, at.x, at.c, at.y] = self.s[:, at.x, at.c, at.y] + self.ry[...]
        for copy in self.zz:
            copy.start()

    def finish(self):
        at = self.at
        for copy in self.zz:
            copy.wait_recv()
        return self.s[at.z, at.x, at.c, at.y] + self.rz[0] + self.rz[1] + self.rz[2]

    def drain(self):
        for copy in [self.cc, self.xx, self.yy] + self.zz:
            copy.wait_send()


def own_part(value, stride):
    if stride == 1:
        return value
    whole = lax.all_gather(value, ("dp", "blk"), axis=0, tiled=True)
    rows = whole.shape[0] // (GROUP * NY)
    index = (lax.axis_index("dp") // stride) * NY + lax.axis_index("blk")
    return lax.dynamic_slice_in_dim(whole, index * rows, rows, axis=0)


def fine_part(value, stride):
    if stride == 1:
        return value
    index = (lax.axis_index("dp") // stride) * NY + lax.axis_index("blk")
    rows = value.shape[0]
    whole = jnp.zeros((rows * GROUP * NY,) + value.shape[1:], value.dtype)
    whole = lax.dynamic_update_slice_in_dim(whole, value, index * rows, axis=0)
    return lax.psum_scatter(whole, ("dp", "blk"), scatter_dimension=0, tiled=True)


def product(left, right):
    return jnp.dot(left, right, preferred_element_type=F32)


def product_left(left, right):
    return lax.dot_general(left, right, (((0,), (0,)), ((), ())), preferred_element_type=F32)


def product_right(left, right):
    return lax.dot_general(left, right, (((1,), (1,)), ((), ())), preferred_element_type=F32)


def tile(i, size):
    return pl.ds(pl.multiple_of(i * size, size), size)


def mean(values):
    return jnp.mean(values, axis=-1, keepdims=True)


def column(values):
    return jnp.sum(values, axis=0, keepdims=True)


def gather_vectors(vg, ibg, sv):
    owners = GROUP * NY

    def pieces(values, pick):
        high = values.astype(BF)
        rest = (values - high.astype(F32)).astype(BF)
        return product(high, pick) + product(rest, pick)

    def grids(shape):
        return [lax.broadcasted_iota(jnp.int32, shape, i) for i in range(len(shape))]

    across, lane = grids((WIDTH, 128))
    device, row, col = grids((owners, 16, WIDTH))
    pick = ((rem(across, 24) == lane) & (lane < 24)).astype(F32).astype(BF)
    first = device * 24
    wide = jnp.where((col >= first) & (col < first + 24), vg[...][None], 0.0)
    total = pieces(wide.reshape(owners * 16, WIDTH), pick)
    first = device * 96
    for i in range(4):
        pick = ((rem(across + WIDTH * i, 96) == lane) & (lane < 96)).astype(F32).astype(BF)
        at = col + WIDTH * i
        values = ibg[0:1, WIDTH * i : WIDTH * (i + 1)][None]
        wide = jnp.where((at >= first) & (at < first + 96) & (row == 8), values, 0.0)
        total = total + pieces(wide.reshape(owners * 16, WIDTH), pick)
    sv[...] = total.reshape(sv.shape)


QB, VB, OB, G1, S1, UB, G2, S2 = range(8)


def layer_kernel(
    stride,
    q, k, v, o, inner, outer, small, hidden, grad, mask,
    out, igrad, dq, dk, dv, do, di, du, dsmall, saved,
    g, gv, wd, u, page, cot, dead, hid, qkv, outp, xt, hidt, ctxt,
    n1, inv1, acc1, acc2, dst, bias, vec, ib, vg, ibg,
    sv, r1, rd0, rd1, rx, ry, rz, vc, vx, vy, vz,
    zs, zr, p1s, p1r, p2s, p2r, cs, cr, vs, vr, es, er,
    css, csr, q2s, q2r, q1s, q1r, zss, zsr, ws, wr, loads, saves,
):
    at = Place(stride)
    gather = Gather(at, g, (zs, zr), (p1s, p1r), (p2s, p2r), (cs, cr))
    scatter = Scatter(
        at, g, r1, rd0, rd1, rx, ry, rz, (css, csr), (q2s, q2r), (q1s, q1r), (zss, zsr)
    )
    vector = VectorScatter(at, sv, vc, vx, vy, vz, (ws, wr))

    def put(ch, value):
        g[ch, at.z, at.x, at.c, at.y] = value

    pack_weights((q, k, v, o, inner, outer), put)
    gv[at.z, at.x, at.c, at.y] = small[...]
    own = pl.ds(pl.multiple_of(at.y * 256, 256), 256)
    theirs = pl.ds(pl.multiple_of(at.oy * 256, 256), 256)
    local = [
        pltpu.make_async_copy(hidden.at[at.y], page.at[own], loads.at[0]),
        pltpu.make_async_copy(grad.at[at.y], cot.at[own], loads.at[1]),
    ]
    for copy in local:
        copy.start()
    at.greet()

    ve, ee = (vs, vr), (es, er)
    swaps = [
        remote(hidden.at[at.oy], page.at[own], ee, 0, at.to_y),
        remote(mask.at[at.oy], dead.at[at.y], ee, 1, at.to_y),
        remote(grad.at[at.oy], cot.at[own], ee, 2, at.to_y),
        remote(outp.at[theirs], out.at[at.y], ee, 3, at.to_y),
        remote(cot.at[theirs], igrad.at[at.y], ee, 4, at.to_y),
    ]
    mine = gv.at[at.z, at.x, at.c, at.y]
    vzs = [remote(mine, mine, ve, kk - 1, at.to_z(kk)) for kk in range(1, NZ)]
    for copy in vzs:
        copy.start()
    swaps[0].start()
    swaps[1].start()
    gather.start_z(0)
    gather.start_own(0)
    gather.start_z(1)
    gather.start_own(1)
    for copy in vzs:
        copy.wait_recv()
    line = gv.at[:, at.x, at.c, at.y]
    vxs = remote(line, line, ve, 3, at.to_x)
    vxs.start()
    loop(CHUNKS - 2, lambda i: gather.start_z(i + 2))
    dead[at.y] = mask[at.y]
    vxs.wait_recv()
    pairs = gv.at[:, :, at.c, at.y]
    vys = remote(pairs, pairs, ve, 4, at.to_y)
    vys.start()
    gather.plane(0)
    vys.wait_recv()
    core = gv.at[:, :, at.c]
    vcs = remote(core, core, ve, 5, at.to_c)
    vcs.start()

    gather.start_own(2)
    gather.plane(1)
    gather.diagonal(0)
    vcs.wait_recv()
    spread(gv, vec, ib)
    gather.start_own(3)
    gather.plane(2)
    gather.diagonal(1)
    gather.cross(0)
    for copy in local:
        copy.wait()
    swaps[0].wait_recv()
    swaps[1].wait_recv()

    def turn(i):
        xt[tile(i, 256), :] = page[:, tile(i, 256)].T

    loop(3, turn)
    for half in range(2):
        bias[256 * half : 256 * half + 256] = jnp.broadcast_to(dead[half, 0:1].T, (256, 128))
    gather.start_own(4)
    gather.plane(3)
    gather.arrive(0)
    unpack_weights(g, 0, wd)

    def queries(i):
        cols = tile(i, 256)
        value = product(page[...], wd[:, cols]) + vec[QB : QB + 1, cols]
        qkv[:, cols] = (value.astype(BF).astype(F32) * 0.125).astype(BF)

    def keys(i):
        cols = tile(i + 3, 256)
        qkv[:, cols] = product(page[...], wd[:, cols]).astype(BF)

    def vals(i):
        cols = tile(i + 6, 256)
        value = product(page[...], wd[:, cols]) + vec[VB : VB + 1, tile(i, 256)]
        qkv[:, cols] = value.astype(BF)

    loop(3, queries)
    loop(3, keys)
    gather.diagonal(2)
    gather.cross(1)
    gather.start_own(5)
    gather.plane(4)
    gather.arrive(1)
    unpack_weights(g, 1, wd)
    loop(3, vals)
    lane = lax.broadcasted_iota(jnp.int32, (512, 128), 1)
    sides = (lane < 64, lane >= 64)

    def side(value, which):
        return jnp.where(sides[which], value.astype(F32), 0.0).astype(BF)

    def save(pair):
        cols = tile(pair, 1024)
        return pltpu.make_async_copy(u.at[:, cols], saved.at[:, cols], saves.at[pair])

    def attend(pair):
        at_q, at_k, at_v = tile(pair, 128), tile(pair + 6, 128), tile(pair + 12, 128)
        k2, v2 = qkv[:, at_k], qkv[:, at_v]
        total = jnp.zeros((128, 512), F32)
        for a in range(2):
            ka, va = side(k2, a), side(v2, a)
            for h in range(2):
                q2 = qkv[256 * h : 256 * h + 256, at_q]
                s = product_right(ka, q2) + jnp.concatenate([bias[...], bias[...]], axis=1)
                e = jnp.exp(s - jnp.max(s, axis=0, keepdims=True))
                p = e * (1.0 / jnp.sum(e, axis=0, keepdims=True))
                cols = pl.ds(pl.multiple_of(1024 * pair + 512 * a + 256 * h, 256), 256)
                u[:, cols] = p.astype(BF)
            cols = pl.ds(pl.multiple_of(1024 * pair + 512 * a, 512), 512)
            total = total + product_left(va, u[:, cols])
        ctxt[tile(pair, 128), :] = total.astype(BF)
        outp[:, tile(pair, 128)] = total.T.astype(BF)
        save(pair).start()

    def steps(*table):
        def run(i):
            for index, work in enumerate(table):
                pl.when(i == index)(work)

        return run

    def attend_and(table):
        def run(i):
            attend(i)
            steps(*table)(i)

        return run

    def start_cot():
        swaps[2].start()
        gather.cross(2)

    loop(
        6,
        attend_and(
            (
                lambda: gather.diagonal(3),
                start_cot,
                lambda: gather.plane(5),
                lambda: gather.diagonal(4),
                lambda: gather.cross(3),
            )
        ),
    )

    def attended(i):
        cols = tile(i, 256)
        value = product(outp[...], wd[:, tile(i + 9, 256)]) + vec[OB : OB + 1, cols]
        acc1[:, cols] = page[:, cols].astype(F32) + value

    loop(3, attended)
    gather.diagonal(5)
    gather.cross(4)

    def first_norm(i):
        rows = tile(i, 64)
        joined = acc1[rows, :]
        center = joined - mean(joined)
        inverse = lax.rsqrt(mean(center * center) + EPSILON)
        normed = center * inverse
        n1[rows, :] = normed
        inv1[rows, :] = jnp.broadcast_to(inverse, (64, 128))
        hid[rows, :] = (normed * vec[G1 : G1 + 1] + vec[S1 : S1 + 1]).astype(BF)

    loop(8, first_norm)

    def turn_hidden(i):
        hidt[tile(i, 256), :] = hid[:, tile(i, 256)].T

    loop(3, turn_hidden)
    gather.arrive(2)
    unpack_weights(g, 2, wd)
    gather.arrive(3)
    unpack_weights(g, 3, wd)
    loop(6, lambda i: save(i).wait())
    gather.cross(5)

    def feed(i):
        cols = tile(i, 384)
        weight = wd[:, pl.ds(pl.multiple_of(4 * WIDTH + 384 * i, 384), 384)]
        acc1[:, 0:384] = product(hid[...], weight) + ib[0:1, cols]

        def one(r):
            rows = tile(r, 64)
            value = acc1[rows, 0:384]
            cdf = 0.5 + 0.5 * lax.erf(value * 0.7071067811865476)
            density = 0.3989422804014327 * jnp.exp(-0.5 * value * value)
            u[rows, cols] = (value * cdf).astype(BF)
            u[rows, pl.ds(pl.multiple_of(3072 + 384 * i, 384), 384)] = (cdf + value * density).astype(BF)

        loop(8, one)

    loop(8, feed)
    for half in range(2):
        gather.arrive(4 + half)
        cols = slice(COLS * half, COLS * half + COLS)
        weight = g[4 + half].reshape(8 * COLS, COLS)
        acc1[:, cols] = product(u[:, 0:3072], weight)
    swaps[2].wait_recv()

    vg[...] = jnp.zeros_like(vg)

    def second_norm(i):
        rows = tile(i, 64)
        second = hid[rows, :].astype(F32) + (acc1[rows, :] + vec[UB : UB + 1])
        center = second - mean(second)
        inverse = lax.rsqrt(mean(center * center) + EPSILON)
        normed = center * inverse
        gain = vec[G2 : G2 + 1]
        outp[rows, :] = (normed * gain + vec[S2 : S2 + 1]).astype(BF)
        dy = cot[rows, :].astype(F32)
        vg[G2 : G2 + 1] += column(dy * normed)
        vg[S2 : S2 + 1] += column(dy)
        scaled = dy * gain
        back = inverse * (scaled - mean(scaled) - normed * mean(scaled * normed))
        acc2[rows, :] = back
        low = back.astype(BF)
        page[rows, :] = low
        vg[UB : UB + 1] += column(low.astype(F32))

    loop(8, second_norm)
    swaps[3].start()
    keep = pltpu.make_async_copy(outp.at[own], out.at[at.y], loads.at[0])
    keep.start()

    low = page
    loop(CHUNKS, gather.drain)

    def outer_grad(i):
        z, x = i // 2, rem(i, 2)
        value = product_left(u[:, tile(i, 384)], low[...]).astype(BF)
        for half in range(2):
            part = value[:, COLS * half : COLS * half + COLS]
            g[half, z, x] = part.reshape(NC, NY, ROWS, COLS)

    loop(8, outer_grad)
    scatter.start(0)
    scatter.start(1)

    def load(part):
        cols = pl.ds(3072 * part, 3072)
        return pltpu.make_async_copy(saved.at[:, cols], u.at[:, cols], loads.at[1])

    load(0).start()

    def inner_back(i):
        z, x = i // 2, rem(i, 2)
        value = product_right(low[:, 0:COLS], g[4, z, x].reshape(COLS, COLS))
        value = value + product_right(low[:, COLS:], g[5, z, x].reshape(COLS, COLS))
        cols = pl.ds(pl.multiple_of(3072 + 384 * i, 384), 384)
        value = (value * u[:, cols].astype(F32)).astype(BF)
        u[:, cols] = value
        total = column(value.astype(F32))
        ibg[:, tile(i, 384)] = jnp.broadcast_to(total, (8, 384))

    loop(8, inner_back)
    scatter.core(0)

    def weight_grad(slot, unit, left, right):
        def one(i):
            value = product(left[tile(i, 384), :], right)
            value = value.reshape(16, 24, WIDTH)
            value = jnp.concatenate([value[:, :, :COLS], value[:, :, COLS:]], axis=1).astype(BF)
            g[slot, pl.ds(2 * i, 2), :, :, :, 48 * unit : 48 * unit + 48, :] = value.reshape(
                2, NX, NC, NY, 48, COLS
            )

        loop(2, one)

    def inner_grad(unit):
        right = u[:, 3072 + WIDTH * unit : 3072 + WIDTH * (unit + 1)]
        weight_grad(2 + unit // 2, unit % 2, hidt, right)

    inner_grad(0)
    inner_grad(1)
    scatter.start(2)
    scatter.core(1)
    inner_grad(2)
    inner_grad(3)
    scatter.start(3)
    scatter.diagonal(0)

    def hidden_back(i):
        cols = tile(i, 256)
        acc2[:, cols] = acc2[:, cols] + product_right(u[:, 3072:6144], wd[cols, 4 * WIDTH :])

    loop(3, hidden_back)
    load(0).wait()
    load(1).start()
    scatter.core(2)
    scatter.diagonal(1)

    def first_back(i):
        rows = tile(i, 64)
        up = acc2[rows, :]
        normed = n1[rows, :]
        vg[G1 : G1 + 1] += column(up * normed)
        vg[S1 : S1 + 1] += column(up)
        scaled = up * vec[G1 : G1 + 1]
        inverse = inv1[rows, 0:1]
        back = inverse * (scaled - mean(scaled) - normed * mean(scaled * normed))
        acc2[rows, :] = back
        short = back.astype(BF)
        low[rows, :] = short
        vg[OB : OB + 1] += column(short.astype(F32))

    loop(8, first_back)
    weight_grad(4, 1, ctxt, low[...])

    def context_back(i):
        cols = tile(i, 256)
        hid[:, cols] = product_right(low[...], wd[cols, 3 * WIDTH : 4 * WIDTH]).astype(BF)

    loop(3, context_back)
    scatter.plane(0)
    load(1).wait()

    def attend_back(pair):
        at_q, at_k, at_v = tile(pair, 128), tile(pair + 6, 128), tile(pair + 12, 128)
        q2, k2, v2, c2 = qkv[:, at_q], qkv[:, at_k], qkv[:, at_v], hid[:, at_q]
        dqt = jnp.zeros((128, 512), F32)
        dk2 = jnp.zeros((512, 128), F32)
        dv2 = jnp.zeros((512, 128), F32)
        for a in range(2):
            va = side(v2, a)
            for h in range(2):
                cols = pl.ds(pl.multiple_of(1024 * pair + 512 * a + 256 * h, 256), 256)
                p = u[:, cols].astype(F32)
                d = product_right(va, c2[256 * h : 256 * h + 256])
                delta = jnp.sum(p * d, axis=0, keepdims=True)
                dst[:, 256 * h : 256 * h + 256] = (p * (d - delta)).astype(BF)
            cols = pl.ds(pl.multiple_of(1024 * pair + 512 * a, 512), 512)
            dv2 = dv2 + product(u[:, cols], side(c2, a))
            dk2 = dk2 + product(dst[...], side(q2, a))
            dqt = dqt + product_left(side(k2, a), dst[...])
        qkv[:, at_q] = (dqt.T * 0.125).astype(BF)
        qkv[:, at_k] = dk2.astype(BF)
        qkv[:, at_v] = dv2.astype(BF)

    def back_and(table):
        def run(i):
            attend_back(i)
            steps(*table)(i)

        return run

    loop(
        6,
        back_and(
            (
                lambda: scatter.diagonal(2),
                lambda: scatter.core(3),
                lambda: scatter.plane(1),
                lambda: scatter.diagonal(3),
                lambda: scatter.plane(2),
            )
        ),
    )
    weight_grad(4, 0, xt, qkv[:, 2 * WIDTH : 3 * WIDTH])
    scatter.start(4)
    weight_grad(5, 0, xt, qkv[:, 0:WIDTH])
    scatter.core(4)
    weight_grad(5, 1, xt, qkv[:, WIDTH : 2 * WIDTH])
    scatter.start(5)

    def sums(i):
        rows = tile(i, 64)
        vg[QB : QB + 1] += column(qkv[rows, 0:WIDTH].astype(F32))
        vg[VB : VB + 1] += column(qkv[rows, 2 * WIDTH : 3 * WIDTH].astype(F32))

    loop(8, sums)
    gather_vectors(vg, ibg, sv)
    vector.start()
    scatter.diagonal(4)
    scatter.core(5)
    scatter.plane(3)
    vector.core()

    def input_back(i):
        cols = tile(i, 256)
        value = acc2[:, cols] + product_right(qkv[...], wd[cols, 0 : 3 * WIDTH])
        cot[:, cols] = value.astype(BF)

    loop(3, input_back)
    vector.over_x()
    scatter.diagonal(5)
    swaps[4].start()
    keep_in = pltpu.make_async_copy(cot.at[own], igrad.at[at.y], loads.at[1])
    keep_in.start()
    scatter.plane(4)
    vector.over_y()

    outs = (q, k, v, o)
    targets = (dq, dk, dv, do)

    def finish(n):
        total = scatter.finish(n)
        if n < 2:
            du[:, COLS * n : COLS * n + COLS] = total
        elif n < 4:
            for unit in range(2):
                index = 2 * (n - 2) + unit
                di[:, WIDTH * index : WIDTH * (index + 1)] = unfold(total, unit)
        else:
            first, second = (dv, do) if n == 4 else (dq, dk)
            first[...] = unfold(total, 0)
            second[...] = unfold(total, 1)

    for n in range(4):
        finish(n)
    scatter.plane(5)
    dsmall[...] = vector.finish()
    finish(4)
    finish(5)

    keep.wait()
    keep_in.wait()
    swaps[3].wait_recv()
    swaps[4].wait_recv()
    loop(CHUNKS, scatter.drain)
    vector.drain()
    for copy in vzs + [vxs, vys, vcs] + swaps:
        copy.wait_send()


def layer_call(stride, args):
    vmem = pl.BlockSpec(memory_space=pltpu.VMEM)
    hbm = pl.BlockSpec(memory_space=pl.ANY)
    dma = pltpu.SemaphoreType.DMA

    def shape(*dims, kind=F32):
        return jax.ShapeDtypeStruct(dims, kind)

    tokens = [shape(2, 256, WIDTH, kind=BF)] * 2
    grads = [shape(24, WIDTH)] * 4 + [shape(24, 4 * WIDTH), shape(96, WIDTH), shape(16, 128)]

    def low(*dims):
        return pltpu.VMEM(dims, BF)

    def full(*dims):
        return pltpu.VMEM(dims, F32)

    def pair(*dims):
        return [dma(dims), dma(dims)]

    return pl.pallas_call(
        partial(layer_kernel, stride),
        out_shape=tuple(tokens + grads + [shape(512, 12 * 512, kind=BF)]),
        in_specs=[vmem] * 7 + [hbm, hbm, vmem],
        out_specs=tuple([hbm] * 2 + [vmem] * len(grads) + [hbm]),
        scratch_shapes=[
            low(CHUNKS, NZ, NX, NC, NY, ROWS, COLS),
            low(NZ, NX, NC, NY, 16, 128),
            low(WIDTH, 8 * WIDTH),
            low(512, 12 * 512),
            low(512, WIDTH),
            low(512, WIDTH),
            full(2, 8, 256),
            low(512, WIDTH),
            low(512, 3 * WIDTH),
            low(512, WIDTH),
            low(WIDTH, 512),
            low(WIDTH, 512),
            low(WIDTH, 512),
            full(512, WIDTH),
            full(512, 128),
            full(512, WIDTH),
            full(512, WIDTH),
            low(512, 512),
            full(512, 128),
            full(16, WIDTH),
            full(8, 4 * WIDTH),
            full(16, WIDTH),
            full(8, 4 * WIDTH),
            full(NZ, NX, NC, NY, 16, 128),
            low(CHUNKS, NZ, NX, NY, ROWS, COLS),
            low(CHUNKS, NZ, CUT, COLS),
            low(CHUNKS, NZ, ROWS - CUT, COLS),
            low(CHUNKS, NZ, ROWS, COLS),
            low(CHUNKS, NZ, ROWS, COLS),
            low(CHUNKS, NZ - 1, ROWS, COLS),
            full(NZ, NX, NY, 16, 128),
            full(NZ, NY, 16, 128),
            full(NZ, 16, 128),
            full(NZ - 1, 16, 128),
            *pair(CHUNKS, NZ - 1),
            *pair(CHUNKS, NZ, 2),
            *pair(CHUNKS, NZ, 2),
            *pair(CHUNKS),
            *pair(6),
            *pair(5),
            *pair(CHUNKS),
            *pair(CHUNKS, 2),
            *pair(CHUNKS, 2),
            *pair(CHUNKS, NZ - 1),
            *pair(6),
            dma((2,)),
            dma((6,)),
        ],
        compiler_params=pltpu.CompilerParams(
            collective_id=0, has_side_effects=True, vmem_limit_bytes=VMEM_LIMIT
        ),
        name="layer",
    )(*args)


def body(
    stride,
    hidden_in,
    page_lengths,
    pad_mask,
    query_weight,
    query_bias,
    key_weight,
    value_weight,
    value_bias,
    output_weight,
    output_bias,
    first_gain,
    first_shift,
    inner_weight,
    inner_bias,
    outer_weight,
    outer_bias,
    second_gain,
    second_shift,
    out_grad,
):
    coarse = partial(own_part, stride=stride)
    fine = partial(fine_part, stride=stride)
    place = lax.axis_index("blk")
    segment = hidden_in.shape[1]
    positions = place * segment + jnp.arange(segment, dtype=jnp.int32)
    live = (positions[None, :] < page_lengths[:, None]) & (pad_mask == 1)
    mask = jnp.where(live, 0.0, NEG_FILL).astype(F32)
    mask = jnp.broadcast_to(mask[:, None, :], (2, 8, segment))
    vectors = (
        query_bias, value_bias, output_bias, first_gain, first_shift, outer_bias, second_gain, second_shift,
    )
    small = jnp.stack([coarse(v) for v in vectors])
    small = jnp.concatenate(
        [
            jnp.pad(small, ((0, 0), (0, 104))),
            jnp.pad(coarse(inner_bias)[None, :], ((0, 7), (0, 32))),
        ]
    )
    weights = [
        coarse(v) for v in (query_weight, key_weight, value_weight, output_weight, inner_weight, outer_weight)
    ]
    output, input_grad, dq, dk, dv, do, di, du, dsmall, _ = layer_call(
        stride, (*weights, small, hidden_in, out_grad, mask)
    )
    qbg, vbg, obg, g1g, s1g, ubg, g2g, s2g = [fine(dsmall[i, :24]) for i in range(8)]
    return (
        output,
        input_grad,
        fine(dq),
        qbg,
        fine(dk),
        fine(dv),
        vbg,
        fine(do),
        obg,
        g1g,
        s1g,
        fine(di),
        fine(dsmall[8, :96]),
        fine(du),
        ubg,
        g2g,
        s2g,
    )


def solution(mesh):
    stride = mesh.shape["dp"] // GROUP
    row = P(("dp", "blk"))
    mat = P(("dp", "blk"), None)
    tok = P("dp", "blk", None)
    in_specs = (
        tok, P("dp"), P("dp", "blk"), mat, row, mat, mat, row, mat, row, row, row, mat, row, mat, row, row, row, tok,
    )
    out_specs = (
        tok, tok, mat, row, mat, mat, row, mat, row, row, row, mat, row, mat, row, row, row,
    )
    return jax.shard_map(
        partial(body, stride), mesh=mesh, in_specs=in_specs, out_specs=out_specs, check_vma=False
    )
```

```python
from functools import partial

import jax
import jax.numpy as jnp
from jax import lax
from jax.experimental import pallas as pl
from jax.experimental.pallas import tpu as pltpu
from jax.sharding import PartitionSpec as P

HEADS = 12
NEG_FILL = -1000000000.0
EPSILON = 1e-05

NZ, NX, NC, NY = 4, 2, 2, 2
GROUP = NZ * NX * NC
CHUNKS = 6
ROWS, COLS = 96, 384
LATE = 5
CUT = 64
WIDTH = 768
FINE = (4, 5)
BF, F32 = jnp.bfloat16, jnp.float32
VMEM_LIMIT = 62 * 2**20

FORWARD = (
    "own 1", "own 5", "vector_z", "z 0", "turn 1 0", "page", "own 2", "vector_x", "own 0", "turn 5 0",
    "plane 0 3", "z 1", "plane 0 1", "page_wait", "z 2", "plane 1 3", "z 4", "plane 1 1", "plane 1 2",
    "turn 0 3", "plane 0 2", "vector_y", "turn 0 1", "turn 0 0", "turn 1 3", "turn 1 2", "z 3", "turn 0 2",
    "turn 1 1", "plane 4 2", "plane 2 3", "late_z", "cross 0", "vector_c", "plane 2 1", "own 3", "plane 2 2",
    "cross 1", "vector_wait", "arrive 0", "plane 3 1", "prepare", "unpack 0", "plane 3 3", "own 4", "turn 2 3",
    "turn 2 1", "arrive 1", "unpack 1", "queries_keys", "turn 2 2", "plane 3 2", "turn 2 0", "values",
    "turn 3 1", "attend 0", "attend 1", "plane 4 3", "attend 2", "attend 3", "turn 3 0", "plane 4 1", "cross 2",
    "turn 3 3", "attend 4", "turn 3 2", "grad", "turn 4 0", "attend 5", "arrive 2", "after_attention",
    "unpack 2", "cross 3", "feed 0", "turn 4 3", "feed 1", "turn 4 2", "feed 2", "late_cross", "arrive 3",
    "turn 4 1", "feed 3", "unpack 3", "feed_on 4", "cross 4", "feed_on 5", "feed_on 6", "feed_on 7", "arrive 4",
    "arrive 5", "outer 0", "grad_wait", "outer 1",
)
BACKWARD = (
    "out", "outer_first", "start 1", "outer_second", "inner_back 0", "inner_back 1", "start 0", "core 1",
    "inner_back 2", "inner_back 3", "inner_back 4", "early_core", "inner_back 5", "inner_back 6", "diagonal 1",
    "inner_back 7", "inner_grad 0", "inner_grad 1", "start 2", "inner_grad 2", "inner_grad 3", "hidden_back 0",
    "hidden_back 1", "core 2", "start 3", "hidden_back 2", "first_back", "context_back", "core 3",
    "attend_back 0", "diagonal 2", "attend_back 1", "attend_back 2", "diagonal 3", "attend_back 3",
    "attend_back 4", "output_grad", "attend_back 5", "query_grad", "plane 1", "value_grad", "start 4",
    "key_grad", "early_plane", "sums", "start 5", "gather_vectors", "vector", "core 4", "plane 2",
    "vector_core", "core 5", "plane 3", "diagonal 4 2", "diagonal 4 0", "finish 1", "input_back 0",
    "diagonal 4 1", "vector_x", "diagonal 4 3", "vector_y", "diagonal 5 2", "diagonal 5 0", "plane 4 2",
    "diagonal 5 1", "input_back 1", "early_diagonal", "finish 2", "plane 4 0", "diagonal 5 3", "plane 4 1",
    "finish 3", "input_back 2", "vector_finish", "grad", "plane 5 2", "plane 5 1", "plane 4 3", "plane 5 3",
    "finish 4", "plane 5 0", "finish 0", "finish 5",
)


def rem(a, b):
    return lax.rem(a, b)


class Place:
    def __init__(self, stride):
        dp = lax.axis_index("dp")
        self.y = lax.axis_index("blk")
        index = dp // stride
        self.low = dp - index * stride
        self.stride = stride
        self.z = index // (NX * NC)
        self.x = (index // NC) % NX
        self.c = index % NC
        self.ox, self.oy, self.oc = 1 - self.x, 1 - self.y, 1 - self.c

    def dev(self, z, x, c, y):
        return ((z * (NX * NC) + x * NC + c) * self.stride + self.low, y)

    def above(self, k):
        return rem(self.z + k, NZ)

    def below(self, k):
        return rem(self.z + NZ - k, NZ)

    def to_z(self, k):
        return self.dev(self.above(k), self.x, self.c, self.y)

    @property
    def to_x(self):
        return self.dev(self.z, self.ox, self.c, self.y)

    @property
    def to_y(self):
        return self.dev(self.z, self.x, self.c, self.oy)

    @property
    def to_c(self):
        return self.dev(self.z, self.x, self.oc, self.y)

    def hail(self):
        partners = [self.to_z(k) for k in range(1, NZ)] + [self.to_x, self.to_y, self.to_c]
        for who in partners:
            pl.semaphore_signal(
                pltpu.get_barrier_semaphore(), inc=1, device_id=who, device_id_type=pl.DeviceIdType.MESH
            )

    def meet(self):
        pl.semaphore_wait(pltpu.get_barrier_semaphore(), NZ + 2)


def remote(src, dst, sems, index, who):
    send, recv = sems
    return pltpu.make_async_remote_copy(
        src_ref=src,
        dst_ref=dst,
        send_sem=send.at[index],
        recv_sem=recv.at[index],
        device_id=who,
        device_id_type=pl.DeviceIdType.MESH,
    )


def loop(count, body):
    def step(i, carry):
        body(i)
        return carry

    lax.fori_loop(0, count, step, 0)


class Gather:
    def __init__(self, at, blocks, zs, p1, p2, cs):
        self.at, self.g = at, blocks
        self.zs, self.p1, self.p2, self.cs = zs, p1, p2, cs

    def z_copy(self, ch, k, mine=True):
        at = self.at
        z = at.z if mine else at.below(k)
        ref = self.g.at[ch, z, at.x, at.c, at.y]
        return remote(ref, ref, self.zs, (ch, k - 1), at.to_z(k))

    def p1_copies(self, ch, k, mine=True):
        at = self.at
        z = at.below(k)
        x, y = (at.x, at.y) if mine else (at.ox, at.oy)
        over_x = self.g.at[ch, z, x, at.c, at.y]
        over_y = self.g.at[ch, z, at.x, at.c, y]
        return (
            remote(over_x, over_x, self.p1, (ch, k, 0), at.to_x),
            remote(over_y, over_y, self.p1, (ch, k, 1), at.to_y),
        )

    def p2_copies(self, ch, k, mine=True):
        at = self.at
        z = at.below(k)
        head, tail = pl.ds(0, CUT), pl.ds(CUT, ROWS - CUT)
        if mine:
            over_x = self.g.at[ch, z, at.x, at.c, at.oy, head]
            over_y = self.g.at[ch, z, at.ox, at.c, at.y, tail]
        else:
            over_x = self.g.at[ch, z, at.ox, at.c, at.oy, head]
            over_y = self.g.at[ch, z, at.ox, at.c, at.oy, tail]
        return (
            remote(over_x, over_x, self.p2, (ch, k, 0), at.to_x),
            remote(over_y, over_y, self.p2, (ch, k, 1), at.to_y),
        )

    def c_copy(self, ch, mine=True):
        at = self.at
        ref = self.g.at[ch, :, :, at.c if mine else at.oc]
        return remote(ref, ref, self.cs, (ch,), at.to_c)

    def start_z(self, ch):
        for k in range(1, NZ):
            self.z_copy(ch, k).start()

    def start_own(self, ch):
        for copy in self.p1_copies(ch, 0):
            copy.start()

    def plane(self, ch, k):
        self.z_copy(ch, k, False).wait_recv()
        for copy in self.p1_copies(ch, k):
            copy.start()

    def turn(self, ch, k):
        from_x, from_y = self.p1_copies(ch, k, False)
        over_x, over_y = self.p2_copies(ch, k)
        from_y.wait_recv()
        over_x.start()
        from_x.wait_recv()
        over_y.start()

    def cross(self, ch):
        def one(k):
            for copy in self.p2_copies(ch, k, False):
                copy.wait_recv()

        loop(NZ, one)
        self.c_copy(ch).start()

    def late_copy(self, k, mine=True):
        at = self.at
        ref = self.g.at[LATE, at.z if mine else at.below(k), :, at.c]
        return remote(ref, ref, self.zs, (LATE, k - 1), at.to_z(k))

    def late_z(self):
        for copy in self.p2_copies(LATE, 0, False):
            copy.wait_recv()
        for k in range(1, NZ):
            self.late_copy(k).start()

    def late_cross(self):
        for k in range(1, NZ):
            self.late_copy(k, False).wait_recv()
        self.c_copy(LATE).start()

    def arrive(self, ch):
        self.c_copy(ch, False).wait_recv()

    def drain(self, ch):
        for k in range(1, NZ):
            self.z_copy(ch, k).wait_send()

        def one(k):
            for copy in self.p1_copies(ch, k) + self.p2_copies(ch, k):
                copy.wait_send()

        loop(NZ, one)
        self.c_copy(ch).wait_send()

    def late_drain(self):
        for k in range(1, NZ):
            self.late_copy(k).wait_send()
        for copy in (*self.p1_copies(LATE, 0), *self.p2_copies(LATE, 0), self.c_copy(LATE)):
            copy.wait_send()


def fold(wide):
    return jnp.concatenate([wide[:, :COLS], wide[:, COLS:]], axis=0)


def pack_weights(refs, put):
    q, k, v, o, inner, outer = refs
    units = [r[...].astype(F32) for r in (q, k, v, o)]
    wide = inner[...].astype(F32)
    units += [wide[:, WIDTH * i : WIDTH * (i + 1)] for i in range(4)]
    for ch in range(4):
        put(ch, jnp.concatenate([fold(units[2 * ch]), fold(units[2 * ch + 1])], axis=0).astype(BF))
    tall = outer[...]
    put(4, tall[:, :COLS])
    put(5, tall[:, COLS:])


def unpack_weights(g, ch, w):
    def one(pair):
        z, x, c = pair // (NX * NC), (pair // NC) % NX, pair % NC
        a = g[ch, z, x, c, 0].astype(F32)
        b = g[ch, z, x, c, 1].astype(F32)
        for unit in range(2):
            base = 48 * unit
            left = jnp.concatenate([a[base : base + 24], b[base : base + 24]], axis=0)
            right = jnp.concatenate([a[base + 24 : base + 48], b[base + 24 : base + 48]], axis=0)
            at = WIDTH * (2 * ch + unit)
            rows = pl.ds(pl.multiple_of(48 * pair, 48), 48)
            w[rows, at : at + COLS] = left.astype(BF)
            w[rows, at + COLS : at + WIDTH] = right.astype(BF)

    loop(GROUP, one)


def spread(gv, vec, ib):
    owners = GROUP * NY
    parts = gv[...].astype(F32).reshape(owners, 16, 128)
    across = lax.broadcasted_iota(jnp.int32, (128, WIDTH), 1)
    lane = lax.broadcasted_iota(jnp.int32, (128, WIDTH), 0)
    device = lax.broadcasted_iota(jnp.int32, (owners, 8, WIDTH), 0)
    col = lax.broadcasted_iota(jnp.int32, (owners, 8, WIDTH), 2)

    def placed(flat, size, start):
        pick = (rem(across + start, size) == lane).astype(F32).astype(BF)
        wide = jnp.dot(flat, pick, preferred_element_type=F32).reshape(owners, 8, WIDTH)
        first = device * size - start
        return jnp.sum(jnp.where((col >= first) & (col < first + size), wide, 0.0), axis=0)

    vec[...] = placed(parts[:, 0:8].reshape(owners * 8, 128).astype(BF), 24, 0)
    flat = parts[:, 8:16].reshape(owners * 8, 128).astype(BF)
    for i in range(4):
        total = placed(flat, 96, WIDTH * i)[0:1]
        ib[:, WIDTH * i : WIDTH * (i + 1)] = jnp.broadcast_to(total, (8, WIDTH))


class Scatter:
    def __init__(self, at, s, r1, rd0, rd1, rx, ry, rz, early, cs, p2, p1, zs):
        self.at, self.s = at, s
        self.early = early
        self.r1, self.rd0, self.rd1, self.rx, self.ry, self.rz = r1, rd0, rd1, rx, ry, rz
        self.cs, self.p2, self.p1, self.zs = cs, p2, p1, zs

    def c_copy(self, ch):
        at = self.at
        return remote(self.s.at[ch, :, :, at.oc], self.r1.at[ch], self.cs, (ch,), at.to_c)

    def zs_of(self, ch, k):
        return slice(None) if k is None else pl.ds(self.at.above(k), 1)

    def p2_copies(self, ch, k=None):
        at, some, index = self.at, self.zs_of(ch, k), k or 0
        head, tail = pl.ds(0, CUT), pl.ds(CUT, ROWS - CUT)
        corner = self.s.at[ch, some, at.ox, at.c, at.oy]
        return (
            remote(corner.at[:, head], self.rd0.at[ch, some], self.p2, (ch, index, 0), at.to_x),
            remote(corner.at[:, tail], self.rd1.at[ch, some], self.p2, (ch, index, 1), at.to_y),
        )

    def p1_copies(self, ch, k=None):
        at, some, index = self.at, self.zs_of(ch, k), k or 0
        return (
            remote(self.s.at[ch, some, at.ox, at.c, at.y], self.rx.at[ch, some], self.p1, (ch, index, 0), at.to_x),
            remote(self.s.at[ch, some, at.x, at.c, at.oy], self.ry.at[ch, some], self.p1, (ch, index, 1), at.to_y),
        )

    def z_copy(self, ch, k):
        at = self.at
        return remote(
            self.s.at[ch, at.above(k), at.x, at.c, at.y], self.rz.at[ch, k - 1], self.zs, (ch, k - 1), at.to_z(k)
        )

    def start(self, ch):
        self.c_copy(ch).start()

    def add_core(self, ch, x, y):
        def one(z):
            total = self.s[ch, z, x, self.at.c, y].astype(F32) + self.r1[ch, z, x, y].astype(F32)
            self.s[ch, z, x, self.at.c, y] = total.astype(BF)

        loop(NZ, one)

    def core(self, ch):
        at = self.at
        self.c_copy(ch).wait_recv()
        self.add_core(ch, at.ox, at.oy)
        for k in (1, 2, 3, 0) if ch in FINE else (None,):
            for copy in self.p2_copies(ch, k):
                copy.start()
        self.add_core(ch, at.ox, at.y)
        self.add_core(ch, at.x, at.oy)
        self.add_core(ch, at.x, at.y)

    def over(self, k, work):
        if k is None:
            loop(NZ, work)
        else:
            work(self.at.above(k))

    def diagonal(self, ch, k=None):
        at = self.at
        over_x, over_y = self.p2_copies(ch, k)
        to_x, to_y = self.p1_copies(ch, k)
        head, tail = pl.ds(0, CUT), pl.ds(CUT, ROWS - CUT)
        over_x.wait_recv()

        def first(z):
            total = self.s[ch, z, at.x, at.c, at.oy, head].astype(F32) + self.rd0[ch, z].astype(F32)
            self.s[ch, z, at.x, at.c, at.oy, head] = total.astype(BF)

        self.over(k, first)
        to_y.start()
        over_y.wait_recv()

        def second(z):
            total = self.s[ch, z, at.ox, at.c, at.y, tail].astype(F32) + self.rd1[ch, z].astype(F32)
            self.s[ch, z, at.ox, at.c, at.y, tail] = total.astype(BF)

        self.over(k, second)
        to_x.start()

    def plane(self, ch, k=None):
        at = self.at
        for copy in self.p1_copies(ch, k):
            copy.wait_recv()

        def one(z):
            total = self.s[ch, z, at.x, at.c, at.y].astype(F32) + self.rx[ch, z].astype(F32)
            total = total + self.ry[ch, z].astype(F32)
            self.s[ch, z, at.x, at.c, at.y] = total.astype(BF)

        self.over(k, one)
        for j in range(1, NZ) if k is None else (k,) if k else ():
            self.z_copy(ch, j).start()

    def finish(self, ch):
        at = self.at
        for k in range(1, NZ):
            self.z_copy(ch, k).wait_recv()
        total = self.s[ch, at.z, at.x, at.c, at.y].astype(F32)
        for k in range(NZ - 1):
            total = total + self.rz[ch, k].astype(F32)
        return total

    def drain(self, ch):
        self.c_copy(ch).wait_send()
        for k in range(NZ) if ch in FINE else (None,):
            for copy in (*self.p2_copies(ch, k), *self.p1_copies(ch, k)):
                copy.wait_send()
        for k in range(1, NZ):
            self.z_copy(ch, k).wait_send()


    def early_z(self):
        at = self.at
        return [
            remote(self.s.at[0, at.above(k), :, at.c], self.early.at[k - 1], self.zs, (0, k - 1), at.to_z(k))
            for k in range(1, NZ)
        ]

    def early_p2(self):
        at = self.at
        head, tail = pl.ds(0, CUT), pl.ds(CUT, ROWS - CUT)
        return (
            remote(self.s.at[0, at.z, at.ox, at.c, at.oy, head], self.rd0.at[0, 0], self.p2, (0, 0, 0), at.to_x),
            remote(self.s.at[0, at.z, at.ox, at.c, at.oy, tail], self.rd1.at[0, 0], self.p2, (0, 0, 1), at.to_y),
        )

    def early_p1(self):
        at = self.at
        return (
            remote(self.s.at[0, at.z, at.ox, at.c, at.y], self.rx.at[0, 0], self.p1, (0, 0, 0), at.to_x),
            remote(self.s.at[0, at.z, at.x, at.c, at.oy], self.ry.at[0, 0], self.p1, (0, 0, 1), at.to_y),
        )

    def early_core(self):
        at = self.at
        self.c_copy(0).wait_recv()

        def one(i):
            z, x, y = i // (NX * NY), rem(i // NY, NX), rem(i, NY)
            total = self.s[0, z, x, at.c, y].astype(F32) + self.r1[0, z, x, y].astype(F32)
            self.s[0, z, x, at.c, y] = total.astype(BF)

        loop(NZ * NX * NY, one)
        for copy in self.early_z():
            copy.start()

    def early_plane(self):
        at = self.at
        for copy in self.early_z():
            copy.wait_recv()

        def one(i):
            x, y = i // NY, rem(i, NY)
            total = self.s[0, at.z, x, at.c, y].astype(F32)
            for k in range(NZ - 1):
                total = total + self.early[k, x, y].astype(F32)
            self.s[0, at.z, x, at.c, y] = total.astype(BF)

        loop(NX * NY, one)
        for copy in self.early_p2():
            copy.start()

    def early_diagonal(self):
        at = self.at
        over_x, over_y = self.early_p2()
        to_x, to_y = self.early_p1()
        head, tail = pl.ds(0, CUT), pl.ds(CUT, ROWS - CUT)
        over_x.wait_recv()
        total = self.s[0, at.z, at.x, at.c, at.oy, head].astype(F32) + self.rd0[0, 0].astype(F32)
        self.s[0, at.z, at.x, at.c, at.oy, head] = total.astype(BF)
        to_y.start()
        over_y.wait_recv()
        total = self.s[0, at.z, at.ox, at.c, at.y, tail].astype(F32) + self.rd1[0, 0].astype(F32)
        self.s[0, at.z, at.ox, at.c, at.y, tail] = total.astype(BF)
        to_x.start()

    def early_finish(self):
        at = self.at
        for copy in self.early_p1():
            copy.wait_recv()
        total = self.s[0, at.z, at.x, at.c, at.y].astype(F32) + self.rx[0, 0].astype(F32)
        return total + self.ry[0, 0].astype(F32)

    def early_drain(self):
        for copy in (self.c_copy(0), *self.early_z(), *self.early_p2(), *self.early_p1()):
            copy.wait_send()


def unfold(total, unit):
    base = 48 * unit
    return jnp.concatenate([total[base : base + 24], total[base + 24 : base + 48]], axis=1)


class VectorScatter:
    def __init__(self, at, s, rc, rx, ry, rz, sems):
        self.at, self.s = at, s
        self.rc, self.rx, self.ry, self.rz, self.sems = rc, rx, ry, rz, sems
        at = self.at
        self.cc = remote(s.at[:, :, at.oc], rc, sems, 0, at.to_c)
        self.xx = remote(s.at[:, at.ox, at.c], rx, sems, 1, at.to_x)
        self.yy = remote(s.at[:, at.x, at.c, at.oy], ry, sems, 2, at.to_y)
        self.zz = [
            remote(s.at[at.above(k), at.x, at.c, at.y], rz.at[k - 1], sems, 2 + k, at.to_z(k)) for k in range(1, NZ)
        ]

    def start(self):
        self.cc.start()

    def core(self):
        self.cc.wait_recv()
        self.s[:, :, self.at.c] = self.s[:, :, self.at.c] + self.rc[...]
        self.xx.start()

    def over_x(self):
        at = self.at
        self.xx.wait_recv()
        self.s[:, at.x, at.c] = self.s[:, at.x, at.c] + self.rx[...]
        self.yy.start()

    def over_y(self):
        at = self.at
        self.yy.wait_recv()
        self.s[:, at.x, at.c, at.y] = self.s[:, at.x, at.c, at.y] + self.ry[...]
        for copy in self.zz:
            copy.start()

    def finish(self):
        at = self.at
        for copy in self.zz:
            copy.wait_recv()
        return self.s[at.z, at.x, at.c, at.y] + self.rz[0] + self.rz[1] + self.rz[2]

    def drain(self):
        for copy in [self.cc, self.xx, self.yy] + self.zz:
            copy.wait_send()


def own_part(value, stride):
    if stride == 1:
        return value
    whole = lax.all_gather(value, ("dp", "blk"), axis=0, tiled=True)
    rows = whole.shape[0] // (GROUP * NY)
    index = (lax.axis_index("dp") // stride) * NY + lax.axis_index("blk")
    return lax.dynamic_slice_in_dim(whole, index * rows, rows, axis=0)


def fine_part(value, stride):
    if stride == 1:
        return value
    index = (lax.axis_index("dp") // stride) * NY + lax.axis_index("blk")
    rows = value.shape[0]
    whole = jnp.zeros((rows * GROUP * NY,) + value.shape[1:], value.dtype)
    whole = lax.dynamic_update_slice_in_dim(whole, value, index * rows, axis=0)
    return lax.psum_scatter(whole, ("dp", "blk"), scatter_dimension=0, tiled=True)


def product(left, right):
    return jnp.dot(left, right, preferred_element_type=F32)


def product_left(left, right):
    return lax.dot_general(left, right, (((0,), (0,)), ((), ())), preferred_element_type=F32)


def product_right(left, right):
    return lax.dot_general(left, right, (((1,), (1,)), ((), ())), preferred_element_type=F32)


def tile(i, size):
    return pl.ds(pl.multiple_of(i * size, size), size)


def mean(values):
    return jnp.mean(values, axis=-1, keepdims=True)


def column(values):
    return jnp.sum(values, axis=0, keepdims=True)


def gather_vectors(vg, ibg, sv):
    owners = GROUP * NY
    across = lax.broadcasted_iota(jnp.int32, (WIDTH, 128), 0)
    lane = lax.broadcasted_iota(jnp.int32, (WIDTH, 128), 1)

    def pieces(wide, size, start):
        pick = ((rem(across + start, size) == lane) & (lane < size)).astype(F32).astype(BF)
        high = wide.astype(BF)
        rest = (wide - high.astype(F32)).astype(BF)
        return product(high, pick) + product(rest, pick)

    def owned(shape, size, start):
        first = lax.broadcasted_iota(jnp.int32, shape, 0) * size - start
        col = lax.broadcasted_iota(jnp.int32, shape, len(shape) - 1)
        return (col >= first) & (col < first + size)

    wide = jnp.where(owned((owners, 8, WIDTH), 24, 0), vg[...][None], 0.0)
    total = pieces(wide.reshape(owners * 8, WIDTH), 24, 0)
    sv[:, :, :, :, 0:8] = total.reshape(NZ, NX, NC, NY, 8, 128)
    total = jnp.zeros((owners, 128), F32)
    for i in range(4):
        part = ibg[0:1, WIDTH * i : WIDTH * (i + 1)]
        wide = jnp.where(owned((owners, WIDTH), 96, WIDTH * i), part, 0.0)
        total = total + pieces(wide, 96, WIDTH * i)
    total = jnp.broadcast_to(total[:, None, :], (owners, 8, 128))
    sv[:, :, :, :, 8:16] = total.reshape(NZ, NX, NC, NY, 8, 128)


def play(schedule, steps, loops):
    at = 0
    while at < len(schedule):
        name, *numbers = schedule[at].split()
        numbers = [int(n) for n in numbers]
        if name not in loops:
            steps[name](*numbers)
            at += 1
            continue
        turns = [i for i, entry in enumerate(schedule) if entry.split()[0] == name]
        between = [schedule[i + 1 : j] for i, j in zip(turns, turns[1:])]

        def turn(i):
            loops[name](i)
            for index, entries in enumerate(between):
                if entries:
                    pl.when(i == index)(partial(play, entries, steps, {}))

        loop(len(turns), turn)
        at = turns[-1] + 1


QB, VB, OB, G1, S1, UB, G2, S2 = range(8)


def layer_kernel(
    stride,
    q, k, v, o, inner, outer, small, hidden, grad, mask,
    out, igrad, dq, dk, dv, do, di, du, dsmall, saved,
    g, gv, wd, u, page, cot, dead, hid, qkv, outp, xt, hidt, ctxt,
    n1, inv1, acc1, acc2, dst, bias, vec, ib, vg, ibg,
    sv, r1, rd0, rd1, rx, ry, rz, early, vc, vx, vy, vz,
    zs, zr, p1s, p1r, p2s, p2r, cs, cr, vs, vr, es, er,
    css, csr, q2s, q2r, q1s, q1r, zss, zsr, ws, wr, loads, saves,
):
    at = Place(stride)
    gather = Gather(at, g, (zs, zr), (p1s, p1r), (p2s, p2r), (cs, cr))
    scatter = Scatter(
        at, g, r1, rd0, rd1, rx, ry, rz, early, (css, csr), (q2s, q2r), (q1s, q1r), (zss, zsr)
    )
    vector = VectorScatter(at, sv, vc, vx, vy, vz, (ws, wr))

    def put(ch, value):
        g[ch, at.z, at.x, at.c, at.y] = value

    at.hail()
    pack_weights((q, k, v, o, inner, outer), put)
    gv[at.z, at.x, at.c, at.y] = small[...]
    own = pl.ds(pl.multiple_of(at.y * 256, 256), 256)
    theirs = pl.ds(pl.multiple_of(at.oy * 256, 256), 256)
    local = [
        pltpu.make_async_copy(hidden.at[at.y], page.at[own], loads.at[0]),
        pltpu.make_async_copy(grad.at[at.y], cot.at[own], loads.at[1]),
    ]
    for copy in local:
        copy.start()
    at.meet()

    ve, ee = (vs, vr), (es, er)
    page_in = remote(hidden.at[at.oy], page.at[own], ee, 0, at.to_y)
    mask_in = remote(mask.at[at.oy], dead.at[at.y], ee, 1, at.to_y)
    grad_in = remote(grad.at[at.oy], cot.at[own], ee, 2, at.to_y)
    out_over = remote(outp.at[theirs], out.at[at.y], ee, 3, at.to_y)
    grad_over = remote(cot.at[theirs], igrad.at[at.y], ee, 4, at.to_y)
    swaps = [page_in, mask_in, grad_in, out_over, grad_over]
    mine = gv.at[at.z, at.x, at.c, at.y]
    line = gv.at[:, at.x, at.c, at.y]
    pairs = gv.at[:, :, at.c, at.y]
    core = gv.at[:, :, at.c]
    vzs = [remote(mine, mine, ve, kk - 1, at.to_z(kk)) for kk in range(1, NZ)]
    vxs = remote(line, line, ve, 3, at.to_x)
    vys = remote(pairs, pairs, ve, 4, at.to_y)
    vcs = remote(core, core, ve, 5, at.to_c)

    def vector_z():
        for copy in vzs:
            copy.start()

    def vector_x():
        for copy in vzs:
            copy.wait_recv()
        vxs.start()

    def vector_y():
        vxs.wait_recv()
        vys.start()

    def vector_c():
        vys.wait_recv()
        vcs.start()

    def page_start():
        page_in.start()
        mask_in.start()

    def page_wait():
        for copy in local:
            copy.wait()
        page_in.wait_recv()
        mask_in.wait_recv()

    def turn(i):
        xt[tile(i, 256), :] = page[:, tile(i, 256)].T

    def prepare():
        dead[at.y] = mask[at.y]
        loop(3, turn)
        for half in range(2):
            bias[256 * half : 256 * half + 256] = jnp.broadcast_to(dead[half, 0:1].T, (256, 128))
        spread(gv, vec, ib)

    def queries(i):
        cols = tile(i, 256)
        value = product(page[...], wd[:, cols]) + vec[QB : QB + 1, cols]
        qkv[:, cols] = (value.astype(BF).astype(F32) * 0.125).astype(BF)

    def keys(i):
        cols = tile(i + 3, 256)
        qkv[:, cols] = product(page[...], wd[:, cols]).astype(BF)

    def vals(i):
        cols = tile(i + 6, 256)
        value = product(page[...], wd[:, cols]) + vec[VB : VB + 1, tile(i, 256)]
        qkv[:, cols] = value.astype(BF)

    def queries_keys():
        loop(3, queries)
        loop(3, keys)

    lane = lax.broadcasted_iota(jnp.int32, (512, 128), 1)
    sides = (lane < 64, lane >= 64)

    def side(value, which):
        return jnp.where(sides[which], value.astype(F32), 0.0).astype(BF)

    def save(pair):
        cols = tile(pair, 1024)
        return pltpu.make_async_copy(u.at[:, cols], saved.at[:, cols], saves.at[pair])

    def attend(pair):
        at_q, at_k, at_v = tile(pair, 128), tile(pair + 6, 128), tile(pair + 12, 128)
        k2, v2 = qkv[:, at_k], qkv[:, at_v]
        total = jnp.zeros((128, 512), F32)
        for a in range(2):
            ka, va = side(k2, a), side(v2, a)
            for h in range(2):
                q2 = qkv[256 * h : 256 * h + 256, at_q]
                s = product_right(ka, q2) + jnp.concatenate([bias[...], bias[...]], axis=1)
                e = jnp.exp(s - jnp.max(s, axis=0, keepdims=True))
                p = e * (1.0 / jnp.sum(e, axis=0, keepdims=True))
                cols = pl.ds(pl.multiple_of(1024 * pair + 512 * a + 256 * h, 256), 256)
                u[:, cols] = p.astype(BF)
            cols = pl.ds(pl.multiple_of(1024 * pair + 512 * a, 512), 512)
            total = total + product_left(va, u[:, cols])
        ctxt[tile(pair, 128), :] = total.astype(BF)
        outp[:, tile(pair, 128)] = total.T.astype(BF)
        save(pair).start()

    def attended(i):
        cols = tile(i, 256)
        value = product(outp[...], wd[:, tile(i + 9, 256)]) + vec[OB : OB + 1, cols]
        acc1[:, cols] = page[:, cols].astype(F32) + value

    def first_norm(i):
        rows = tile(i, 64)
        joined = acc1[rows, :]
        center = joined - mean(joined)
        inverse = lax.rsqrt(mean(center * center) + EPSILON)
        normed = center * inverse
        n1[rows, :] = normed
        inv1[rows, :] = jnp.broadcast_to(inverse, (64, 128))
        hid[rows, :] = (normed * vec[G1 : G1 + 1] + vec[S1 : S1 + 1]).astype(BF)

    def turn_hidden(i):
        hidt[tile(i, 256), :] = hid[:, tile(i, 256)].T

    def after_attention():
        loop(3, attended)
        loop(8, first_norm)
        loop(3, turn_hidden)
        loop(6, lambda i: save(i).wait())

    def feed(i):
        cols = tile(i, 384)
        weight = wd[:, pl.ds(pl.multiple_of(4 * WIDTH + 384 * i, 384), 384)]
        acc1[:, 0:384] = product(hid[...], weight) + ib[0:1, cols]

        def one(r):
            rows = tile(r, 64)
            value = acc1[rows, 0:384]
            cdf = 0.5 + 0.5 * lax.erf(value * 0.7071067811865476)
            density = 0.3989422804014327 * jnp.exp(-0.5 * value * value)
            u[rows, cols] = (value * cdf).astype(BF)
            u[rows, pl.ds(pl.multiple_of(3072 + 384 * i, 384), 384)] = (cdf + value * density).astype(BF)

        loop(8, one)

    def outer_half(half):
        cols = slice(COLS * half, COLS * half + COLS)
        weight = g[4 + half].reshape(8 * COLS, COLS)
        acc1[:, cols] = product(u[:, 0:3072], weight)

    def second_norm(i):
        rows = tile(i, 64)
        second = hid[rows, :].astype(F32) + (acc1[rows, :] + vec[UB : UB + 1])
        center = second - mean(second)
        inverse = lax.rsqrt(mean(center * center) + EPSILON)
        normed = center * inverse
        gain = vec[G2 : G2 + 1]
        outp[rows, :] = (normed * gain + vec[S2 : S2 + 1]).astype(BF)
        dy = cot[rows, :].astype(F32)
        vg[G2 : G2 + 1] += column(dy * normed)
        vg[S2 : S2 + 1] += column(dy)
        scaled = dy * gain
        back = inverse * (scaled - mean(scaled) - normed * mean(scaled * normed))
        acc2[rows, :] = back
        low = back.astype(BF)
        page[rows, :] = low
        vg[UB : UB + 1] += column(low.astype(F32))

    play(
        FORWARD,
        {
            "z": gather.start_z,
            "own": gather.start_own,
            "plane": gather.plane,
            "turn": gather.turn,
            "cross": gather.cross,
            "arrive": gather.arrive,
            "late_z": gather.late_z,
            "late_cross": gather.late_cross,
            "vector_z": vector_z,
            "vector_x": vector_x,
            "vector_y": vector_y,
            "vector_c": vector_c,
            "vector_wait": vcs.wait_recv,
            "page": page_start,
            "page_wait": page_wait,
            "grad": grad_in.start,
            "grad_wait": grad_in.wait_recv,
            "prepare": prepare,
            "unpack": lambda ch: unpack_weights(g, ch, wd),
            "queries_keys": queries_keys,
            "values": lambda: loop(3, vals),
            "after_attention": after_attention,
            "outer": outer_half,
        },
        {"attend": attend, "feed": feed, "feed_on": lambda i: feed(i + 4)},
    )
    vg[...] = jnp.zeros_like(vg)
    loop(8, second_norm)

    low = page
    keep = pltpu.make_async_copy(outp.at[own], out.at[at.y], loads.at[0])
    loop(CHUNKS - 1, gather.drain)
    gather.late_drain()

    def out_start():
        out_over.start()
        keep.start()

    def outer_grad(half, slot):
        def one(i):
            z, x = i // 2, rem(i, 2)
            cols = slice(COLS * half, COLS * half + COLS)
            value = product_left(u[:, tile(i, 384)], low[:, cols]).astype(BF)
            g[slot, z, x] = value.reshape(NC, NY, ROWS, COLS)

        loop(8, one)

    def load(part):
        cols = pl.ds(3072 * part, 3072)
        return pltpu.make_async_copy(saved.at[:, cols], u.at[:, cols], loads.at[1])

    def inner_back(i):
        z, x = i // 2, rem(i, 2)
        value = product_right(low[:, 0:COLS], g[4, z, x].reshape(COLS, COLS))
        value = value + product_right(low[:, COLS:], g[5, z, x].reshape(COLS, COLS))
        cols = pl.ds(pl.multiple_of(3072 + 384 * i, 384), 384)
        value = (value * u[:, cols].astype(F32)).astype(BF)
        u[:, cols] = value
        total = column(value.astype(F32))
        ibg[:, tile(i, 384)] = jnp.broadcast_to(total, (8, 384))

    def weight_grad(slot, unit, left, right):
        def one(i):
            value = product(left[tile(i, 384), :], right)
            value = value.reshape(16, 24, WIDTH)
            value = jnp.concatenate([value[:, :, :COLS], value[:, :, COLS:]], axis=1).astype(BF)
            g[slot, pl.ds(2 * i, 2), :, :, :, 48 * unit : 48 * unit + 48, :] = value.reshape(
                2, NX, NC, NY, 48, COLS
            )

        loop(2, one)

    def inner_grad(unit):
        right = u[:, 3072 + WIDTH * unit : 3072 + WIDTH * (unit + 1)]
        weight_grad(2 + unit // 2, unit % 2, hidt, right)

    def hidden_back(i):
        cols = tile(i, 256)
        acc2[:, cols] = acc2[:, cols] + product_right(u[:, 3072:6144], wd[cols, 4 * WIDTH :])

    def first_back(i):
        rows = tile(i, 64)
        up = acc2[rows, :]
        normed = n1[rows, :]
        vg[G1 : G1 + 1] += column(up * normed)
        vg[S1 : S1 + 1] += column(up)
        scaled = up * vec[G1 : G1 + 1]
        inverse = inv1[rows, 0:1]
        back = inverse * (scaled - mean(scaled) - normed * mean(scaled * normed))
        acc2[rows, :] = back
        short = back.astype(BF)
        low[rows, :] = short
        vg[OB : OB + 1] += column(short.astype(F32))

    def context_back(i):
        cols = tile(i, 256)
        hid[:, cols] = product_right(low[...], wd[cols, 3 * WIDTH : 4 * WIDTH]).astype(BF)

    def attend_back(pair):
        at_q, at_k, at_v = tile(pair, 128), tile(pair + 6, 128), tile(pair + 12, 128)
        q2, k2, v2, c2 = qkv[:, at_q], qkv[:, at_k], qkv[:, at_v], hid[:, at_q]
        dqt = jnp.zeros((128, 512), F32)
        dk2 = jnp.zeros((512, 128), F32)
        dv2 = jnp.zeros((512, 128), F32)
        for a in range(2):
            va = side(v2, a)
            for h in range(2):
                cols = pl.ds(pl.multiple_of(1024 * pair + 512 * a + 256 * h, 256), 256)
                p = u[:, cols].astype(F32)
                d = product_right(va, c2[256 * h : 256 * h + 256])
                delta = jnp.sum(p * d, axis=0, keepdims=True)
                dst[:, 256 * h : 256 * h + 256] = (p * (d - delta)).astype(BF)
            cols = pl.ds(pl.multiple_of(1024 * pair + 512 * a, 512), 512)
            dv2 = dv2 + product(u[:, cols], side(c2, a))
            dk2 = dk2 + product(dst[...], side(q2, a))
            dqt = dqt + product_left(side(k2, a), dst[...])
        qkv[:, at_q] = (dqt.T * 0.125).astype(BF)
        qkv[:, at_k] = dk2.astype(BF)
        qkv[:, at_v] = dv2.astype(BF)

    def sums(i):
        rows = tile(i, 64)
        vg[QB : QB + 1] += column(qkv[rows, 0:WIDTH].astype(F32))
        vg[VB : VB + 1] += column(qkv[rows, 2 * WIDTH : 3 * WIDTH].astype(F32))

    def input_back(i):
        cols = tile(i, 256)
        value = acc2[:, cols] + product_right(qkv[...], wd[cols, 0 : 3 * WIDTH])
        cot[:, cols] = value.astype(BF)

    keep_in = pltpu.make_async_copy(cot.at[own], igrad.at[at.y], loads.at[1])

    def grad_start():
        grad_over.start()
        keep_in.start()

    def finish(n):
        total = scatter.finish(n) if n else scatter.early_finish()
        if n < 2:
            half = 1 - n
            du[:, COLS * half : COLS * half + COLS] = total
        elif n < 4:
            for unit in range(2):
                index = 2 * (n - 2) + unit
                di[:, WIDTH * index : WIDTH * (index + 1)] = unfold(total, unit)
        else:
            first, second = (dv, do) if n == 4 else (dq, dk)
            first[...] = unfold(total, 0)
            second[...] = unfold(total, 1)

    def vector_finish():
        dsmall[...] = vector.finish()

    def context_grad():
        load(1).start()
        loop(3, context_back)
        load(1).wait()

    def outer_second():
        outer_grad(1, 0)
        load(0).start()

    def output_grad():
        weight_grad(4, 1, ctxt, low[...])

    def first_grad():
        loop(8, first_back)
        load(0).wait()

    play(
        BACKWARD,
        {
            "start": scatter.start,
            "core": scatter.core,
            "diagonal": scatter.diagonal,
            "plane": scatter.plane,
            "finish": finish,
            "early_core": scatter.early_core,
            "early_plane": scatter.early_plane,
            "early_diagonal": scatter.early_diagonal,
            "vector": vector.start,
            "vector_core": vector.core,
            "vector_x": vector.over_x,
            "vector_y": vector.over_y,
            "vector_finish": vector_finish,
            "out": out_start,
            "grad": grad_start,
            "outer_first": lambda: outer_grad(0, 1),
            "outer_second": outer_second,
            "inner_grad": inner_grad,
            "first_back": first_grad,
            "output_grad": output_grad,
            "context_back": context_grad,
            "value_grad": lambda: weight_grad(4, 0, xt, qkv[:, 2 * WIDTH : 3 * WIDTH]),
            "query_grad": lambda: weight_grad(5, 0, xt, qkv[:, 0:WIDTH]),
            "key_grad": lambda: weight_grad(5, 1, xt, qkv[:, WIDTH : 2 * WIDTH]),
            "sums": lambda: loop(8, sums),
            "gather_vectors": lambda: gather_vectors(vg, ibg, sv),
        },
        {
            "inner_back": inner_back,
            "hidden_back": hidden_back,
            "attend_back": attend_back,
            "input_back": input_back,
        },
    )
    keep.wait()
    keep_in.wait()
    out_over.wait_recv()
    grad_over.wait_recv()
    for n in range(1, CHUNKS):
        scatter.drain(n)
    scatter.early_drain()
    vector.drain()
    for copy in vzs + [vxs, vys, vcs] + swaps:
        copy.wait_send()


def layer_call(stride, args):
    vmem = pl.BlockSpec(memory_space=pltpu.VMEM)
    hbm = pl.BlockSpec(memory_space=pl.ANY)
    dma = pltpu.SemaphoreType.DMA

    def shape(*dims, kind=F32):
        return jax.ShapeDtypeStruct(dims, kind)

    tokens = [shape(2, 256, WIDTH, kind=BF)] * 2
    grads = [shape(24, WIDTH)] * 4 + [shape(24, 4 * WIDTH), shape(96, WIDTH), shape(16, 128)]

    def low(*dims):
        return pltpu.VMEM(dims, BF)

    def full(*dims):
        return pltpu.VMEM(dims, F32)

    def pair(*dims):
        return [dma(dims), dma(dims)]

    return pl.pallas_call(
        partial(layer_kernel, stride),
        out_shape=tuple(tokens + grads + [shape(512, 12 * 512, kind=BF)]),
        in_specs=[vmem] * 7 + [hbm, hbm, vmem],
        out_specs=tuple([hbm] * 2 + [vmem] * len(grads) + [hbm]),
        scratch_shapes=[
            low(CHUNKS, NZ, NX, NC, NY, ROWS, COLS),
            low(NZ, NX, NC, NY, 16, 128),
            low(WIDTH, 8 * WIDTH),
            low(512, 12 * 512),
            low(512, WIDTH),
            low(512, WIDTH),
            full(2, 8, 256),
            low(512, WIDTH),
            low(512, 3 * WIDTH),
            low(512, WIDTH),
            low(WIDTH, 512),
            low(WIDTH, 512),
            low(WIDTH, 512),
            full(512, WIDTH),
            full(512, 128),
            full(512, WIDTH),
            full(512, WIDTH),
            low(512, 512),
            full(512, 128),
            full(8, WIDTH),
            full(8, 4 * WIDTH),
            full(8, WIDTH),
            full(8, 4 * WIDTH),
            full(NZ, NX, NC, NY, 16, 128),
            low(CHUNKS, NZ, NX, NY, ROWS, COLS),
            low(CHUNKS, NZ, CUT, COLS),
            low(CHUNKS, NZ, ROWS - CUT, COLS),
            low(CHUNKS, NZ, ROWS, COLS),
            low(CHUNKS, NZ, ROWS, COLS),
            low(CHUNKS, NZ - 1, ROWS, COLS),
            low(NZ - 1, NX, NY, ROWS, COLS),
            full(NZ, NX, NY, 16, 128),
            full(NZ, NY, 16, 128),
            full(NZ, 16, 128),
            full(NZ - 1, 16, 128),
            *pair(CHUNKS, NZ - 1),
            *pair(CHUNKS, NZ, 2),
            *pair(CHUNKS, NZ, 2),
            *pair(CHUNKS),
            *pair(6),
            *pair(5),
            *pair(CHUNKS),
            *pair(CHUNKS, NZ, 2),
            *pair(CHUNKS, NZ, 2),
            *pair(CHUNKS, NZ - 1),
            *pair(6),
            dma((2,)),
            dma((6,)),
        ],
        compiler_params=pltpu.CompilerParams(
            collective_id=0, has_side_effects=True, vmem_limit_bytes=VMEM_LIMIT
        ),
        name="layer",
    )(*args)


def hand_out_kernel(*refs):
    large, small, outs, vectors = refs[:8], refs[8], refs[9:17], refs[17:26]
    held, into, back = refs[26:34], refs[34], refs[35]
    loads = [pltpu.make_async_copy(a, b, into.at[i]) for i, (a, b) in enumerate(zip(large, held))]
    stores = [pltpu.make_async_copy(a, b, back.at[i]) for i, (a, b) in enumerate(zip(held, outs))]
    for copy in loads:
        copy.start()
    for i, ref in enumerate(vectors):
        ref[...] = small[i, : ref.shape[0]]
    for load, store in zip(loads, stores):
        load.wait()
        store.start()
    for store in stores:
        store.wait()


def hand_out(large, small):
    vmem = pl.BlockSpec(memory_space=pltpu.VMEM)
    hbm = pl.BlockSpec(memory_space=pl.ANY)
    vectors = [jax.ShapeDtypeStruct((24,), F32)] * 8 + [jax.ShapeDtypeStruct((96,), F32)]
    return pl.pallas_call(
        hand_out_kernel,
        out_shape=tuple([jax.ShapeDtypeStruct(v.shape, v.dtype) for v in large] + vectors),
        in_specs=[hbm] * 8 + [vmem],
        out_specs=tuple([hbm] * 8 + [vmem] * 9),
        scratch_shapes=[pltpu.VMEM(v.shape, v.dtype) for v in large]
        + [pltpu.SemaphoreType.DMA((8,)), pltpu.SemaphoreType.DMA((8,))],
        name="hand_out",
    )(*large, small)


def body(
    stride,
    hidden_in,
    page_lengths,
    pad_mask,
    query_weight,
    query_bias,
    key_weight,
    value_weight,
    value_bias,
    output_weight,
    output_bias,
    first_gain,
    first_shift,
    inner_weight,
    inner_bias,
    outer_weight,
    outer_bias,
    second_gain,
    second_shift,
    out_grad,
):
    coarse = partial(own_part, stride=stride)
    fine = partial(fine_part, stride=stride)
    place = lax.axis_index("blk")
    segment = hidden_in.shape[1]
    positions = place * segment + jnp.arange(segment, dtype=jnp.int32)
    live = (positions[None, :] < page_lengths[:, None]) & (pad_mask == 1)
    mask = jnp.where(live, 0.0, NEG_FILL).astype(F32)
    mask = jnp.broadcast_to(mask[:, None, :], (2, 8, segment))
    vectors = (
        query_bias, value_bias, output_bias, first_gain, first_shift, outer_bias, second_gain, second_shift,
    )
    small = jnp.stack([coarse(v) for v in vectors])
    small = jnp.concatenate(
        [
            jnp.pad(small, ((0, 0), (0, 104))),
            jnp.pad(coarse(inner_bias)[None, :], ((0, 7), (0, 32))),
        ]
    )
    weights = [
        coarse(v) for v in (query_weight, key_weight, value_weight, output_weight, inner_weight, outer_weight)
    ]
    *large, dsmall, _ = layer_call(stride, (*weights, small, hidden_in, out_grad, mask))
    output, input_grad, *grads = hand_out(large, dsmall)
    dq, dk, dv, do, di, du, qbg, vbg, obg, g1g, s1g, ubg, g2g, s2g, ibg = [fine(v) for v in grads]
    return (
        output, input_grad, dq, qbg, dk, dv, vbg, do, obg, g1g, s1g, di, ibg, du, ubg, g2g, s2g,
    )


def solution(mesh):
    stride = mesh.shape["dp"] // GROUP
    row = P(("dp", "blk"))
    mat = P(("dp", "blk"), None)
    tok = P("dp", "blk", None)
    in_specs = (
        tok, P("dp"), P("dp", "blk"), mat, row, mat, mat, row, mat, row, row, row, mat, row, mat, row, row, row, tok,
    )
    out_specs = (
        tok, tok, mat, row, mat, mat, row, mat, row, row, row, mat, row, mat, row, row, row,
    )
    return jax.shard_map(
        partial(body, stride), mesh=mesh, in_specs=in_specs, out_specs=out_specs, check_vma=False
    )
```

```python
from functools import partial

import jax
import jax.numpy as jnp
from jax import lax
from jax.experimental import pallas as pl
from jax.experimental.pallas import tpu as pltpu
from jax.sharding import PartitionSpec as P

HEADS = 12
NEG_FILL = -1000000000.0
EPSILON = 1e-05

NZ, NX, NC, NY = 4, 2, 2, 2
GROUP = NZ * NX * NC
CHUNKS = 6
ROWS, COLS = 96, 384
LATE = 5
FINE_G, COARSE = (0, 1), (2, 3, 4)
G_STEPS = NZ * len(FINE_G) + len(COARSE) + 1
CUT = 64
WIDTH = 768
FINE = (4, 5)
S_STEPS = FINE[0] + NZ * len(FINE)
BF, F32 = jnp.bfloat16, jnp.float32
VMEM_LIMIT = 63 * 2**20

FORWARD = (
    "vector_z", "own 1", "z 0", "own 5", "page", "z 1", "turn 1 0", "own 0", "z 2", "plane 0 2", "vector_x",
    "plane 0 1", "z 3", "turn 5 0", "plane 0 3", "plane 1 1", "plane 1 2", "plane 1 3", "turn 0 2", "vector_y",
    "turn 0 1", "turn 0 0", "turn 0 3", "turn 1 1", "turn 1 2", "z 4", "turn 1 3", "plane_all 2", "vector_c",
    "vector_wait", "page_wait", "late_z", "cross 0", "cross 1", "plane_all 3", "arrive 0", "prepare",
    "arrive 1", "late_arrive 0", "unpack 1", "unpack 0", "queries_keys", "turn 2", "values", "attend 0",
    "plane_all 4", "attend 1", "turn 3", "attend 2", "attend 3", "cross 2", "attend 4", "attend 5",
    "after_attention", "arrive 2", "turn 4", "grad", "unpack 2", "feed 0", "late_cross 1", "feed 1", "cross 3",
    "feed 2", "late_arrive 1", "feed 3", "arrive 3", "unpack 3", "late_cross 3", "late_cross 2", "feed_on 4",
    "cross 4", "feed_on 5", "feed_on 6", "late_arrive 2", "feed_on 7", "arrive 4", "outer_left",
    "outer_right 0", "grad_wait", "outer_right 1", "late_arrive 3", "cotangent", "outer_right 2",
    "outer_right 3",
)
BACKWARD = (
    "out", "outer_first", "start 1", "outer_second", "start 0", "inner_back 0", "core 1", "inner_back 1",
    "early_core", "inner_back 2", "inner_back 3", "inner_grad 0", "diagonal 1", "inner_grad 1", "start 2",
    "inner_grad 2", "inner_grad 3", "hidden_back 0", "start 3", "hidden_back 1", "hidden_back 2", "core 2",
    "first_back", "output_grad", "core 3", "context_back", "diagonal 2", "attend_back 0", "plane 1",
    "attend_back 1", "attend_back 2", "diagonal 3", "attend_back 3", "attend_back 4", "attend_back 5",
    "value_grad", "start 4", "key_grad", "query_grad", "start 5", "sums", "plane 2", "core 4", "core 5",
    "diagonal 4 2", "early_plane", "plane 3", "diagonal 4 0", "gather_vectors", "vector", "diagonal 4 3",
    "diagonal 5 3", "vector_core", "diagonal 5 2", "early_diagonal", "finish 1", "input_back 0", "diagonal 4 1",
    "plane 4 2", "diagonal 5 1", "diagonal 5 0", "finish 3", "plane 4 3", "plane 4 0", "plane 5 3",
    "input_back 1", "vector_x", "input_back 2", "grad", "plane 5 2", "finish 2", "vector_y", "plane 4 1",
    "finish 0", "plane 5 1", "vector_finish", "plane 5 0", "finish 4", "finish 5",
)


def rem(a, b):
    return lax.rem(a, b)


class Place:
    def __init__(self, stride):
        dp = lax.axis_index("dp")
        self.y = lax.axis_index("blk")
        index = dp // stride
        self.low = dp - index * stride
        self.stride = stride
        self.z = index // (NX * NC)
        self.x = (index // NC) % NX
        self.c = index % NC
        self.ox, self.oy, self.oc = 1 - self.x, 1 - self.y, 1 - self.c

    def dev(self, z, x, c, y):
        return ((z * (NX * NC) + x * NC + c) * self.stride + self.low, y)

    def above(self, k):
        return rem(self.z + k, NZ)

    def below(self, k):
        return rem(self.z + NZ - k, NZ)

    def to_z(self, k):
        return self.dev(self.above(k), self.x, self.c, self.y)

    @property
    def to_x(self):
        return self.dev(self.z, self.ox, self.c, self.y)

    @property
    def to_y(self):
        return self.dev(self.z, self.x, self.c, self.oy)

    @property
    def to_c(self):
        return self.dev(self.z, self.x, self.oc, self.y)

    def hail(self):
        partners = [self.to_z(k) for k in range(1, NZ)] + [self.to_x, self.to_y, self.to_c]
        for who in partners:
            pl.semaphore_signal(
                pltpu.get_barrier_semaphore(), inc=1, device_id=who, device_id_type=pl.DeviceIdType.MESH
            )

    def meet(self):
        pl.semaphore_wait(pltpu.get_barrier_semaphore(), NZ + 2)


def remote(src, dst, sems, index, who, group=None):
    send, recv = sems
    return pltpu.make_async_remote_copy(
        src_ref=src,
        dst_ref=dst,
        send_sem=send.at[index if group is None else group],
        recv_sem=recv.at[index],
        device_id=who,
        device_id_type=pl.DeviceIdType.MESH,
    )


def loop(count, body):
    def step(i, carry):
        body(i)
        return carry

    lax.fori_loop(0, count, step, 0)


class Gather:
    def __init__(self, at, blocks, zs, p1, p2, cs):
        self.at, self.g = at, blocks
        self.zs, self.p1, self.p2, self.cs = zs, p1, p2, cs

    def z_copy(self, ch, k, mine=True):
        at = self.at
        z = at.z if mine else at.below(k)
        ref = self.g.at[ch, z, at.x, at.c, at.y]
        return remote(ref, ref, self.zs, (ch, k - 1), at.to_z(k), (ch,))

    def some(self, ch, k):
        if ch in COARSE:
            return slice(None), NZ * len(FINE_G) + COARSE.index(ch)
        if ch == LATE:
            return pl.ds(self.at.z, 1), NZ * len(FINE_G) + len(COARSE)
        return pl.ds(self.at.below(k), 1), NZ * FINE_G.index(ch) + k

    def p1_copies(self, ch, k, mine=True):
        at = self.at
        z, index = self.some(ch, k)
        x, y = (at.x, at.y) if mine else (at.ox, at.oy)
        over_x = self.g.at[ch, z, x, at.c, at.y]
        over_y = self.g.at[ch, z, at.x, at.c, y]
        return (
            remote(over_x, over_x, self.p1, (index, 0), at.to_x, (ch,)),
            remote(over_y, over_y, self.p1, (index, 1), at.to_y, (ch,)),
        )

    def p2_copies(self, ch, k, mine=True):
        at = self.at
        z, index = self.some(ch, k)
        head, tail = pl.ds(0, CUT), pl.ds(CUT, ROWS - CUT)
        if mine:
            over_x = self.g.at[ch, z, at.x, at.c, at.oy, head]
            over_y = self.g.at[ch, z, at.ox, at.c, at.y, tail]
        else:
            over_x = self.g.at[ch, z, at.ox, at.c, at.oy, head]
            over_y = self.g.at[ch, z, at.ox, at.c, at.oy, tail]
        return (
            remote(over_x, over_x, self.p2, (index, 0), at.to_x, (ch,)),
            remote(over_y, over_y, self.p2, (index, 1), at.to_y, (ch,)),
        )

    def c_copy(self, ch, mine=True):
        at = self.at
        ref = self.g.at[ch, :, :, at.c if mine else at.oc]
        return remote(ref, ref, self.cs, (ch,), at.to_c)

    def start_z(self, ch):
        for k in range(1, NZ):
            self.z_copy(ch, k).start()

    def start_own(self, ch):
        for copy in self.p1_copies(ch, 0):
            copy.start()

    def plane(self, ch, k):
        self.z_copy(ch, k, False).wait_recv()
        for copy in self.p1_copies(ch, k):
            copy.start()

    def plane_all(self, ch):
        for k in range(1, NZ):
            self.z_copy(ch, k, False).wait_recv()
        for copy in self.p1_copies(ch, 0):
            copy.start()

    def turn(self, ch, k=0):
        from_x, from_y = self.p1_copies(ch, k, False)
        over_x, over_y = self.p2_copies(ch, k)
        from_y.wait_recv()
        over_x.start()
        from_x.wait_recv()
        over_y.start()

    def cross(self, ch):
        for k in range(NZ) if ch in FINE_G else (0,):
            for copy in self.p2_copies(ch, k, False):
                copy.wait_recv()
        self.c_copy(ch).start()

    def arrive(self, ch):
        self.c_copy(ch, False).wait_recv()


    def late_copy(self, k, mine=True):
        at = self.at
        ref = self.g.at[LATE, at.z if mine else at.below(k), :, at.c]
        return remote(ref, ref, self.zs, (LATE, k - 1), at.to_z(k), (LATE,))

    def late_core(self, k, mine=True):
        at = self.at
        ref = self.g.at[LATE, at.below(k), :, at.c if mine else at.oc]
        return remote(ref, ref, self.cs, (LATE + k,), at.to_c)

    def late_z(self):
        for copy in self.p2_copies(LATE, 0, False):
            copy.wait_recv()
        for k in range(1, NZ):
            self.late_copy(k).start()
        self.late_core(0).start()

    def late_cross(self, k):
        self.late_copy(k, False).wait_recv()
        self.late_core(k).start()

    def late_arrive(self, k):
        self.late_core(k, False).wait_recv()

    def sent(self, ref, sem):
        pltpu.make_async_remote_copy(
            src_ref=ref, dst_ref=ref, send_sem=sem, recv_sem=sem, device_id=self.at.to_c,
            device_id_type=pl.DeviceIdType.MESH,
        ).wait_send()

    def drain(self, ch):
        self.sent(self.g.at[ch, 0:3, 0, 0, 0], self.zs[0].at[ch])
        self.sent(self.g.at[ch, :, :, 0, 0], self.p1[0].at[ch])
        self.sent(self.g.at[ch, :, 0, 0, 0], self.p2[0].at[ch])
        self.c_copy(ch).wait_send()

    def late_drain(self):
        self.sent(self.g.at[LATE, 0:3, :, 0], self.zs[0].at[LATE])
        self.sent(self.g.at[LATE, 0:1, :, 0, 0], self.p1[0].at[LATE])
        self.sent(self.g.at[LATE, 0:1, 0, 0, 0], self.p2[0].at[LATE])
        for k in range(NZ):
            self.late_core(k).wait_send()


def fold(wide):
    return jnp.concatenate([wide[:, :COLS], wide[:, COLS:]], axis=0)


def pack_weights(refs, put):
    q, k, v, o, inner, outer = refs
    units = [r[...].astype(F32) for r in (q, k, v, o)]
    wide = inner[...].astype(F32)
    units += [wide[:, WIDTH * i : WIDTH * (i + 1)] for i in range(4)]
    for ch in range(4):
        put(ch, jnp.concatenate([fold(units[2 * ch]), fold(units[2 * ch + 1])], axis=0).astype(BF))
    tall = outer[...]
    put(4, tall[:, :COLS])
    put(5, tall[:, COLS:])


def unpack_weights(g, ch, w):
    def one(pair):
        z, x, c = pair // (NX * NC), (pair // NC) % NX, pair % NC
        a = g[ch, z, x, c, 0].astype(F32)
        b = g[ch, z, x, c, 1].astype(F32)
        for unit in range(2):
            base = 48 * unit
            left = jnp.concatenate([a[base : base + 24], b[base : base + 24]], axis=0)
            right = jnp.concatenate([a[base + 24 : base + 48], b[base + 24 : base + 48]], axis=0)
            at = WIDTH * (2 * ch + unit)
            rows = pl.ds(pl.multiple_of(48 * pair, 48), 48)
            w[rows, at : at + COLS] = left.astype(BF)
            w[rows, at + COLS : at + WIDTH] = right.astype(BF)

    loop(GROUP, one)


def spread(gv, vec, ib):
    owners = GROUP * NY
    parts = gv[...].astype(F32).reshape(owners, 16, 128)
    across = lax.broadcasted_iota(jnp.int32, (128, WIDTH), 1)
    lane = lax.broadcasted_iota(jnp.int32, (128, WIDTH), 0)
    device = lax.broadcasted_iota(jnp.int32, (owners, 8, WIDTH), 0)
    col = lax.broadcasted_iota(jnp.int32, (owners, 8, WIDTH), 2)

    def placed(flat, size, start):
        pick = (rem(across + start, size) == lane).astype(F32).astype(BF)
        wide = jnp.dot(flat, pick, preferred_element_type=F32).reshape(owners, 8, WIDTH)
        first = device * size - start
        return jnp.sum(jnp.where((col >= first) & (col < first + size), wide, 0.0), axis=0)

    vec[...] = placed(parts[:, 0:8].reshape(owners * 8, 128).astype(BF), 24, 0)
    flat = parts[:, 8:16].reshape(owners * 8, 128).astype(BF)
    for i in range(4):
        total = placed(flat, 96, WIDTH * i)[0:1]
        ib[:, WIDTH * i : WIDTH * (i + 1)] = jnp.broadcast_to(total, (8, WIDTH))


class Scatter:
    def __init__(self, at, s, r1, rd0, rd1, rx, ry, rz, early, earlier, sent, cs, p2, p1, zs):
        self.at, self.s = at, s
        self.early, self.sent = early, sent
        self.erd0, self.erd1, self.erx, self.ery = earlier
        self.r1, self.rd0, self.rd1, self.rx, self.ry, self.rz = r1, rd0, rd1, rx, ry, rz
        self.cs, self.p2, self.p1, self.zs = cs, p2, p1, zs

    def c_copy(self, ch):
        at = self.at
        return remote(self.s.at[ch, :, :, at.oc], self.r1.at[ch], self.cs, (ch,), at.to_c)

    def some(self, ch, k):
        if k is None:
            return slice(None), ch
        return pl.ds(self.at.above(k), 1), FINE[0] + NZ * FINE.index(ch) + k

    def p2_copies(self, ch, k=None):
        at = self.at
        some, index = self.some(ch, k)
        head, tail = pl.ds(0, CUT), pl.ds(CUT, ROWS - CUT)
        corner = self.s.at[ch, some, at.ox, at.c, at.oy]
        return (
            remote(corner.at[:, head], self.rd0.at[ch - 1, some], self.p2, (index, 0), at.to_x, (ch,)),
            remote(corner.at[:, tail], self.rd1.at[ch - 1, some], self.p2, (index, 1), at.to_y, (ch,)),
        )

    def p1_copies(self, ch, k=None):
        at = self.at
        some, index = self.some(ch, k)
        return (
            remote(self.s.at[ch, some, at.ox, at.c, at.y], self.rx.at[ch - 1, some], self.p1, (index, 0), at.to_x, (ch,)),
            remote(self.s.at[ch, some, at.x, at.c, at.oy], self.ry.at[ch - 1, some], self.p1, (index, 1), at.to_y, (ch,)),
        )

    def z_copy(self, ch, k):
        at = self.at
        return remote(
            self.s.at[ch, at.above(k), at.x, at.c, at.y], self.rz.at[ch - 1, k - 1], self.zs, (ch, k - 1), at.to_z(k), (ch,)
        )

    def first_copies(self):
        at, s, r1 = self.at, self.s, self.r1
        pieces = (
            (s.at[1, :, at.ox, at.oc, at.oy], r1.at[1, :, at.ox, at.oy]),
            (s.at[1, :, at.ox, at.oc, at.y], r1.at[1, :, at.ox, at.y]),
            (s.at[1, :, at.x, at.oc], r1.at[1, :, at.x]),
        )
        return [remote(src, dst, self.cs, (index,), at.to_c) for (src, dst), index in zip(pieces, (1, CHUNKS, CHUNKS + 1))]

    def start(self, ch):
        for copy in self.first_copies() if ch == 1 else (self.c_copy(ch),):
            copy.start()

    def add_core(self, ch, x, y):
        def one(z):
            total = self.s[ch, z, x, self.at.c, y].astype(F32) + self.r1[ch, z, x, y].astype(F32)
            self.s[ch, z, x, self.at.c, y] = total.astype(BF)

        loop(NZ, one)

    def core(self, ch):
        at = self.at
        copies = self.first_copies() if ch == 1 else [self.c_copy(ch)]
        copies[0].wait_recv()
        self.add_core(ch, at.ox, at.oy)
        for k in (1, 2, 3, 0) if ch in FINE else (None,):
            for copy in self.p2_copies(ch, k):
                copy.start()
        for copy in copies[1:]:
            copy.wait_recv()
        self.add_core(ch, at.ox, at.y)
        self.add_core(ch, at.x, at.oy)
        self.add_core(ch, at.x, at.y)

    def over(self, k, work):
        if k is None:
            loop(NZ, work)
        else:
            work(self.at.above(k))

    def diagonal(self, ch, k=None):
        at = self.at
        over_x, over_y = self.p2_copies(ch, k)
        to_x, to_y = self.p1_copies(ch, k)
        head, tail = pl.ds(0, CUT), pl.ds(CUT, ROWS - CUT)
        over_x.wait_recv()

        def first(z):
            total = self.s[ch, z, at.x, at.c, at.oy, head].astype(F32) + self.rd0[ch - 1, z].astype(F32)
            self.s[ch, z, at.x, at.c, at.oy, head] = total.astype(BF)

        self.over(k, first)
        to_y.start()
        over_y.wait_recv()

        def second(z):
            total = self.s[ch, z, at.ox, at.c, at.y, tail].astype(F32) + self.rd1[ch - 1, z].astype(F32)
            self.s[ch, z, at.ox, at.c, at.y, tail] = total.astype(BF)

        self.over(k, second)
        to_x.start()

    def plane(self, ch, k=None):
        at = self.at
        for copy in self.p1_copies(ch, k):
            copy.wait_recv()

        def one(z):
            total = self.s[ch, z, at.x, at.c, at.y].astype(F32) + self.rx[ch - 1, z].astype(F32)
            total = total + self.ry[ch - 1, z].astype(F32)
            self.s[ch, z, at.x, at.c, at.y] = total.astype(BF)

        self.over(k, one)
        for j in range(1, NZ) if k is None else (k,) if k else ():
            self.z_copy(ch, j).start()

    def finish(self, ch):
        at = self.at
        for k in range(1, NZ):
            self.z_copy(ch, k).wait_recv()
        total = self.s[ch, at.z, at.x, at.c, at.y].astype(F32)
        for k in range(NZ - 1):
            total = total + self.rz[ch - 1, k].astype(F32)
        return total

    def drain(self, ch):
        for copy in self.first_copies() if ch == 1 else (self.c_copy(ch),):
            copy.wait_send()
        self.sent(self.s.at[ch, :, 0, 0, 0], self.p2[0].at[ch])
        self.sent(self.s.at[ch, :, :, 0, 0], self.p1[0].at[ch])
        self.sent(self.s.at[ch, 0:3, 0, 0, 0], self.zs[0].at[ch])


    def early_z(self):
        at = self.at
        return [
            remote(self.s.at[0, at.above(k), :, at.c], self.early.at[k - 1], self.zs, (0, k - 1), at.to_z(k), (0,))
            for k in range(1, NZ)
        ]

    def early_p2(self):
        at = self.at
        head, tail = pl.ds(0, CUT), pl.ds(CUT, ROWS - CUT)
        return (
            remote(self.s.at[0, at.z, at.ox, at.c, at.oy, head], self.erd0, self.p2, (0, 0), at.to_x, (0,)),
            remote(self.s.at[0, at.z, at.ox, at.c, at.oy, tail], self.erd1, self.p2, (0, 1), at.to_y, (0,)),
        )

    def early_p1(self):
        at = self.at
        return (
            remote(self.s.at[0, at.z, at.ox, at.c, at.y], self.erx, self.p1, (0, 0), at.to_x, (0,)),
            remote(self.s.at[0, at.z, at.x, at.c, at.oy], self.ery, self.p1, (0, 1), at.to_y, (0,)),
        )

    def early_core(self):
        at = self.at
        self.c_copy(0).wait_recv()

        def one(i):
            z, x, y = i // (NX * NY), rem(i // NY, NX), rem(i, NY)
            total = self.s[0, z, x, at.c, y].astype(F32) + self.r1[0, z, x, y].astype(F32)
            self.s[0, z, x, at.c, y] = total.astype(BF)

        loop(NZ * NX * NY, one)
        for copy in self.early_z():
            copy.start()

    def early_plane(self):
        at = self.at
        for copy in self.early_z():
            copy.wait_recv()

        def one(i):
            x, y = i // NY, rem(i, NY)
            total = self.s[0, at.z, x, at.c, y].astype(F32)
            for k in range(NZ - 1):
                total = total + self.early[k, x, y].astype(F32)
            self.s[0, at.z, x, at.c, y] = total.astype(BF)

        loop(NX * NY, one)
        for copy in self.early_p2():
            copy.start()

    def early_diagonal(self):
        at = self.at
        over_x, over_y = self.early_p2()
        to_x, to_y = self.early_p1()
        head, tail = pl.ds(0, CUT), pl.ds(CUT, ROWS - CUT)
        over_x.wait_recv()
        total = self.s[0, at.z, at.x, at.c, at.oy, head].astype(F32) + self.erd0[...].astype(F32)
        self.s[0, at.z, at.x, at.c, at.oy, head] = total.astype(BF)
        to_y.start()
        over_y.wait_recv()
        total = self.s[0, at.z, at.ox, at.c, at.y, tail].astype(F32) + self.erd1[...].astype(F32)
        self.s[0, at.z, at.ox, at.c, at.y, tail] = total.astype(BF)
        to_x.start()

    def early_finish(self):
        at = self.at
        for copy in self.early_p1():
            copy.wait_recv()
        total = self.s[0, at.z, at.x, at.c, at.y].astype(F32) + self.erx[...].astype(F32)
        return total + self.ery[...].astype(F32)

    def early_drain(self):
        self.c_copy(0).wait_send()
        self.sent(self.s.at[0, 0:1, 0, 0, 0], self.p2[0].at[0])
        self.sent(self.s.at[0, 0:1, :, 0, 0], self.p1[0].at[0])
        self.sent(self.s.at[0, 0:3, :, 0], self.zs[0].at[0])


def unfold(total, unit):
    base = 48 * unit
    return jnp.concatenate([total[base : base + 24], total[base + 24 : base + 48]], axis=1)


class VectorScatter:
    def __init__(self, at, s, rc, rx, ry, rz, sems):
        self.at, self.s = at, s
        self.rc, self.rx, self.ry, self.rz, self.sems = rc, rx, ry, rz, sems
        at = self.at
        self.cc = remote(s.at[:, :, at.oc], rc, sems, 0, at.to_c)
        self.xx = remote(s.at[:, at.ox, at.c], rx, sems, 1, at.to_x)
        self.yy = remote(s.at[:, at.x, at.c, at.oy], ry, sems, 2, at.to_y)
        self.zz = [
            remote(s.at[at.above(k), at.x, at.c, at.y], rz.at[k - 1], sems, 2 + k, at.to_z(k)) for k in range(1, NZ)
        ]

    def start(self):
        self.cc.start()

    def core(self):
        self.cc.wait_recv()
        self.s[:, :, self.at.c] = self.s[:, :, self.at.c] + self.rc[...]
        self.xx.start()

    def over_x(self):
        at = self.at
        self.xx.wait_recv()
        self.s[:, at.x, at.c] = self.s[:, at.x, at.c] + self.rx[...]
        self.yy.start()

    def over_y(self):
        at = self.at
        self.yy.wait_recv()
        self.s[:, at.x, at.c, at.y] = self.s[:, at.x, at.c, at.y] + self.ry[...]
        for copy in self.zz:
            copy.start()

    def finish(self):
        at = self.at
        for copy in self.zz:
            copy.wait_recv()
        return self.s[at.z, at.x, at.c, at.y] + self.rz[0] + self.rz[1] + self.rz[2]

    def drain(self):
        for copy in [self.cc, self.xx, self.yy] + self.zz:
            copy.wait_send()


def own_part(value, stride):
    if stride == 1:
        return value
    whole = lax.all_gather(value, ("dp", "blk"), axis=0, tiled=True)
    rows = whole.shape[0] // (GROUP * NY)
    index = (lax.axis_index("dp") // stride) * NY + lax.axis_index("blk")
    return lax.dynamic_slice_in_dim(whole, index * rows, rows, axis=0)


def fine_part(value, stride):
    if stride == 1:
        return value
    index = (lax.axis_index("dp") // stride) * NY + lax.axis_index("blk")
    rows = value.shape[0]
    whole = jnp.zeros((rows * GROUP * NY,) + value.shape[1:], value.dtype)
    whole = lax.dynamic_update_slice_in_dim(whole, value, index * rows, axis=0)
    return lax.psum_scatter(whole, ("dp", "blk"), scatter_dimension=0, tiled=True)


def product(left, right):
    return jnp.dot(left, right, preferred_element_type=F32)


def product_left(left, right):
    return lax.dot_general(left, right, (((0,), (0,)), ((), ())), preferred_element_type=F32)


def product_right(left, right):
    return lax.dot_general(left, right, (((1,), (1,)), ((), ())), preferred_element_type=F32)


def tile(i, size):
    return pl.ds(pl.multiple_of(i * size, size), size)


def mean(values):
    return jnp.mean(values, axis=-1, keepdims=True)


def column(values):
    return jnp.sum(values, axis=0, keepdims=True)


def gather_vectors(vg, ibg, sv):
    owners = GROUP * NY
    across = lax.broadcasted_iota(jnp.int32, (WIDTH, 128), 0)
    lane = lax.broadcasted_iota(jnp.int32, (WIDTH, 128), 1)

    def pieces(wide, size, start):
        pick = ((rem(across + start, size) == lane) & (lane < size)).astype(F32).astype(BF)
        high = wide.astype(BF)
        rest = (wide - high.astype(F32)).astype(BF)
        return product(high, pick) + product(rest, pick)

    def owned(shape, size, start):
        first = lax.broadcasted_iota(jnp.int32, shape, 0) * size - start
        col = lax.broadcasted_iota(jnp.int32, shape, len(shape) - 1)
        return (col >= first) & (col < first + size)

    wide = jnp.where(owned((owners, 8, WIDTH), 24, 0), vg[...][None], 0.0)
    total = pieces(wide.reshape(owners * 8, WIDTH), 24, 0)
    sv[:, :, :, :, 0:8] = total.reshape(NZ, NX, NC, NY, 8, 128)
    total = jnp.zeros((owners, 128), F32)
    for i in range(4):
        part = ibg[0:1, WIDTH * i : WIDTH * (i + 1)]
        wide = jnp.where(owned((owners, WIDTH), 96, WIDTH * i), part, 0.0)
        total = total + pieces(wide, 96, WIDTH * i)
    total = jnp.broadcast_to(total[:, None, :], (owners, 8, 128))
    sv[:, :, :, :, 8:16] = total.reshape(NZ, NX, NC, NY, 8, 128)


def play(schedule, steps, loops):
    at = 0
    while at < len(schedule):
        name, *numbers = schedule[at].split()
        numbers = [int(n) for n in numbers]
        if name not in loops:
            steps[name](*numbers)
            at += 1
            continue
        turns = [i for i, entry in enumerate(schedule) if entry.split()[0] == name]
        between = [schedule[i + 1 : j] for i, j in zip(turns, turns[1:])]

        def turn(i):
            loops[name](i)
            for index, entries in enumerate(between):
                if entries:
                    pl.when(i == index)(partial(play, entries, steps, {}))

        loop(len(turns), turn)
        at = turns[-1] + 1


QB, VB, OB, G1, S1, UB, G2, S2 = range(8)


def layer_kernel(
    stride,
    q, k, v, o, inner, outer, qb, vb, ob, g1, s1, ub, g2, s2, inner_bias, pad, hidden, grad, lengths,
    out, igrad, dq, dk, dv, do, di, du, dsmall, saved,
    g, gv, wd, u, page, cot, dead, mask, small, hid, qkv, outp, xt, hidt, ctxt, actt,
    n1, inv1, acc1, acc2, dst, bias, vec, ib, vg, ibg,
    sv, r1, rd0, rd1, rx, ry, rz, early, erd0, erd1, erx, ery, vc, vx, vy, vz,
    zs, zr, p1s, p1r, p2s, p2r, cs, cr, vs, vr, es, er,
    csr, q2r, q1r, zsr, wr, loads, saves, stores,
):
    at = Place(stride)
    gather = Gather(at, g, (zs, zr), (p1s, p1r), (p2s, p2r), (cs, cr))
    scatter = Scatter(
        at, g, r1, rd0, rd1, rx, ry, rz, early, (erd0, erd1, erx, ery), gather.sent, (cs, csr), (p2s, q2r), (p1s, q1r), (zs, zsr)
    )
    vector = VectorScatter(at, sv, vc, vx, vy, vz, (vs, wr))

    def put(ch, value):
        g[ch, at.z, at.x, at.c, at.y] = value

    at.hail()
    pack_weights((q, k, v, o, inner, outer), put)
    small[...] = jnp.zeros_like(small)
    for i, ref in enumerate((qb, vb, ob, g1, s1, ub, g2, s2, inner_bias)):
        small[i : i + 1, 0 : ref.shape[-1]] = ref[...].astype(F32).reshape(1, ref.shape[-1])
    gv[at.z, at.x, at.c, at.y] = small[...].astype(BF)
    position = lax.broadcasted_iota(jnp.int32, (8, 256), 1) + at.y * 256
    for i in range(2):
        live = (position < lengths[i]) & (jnp.broadcast_to(pad[i : i + 1], (8, 256)) == 1)
        mask[i] = jnp.where(live, 0.0, NEG_FILL)
    own = pl.ds(pl.multiple_of(at.y * 256, 256), 256)
    theirs = pl.ds(pl.multiple_of(at.oy * 256, 256), 256)
    local = [
        pltpu.make_async_copy(hidden.at[at.y], page.at[own], loads.at[0]),
        pltpu.make_async_copy(grad.at[at.y], cot.at[own], loads.at[1]),
    ]
    for copy in local:
        copy.start()
    at.meet()

    ve, ee = (vs, vr), (es, er)
    page_in = remote(hidden.at[at.oy], page.at[own], ee, 0, at.to_y)
    mask_in = remote(mask.at[at.oy], dead.at[at.y], ee, 1, at.to_y)
    grad_in = remote(grad.at[at.oy], cot.at[own], ee, 2, at.to_y)
    out_over = remote(outp.at[theirs], out.at[at.y], ee, 3, at.to_y)
    grad_over = remote(cot.at[theirs], igrad.at[at.y], ee, 4, at.to_y)
    swaps = [page_in, mask_in, grad_in, out_over, grad_over]
    mine = gv.at[at.z, at.x, at.c, at.y]
    line = gv.at[:, at.x, at.c, at.y]
    pairs = gv.at[:, :, at.c, at.y]
    core = gv.at[:, :, at.c]
    vzs = [remote(mine, mine, ve, kk - 1, at.to_z(kk)) for kk in range(1, NZ)]
    vxs = remote(line, line, ve, 3, at.to_x)
    vys = remote(pairs, pairs, ve, 4, at.to_y)
    vcs = remote(core, core, ve, 5, at.to_c)

    def vector_z():
        for copy in vzs:
            copy.start()

    def vector_x():
        for copy in vzs:
            copy.wait_recv()
        vxs.start()

    def vector_y():
        vxs.wait_recv()
        vys.start()

    def vector_c():
        vys.wait_recv()
        vcs.start()

    def page_start():
        page_in.start()
        mask_in.start()

    def page_wait():
        for copy in local:
            copy.wait()
        page_in.wait_recv()
        mask_in.wait_recv()

    def turn(i):
        xt[tile(i, 256), :] = page[:, tile(i, 256)].T

    def prepare():
        dead[at.y] = mask[at.y]
        loop(3, turn)
        for half in range(2):
            bias[256 * half : 256 * half + 256] = jnp.broadcast_to(dead[half, 0:1].T, (256, 128))
        spread(gv, vec, ib)

    def queries(i):
        cols = tile(i, 256)
        value = product(page[...], wd[:, cols]) + vec[QB : QB + 1, cols]
        qkv[:, cols] = (value.astype(BF).astype(F32) * 0.125).astype(BF)

    def keys(i):
        cols = tile(i + 3, 256)
        qkv[:, cols] = product(page[...], wd[:, cols]).astype(BF)

    def vals(i):
        cols = tile(i + 6, 256)
        value = product(page[...], wd[:, cols]) + vec[VB : VB + 1, tile(i, 256)]
        qkv[:, cols] = value.astype(BF)

    def queries_keys():
        loop(3, queries)
        loop(3, keys)

    lane = lax.broadcasted_iota(jnp.int32, (512, 128), 1)
    sides = (lane < 64, lane >= 64)

    def side(value, which):
        return jnp.where(sides[which], value.astype(F32), 0.0).astype(BF)

    def save(pair):
        cols = tile(pair, 1024)
        return pltpu.make_async_copy(u.at[:, cols], saved.at[:, cols], saves.at[pair])

    def attend(pair):
        at_q, at_k, at_v = tile(pair, 128), tile(pair + 6, 128), tile(pair + 12, 128)
        k2, v2 = qkv[:, at_k], qkv[:, at_v]
        total = jnp.zeros((128, 512), F32)
        for a in range(2):
            ka, va = side(k2, a), side(v2, a)
            for h in range(2):
                q2 = qkv[256 * h : 256 * h + 256, at_q]
                s = product_right(ka, q2) + jnp.concatenate([bias[...], bias[...]], axis=1)
                e = jnp.exp(s - jnp.max(s, axis=0, keepdims=True))
                p = e * (1.0 / jnp.sum(e, axis=0, keepdims=True))
                cols = pl.ds(pl.multiple_of(1024 * pair + 512 * a + 256 * h, 256), 256)
                u[:, cols] = p.astype(BF)
            cols = pl.ds(pl.multiple_of(1024 * pair + 512 * a, 512), 512)
            total = total + product_left(va, u[:, cols])
        ctxt[tile(pair, 128), :] = total.astype(BF)
        outp[:, tile(pair, 128)] = total.T.astype(BF)
        save(pair).start()

    def attended(i):
        cols = tile(i, 256)
        value = product(outp[...], wd[:, tile(i + 9, 256)]) + vec[OB : OB + 1, cols]
        acc1[:, cols] = page[:, cols].astype(F32) + value

    def first_norm(i):
        rows = tile(i, 64)
        joined = acc1[rows, :]
        center = joined - mean(joined)
        inverse = lax.rsqrt(mean(center * center) + EPSILON)
        normed = center * inverse
        n1[rows, :] = normed
        inv1[rows, :] = jnp.broadcast_to(inverse, (64, 128))
        hid[rows, :] = (normed * vec[G1 : G1 + 1] + vec[S1 : S1 + 1]).astype(BF)

    def turn_hidden(i):
        hidt[tile(i, 256), :] = hid[:, tile(i, 256)].T

    def after_attention():
        loop(3, attended)
        loop(8, first_norm)
        loop(3, turn_hidden)
        loop(6, lambda i: save(i).wait())

    def feed(i):
        cols = tile(i, 384)
        weight = wd[:, pl.ds(pl.multiple_of(4 * WIDTH + 384 * i, 384), 384)]
        acc1[:, 0:384] = product(hid[...], weight) + ib[0:1, cols]

        def one(r):
            rows = tile(r, 64)
            value = acc1[rows, 0:384]
            cdf = 0.5 + 0.5 * lax.erf(value * 0.7071067811865476)
            density = 0.3989422804014327 * jnp.exp(-0.5 * value * value)
            u[rows, cols] = (value * cdf).astype(BF)
            u[rows, pl.ds(pl.multiple_of(3072 + 384 * i, 384), 384)] = (cdf + value * density).astype(BF)

        loop(8, one)
        actt[cols, :] = u[:, cols].T

    def outer_left():
        acc1[:, 0:COLS] = product(u[:, 0:3072], g[4].reshape(8 * COLS, COLS))

    def outer_right(step):
        z = at.below(step)
        value = product(u[:, tile(z, 768)], g[LATE, z].reshape(2 * COLS, COLS))
        acc1[:, COLS:] = value if step == 0 else acc1[:, COLS:] + value

    def cotangent():
        vg[...] = jnp.zeros_like(vg)

        def one(i):
            rows = tile(i, 64)
            dy = cot[rows, :].astype(F32)
            vg[S2 : S2 + 1] += column(dy)
            bias[rows, :] = jnp.broadcast_to(mean(dy * vec[G2 : G2 + 1]), (64, 128))

        loop(8, one)

    def second_norm(i):
        gain = vec[G2 : G2 + 1]
        sums = [jnp.zeros((1, WIDTH), F32)] * 2
        for part in range(2):
            rows = tile(2 * i + part, 64)
            second = hid[rows, :].astype(F32) + (acc1[rows, :] + vec[UB : UB + 1])
            center = second - mean(second)
            inverse = lax.rsqrt(mean(center * center) + EPSILON)
            normed = center * inverse
            outp[rows, :] = (normed * gain + vec[S2 : S2 + 1]).astype(BF)
            dy = cot[rows, :].astype(F32)
            product_normed = dy * normed
            back = inverse * (dy * gain - bias[rows, 0:1] - normed * mean(product_normed * gain))
            acc2[rows, :] = back
            low = back.astype(BF)
            page[rows, :] = low
            sums = [sums[0] + column(product_normed), sums[1] + column(low.astype(F32))]
        vg[G2 : G2 + 1] += sums[0]
        vg[UB : UB + 1] += sums[1]

    play(
        FORWARD,
        {
            "z": gather.start_z,
            "own": gather.start_own,
            "plane": gather.plane,
            "turn": gather.turn,
            "cross": gather.cross,
            "arrive": gather.arrive,
            "late_z": gather.late_z,
            "late_cross": gather.late_cross,
            "late_arrive": gather.late_arrive,
            "plane_all": gather.plane_all,
            "cotangent": cotangent,
            "vector_z": vector_z,
            "vector_x": vector_x,
            "vector_y": vector_y,
            "vector_c": vector_c,
            "vector_wait": vcs.wait_recv,
            "page": page_start,
            "page_wait": page_wait,
            "grad": grad_in.start,
            "grad_wait": grad_in.wait_recv,
            "prepare": prepare,
            "unpack": lambda ch: unpack_weights(g, ch, wd),
            "queries_keys": queries_keys,
            "values": lambda: loop(3, vals),
            "after_attention": after_attention,
            "outer_left": outer_left,
            "outer_right": outer_right,
        },
        {"attend": attend, "feed": feed, "feed_on": lambda i: feed(i + 4)},
    )
    loop(4, second_norm)

    low = page
    keep = pltpu.make_async_copy(outp.at[own], out.at[at.y], loads.at[0])
    for ch in range(LATE):
        gather.drain(ch)
    gather.late_drain()

    for copy in vzs + [vxs, vys, vcs]:
        copy.wait_send()

    def out_start():
        out_over.start()
        keep.start()

    def outer_grad(half, slot):
        def one(i):
            cols = slice(COLS * half, COLS * half + COLS)
            value = product(actt[tile(i, 1536), :], low[:, cols]).astype(BF)
            g[slot, pl.ds(2 * i, 2)] = value.reshape(2, NX, NC, NY, ROWS, COLS)

        loop(2, one)

    def load(part):
        cols = pl.ds(3072 * part, 3072)
        return pltpu.make_async_copy(saved.at[:, cols], u.at[:, cols], loads.at[1])

    def inner_back(i):
        weight = [g[4 + half, i].reshape(2 * COLS, COLS) for half in range(2)]
        value = product_right(low[...], jnp.concatenate(weight, axis=1))
        cols = pl.ds(pl.multiple_of(3072 + 768 * i, 768), 768)
        value = (value * u[:, cols].astype(F32)).astype(BF)
        u[:, cols] = value
        total = column(value.astype(F32))
        ibg[:, tile(i, 768)] = jnp.broadcast_to(total, (8, 768))

    def weight_grad(slot, unit, left, right):
        def one(i):
            value = product(left[tile(i, 384), :], right)
            value = value.reshape(16, 24, WIDTH)
            value = jnp.concatenate([value[:, :, :COLS], value[:, :, COLS:]], axis=1).astype(BF)
            g[slot, pl.ds(2 * i, 2), :, :, :, 48 * unit : 48 * unit + 48, :] = value.reshape(
                2, NX, NC, NY, 48, COLS
            )

        loop(2, one)

    def inner_grad(unit):
        right = u[:, 3072 + WIDTH * unit : 3072 + WIDTH * (unit + 1)]
        weight_grad(2 + unit // 2, unit % 2, hidt, right)

    def hidden_back(i):
        cols = tile(i, 256)
        acc2[:, cols] = acc2[:, cols] + product_right(u[:, 3072:6144], wd[cols, 4 * WIDTH :])

    def first_back(i):
        rows = tile(i, 64)
        up = acc2[rows, :]
        normed = n1[rows, :]
        vg[G1 : G1 + 1] += column(up * normed)
        vg[S1 : S1 + 1] += column(up)
        scaled = up * vec[G1 : G1 + 1]
        inverse = inv1[rows, 0:1]
        back = inverse * (scaled - mean(scaled) - normed * mean(scaled * normed))
        acc2[rows, :] = back
        short = back.astype(BF)
        low[rows, :] = short
        vg[OB : OB + 1] += column(short.astype(F32))

    def context_back(i):
        cols = tile(i, 256)
        hid[:, cols] = product_right(low[...], wd[cols, 3 * WIDTH : 4 * WIDTH]).astype(BF)

    def attend_back(pair):
        at_q, at_k, at_v = tile(pair, 128), tile(pair + 6, 128), tile(pair + 12, 128)
        q2, k2, v2, c2 = qkv[:, at_q], qkv[:, at_k], qkv[:, at_v], hid[:, at_q]
        dqt = jnp.zeros((128, 512), F32)
        dk2 = jnp.zeros((512, 128), F32)
        dv2 = jnp.zeros((512, 128), F32)
        for a in range(2):
            va = side(v2, a)
            for h in range(2):
                cols = pl.ds(pl.multiple_of(1024 * pair + 512 * a + 256 * h, 256), 256)
                p = u[:, cols].astype(F32)
                d = product_right(va, c2[256 * h : 256 * h + 256])
                delta = jnp.sum(p * d, axis=0, keepdims=True)
                dst[:, 256 * h : 256 * h + 256] = (p * (d - delta)).astype(BF)
            cols = pl.ds(pl.multiple_of(1024 * pair + 512 * a, 512), 512)
            dv2 = dv2 + product(u[:, cols], side(c2, a))
            dk2 = dk2 + product(dst[...], side(q2, a))
            dqt = dqt + product_left(side(k2, a), dst[...])
        qkv[:, at_q] = (dqt.T * 0.125).astype(BF)
        qkv[:, at_k] = dk2.astype(BF)
        qkv[:, at_v] = dv2.astype(BF)

    def sums(i):
        rows = tile(i, 64)
        vg[QB : QB + 1] += column(qkv[rows, 0:WIDTH].astype(F32))
        vg[VB : VB + 1] += column(qkv[rows, 2 * WIDTH : 3 * WIDTH].astype(F32))

    def input_back(i):
        cols = tile(i, 256)
        value = acc2[:, cols] + product_right(qkv[...], wd[cols, 0 : 3 * WIDTH])
        cot[:, cols] = value.astype(BF)

    keep_in = pltpu.make_async_copy(cot.at[own], igrad.at[at.y], loads.at[1])

    def grad_start():
        grad_over.start()
        keep_in.start()

    def result(index):
        if index < 2:
            rows, cols = pl.ds(0, ROWS), pl.ds(COLS * (1 - index), COLS)
            target = du.at[:, cols]
        else:
            rows, cols = pl.ds(ROWS + 24 * (index - 2), 24), pl.ds(0, WIDTH)
            target = di.at[:, pl.ds(WIDTH * (index - 2), WIDTH)] if index < 6 else (dv, do, dq, dk)[index - 6]
        place = acc1.at[rows, cols]
        return place, pltpu.make_async_copy(place, target, stores.at[index])

    def store(index, value):
        place, copy = result(index)
        place[...] = value
        copy.start()

    def finish(n):
        total = scatter.finish(n) if n else scatter.early_finish()
        if n < 2:
            store(n, total)
        else:
            store(2 * n - 2, unfold(total, 0))
            store(2 * n - 1, unfold(total, 1))

    def vector_finish():
        dsmall[...] = vector.finish()

    def context_grad():
        load(1).start()
        loop(3, context_back)
        load(1).wait()

    def outer_second():
        outer_grad(1, 0)
        load(0).start()

    def output_grad():
        weight_grad(4, 1, ctxt, low[...])

    def first_grad():
        loop(8, first_back)
        load(0).wait()

    play(
        BACKWARD,
        {
            "start": scatter.start,
            "core": scatter.core,
            "diagonal": scatter.diagonal,
            "plane": scatter.plane,
            "finish": finish,
            "early_core": scatter.early_core,
            "early_plane": scatter.early_plane,
            "early_diagonal": scatter.early_diagonal,
            "vector": vector.start,
            "vector_core": vector.core,
            "vector_x": vector.over_x,
            "vector_y": vector.over_y,
            "vector_finish": vector_finish,
            "out": out_start,
            "grad": grad_start,
            "outer_first": lambda: outer_grad(0, 1),
            "outer_second": outer_second,
            "inner_grad": inner_grad,
            "first_back": first_grad,
            "output_grad": output_grad,
            "context_back": context_grad,
            "value_grad": lambda: weight_grad(4, 0, xt, qkv[:, 2 * WIDTH : 3 * WIDTH]),
            "query_grad": lambda: weight_grad(5, 0, xt, qkv[:, 0:WIDTH]),
            "key_grad": lambda: weight_grad(5, 1, xt, qkv[:, WIDTH : 2 * WIDTH]),
            "sums": lambda: loop(8, sums),
            "gather_vectors": lambda: gather_vectors(vg, ibg, sv),
        },
        {
            "inner_back": inner_back,
            "hidden_back": hidden_back,
            "attend_back": attend_back,
            "input_back": input_back,
        },
    )
    keep.wait()
    keep_in.wait()
    for index in range(10):
        result(index)[1].wait()
    out_over.wait_recv()
    grad_over.wait_recv()
    for n in range(1, CHUNKS):
        scatter.drain(n)
    scatter.early_drain()
    vector.drain()
    for copy in swaps:
        copy.wait_send()


def layer_call(stride, args):
    vmem = pl.BlockSpec(memory_space=pltpu.VMEM)
    hbm = pl.BlockSpec(memory_space=pl.ANY)
    dma = pltpu.SemaphoreType.DMA

    def shape(*dims, kind=F32):
        return jax.ShapeDtypeStruct(dims, kind)

    tokens = [shape(2, 256, WIDTH, kind=BF)] * 2
    grads = [shape(24, WIDTH)] * 4 + [shape(24, 4 * WIDTH), shape(96, WIDTH), shape(16, 128)]

    def low(*dims):
        return pltpu.VMEM(dims, BF)

    def full(*dims):
        return pltpu.VMEM(dims, F32)

    def pair(*dims):
        return [dma(dims), dma(dims)]

    return pl.pallas_call(
        partial(layer_kernel, stride),
        out_shape=tuple(tokens + grads + [shape(512, 12 * 512, kind=BF)]),
        in_specs=[vmem] * 16 + [hbm, hbm, pl.BlockSpec(memory_space=pltpu.SMEM)],
        out_specs=tuple([hbm] * 8 + [vmem, hbm]),
        scratch_shapes=[
            low(CHUNKS, NZ, NX, NC, NY, ROWS, COLS),
            low(NZ, NX, NC, NY, 16, 128),
            low(WIDTH, 8 * WIDTH),
            low(512, 12 * 512),
            low(512, WIDTH),
            low(512, WIDTH),
            full(2, 8, 256),
            full(2, 8, 256),
            full(16, 128),
            low(512, WIDTH),
            low(512, 3 * WIDTH),
            low(512, WIDTH),
            low(WIDTH, 512),
            low(WIDTH, 512),
            low(WIDTH, 512),
            low(4 * WIDTH, 512),
            full(512, WIDTH),
            full(512, 128),
            full(512, WIDTH),
            full(512, WIDTH),
            low(512, 512),
            full(512, 128),
            full(8, WIDTH),
            full(8, 4 * WIDTH),
            full(8, WIDTH),
            full(8, 4 * WIDTH),
            full(NZ, NX, NC, NY, 16, 128),
            low(CHUNKS, NZ, NX, NY, ROWS, COLS),
            low(CHUNKS - 1, NZ, CUT, COLS),
            low(CHUNKS - 1, NZ, ROWS - CUT, COLS),
            low(CHUNKS - 1, NZ, ROWS, COLS),
            low(CHUNKS - 1, NZ, ROWS, COLS),
            low(CHUNKS - 1, NZ - 1, ROWS, COLS),
            low(NZ - 1, NX, NY, ROWS, COLS),
            low(CUT, COLS),
            low(ROWS - CUT, COLS),
            low(ROWS, COLS),
            low(ROWS, COLS),
            full(NZ, NX, NY, 16, 128),
            full(NZ, NY, 16, 128),
            full(NZ, 16, 128),
            full(NZ - 1, 16, 128),
            dma((CHUNKS,)), dma((CHUNKS, NZ - 1)),
            dma((CHUNKS,)), dma((G_STEPS, 2)),
            dma((CHUNKS,)), dma((G_STEPS, 2)),
            *pair(LATE + NZ),
            *pair(6),
            *pair(5),
            dma((CHUNKS + 2,)),
            dma((S_STEPS, 2)),
            dma((S_STEPS, 2)),
            dma((CHUNKS, NZ - 1)),
            dma((6,)),
            dma((2,)),
            dma((6,)),
            dma((10,)),
        ],
        compiler_params=pltpu.CompilerParams(
            collective_id=0, has_side_effects=True, vmem_limit_bytes=VMEM_LIMIT
        ),
        name="layer",
    )(*args)


def hand_out_kernel(*refs):
    large, small, outs, vectors = refs[:8], refs[8], refs[9:17], refs[17:26]
    held, into, back = refs[26:34], refs[34], refs[35]
    loads = [pltpu.make_async_copy(a, b, into.at[i]) for i, (a, b) in enumerate(zip(large, held))]
    stores = [pltpu.make_async_copy(a, b, back.at[i]) for i, (a, b) in enumerate(zip(held, outs))]
    for copy in loads:
        copy.start()
    for i, ref in enumerate(vectors):
        ref[...] = small[i, : ref.shape[0]]
    for load, store in zip(loads, stores):
        load.wait()
        store.start()
    for store in stores:
        store.wait()


def hand_out(large, small):
    vmem = pl.BlockSpec(memory_space=pltpu.VMEM)
    hbm = pl.BlockSpec(memory_space=pl.ANY)
    vectors = [jax.ShapeDtypeStruct((24,), F32)] * 8 + [jax.ShapeDtypeStruct((96,), F32)]
    return pl.pallas_call(
        hand_out_kernel,
        out_shape=tuple([jax.ShapeDtypeStruct(v.shape, v.dtype) for v in large] + vectors),
        in_specs=[hbm] * 8 + [vmem],
        out_specs=tuple([hbm] * 8 + [vmem] * 9),
        scratch_shapes=[pltpu.VMEM(v.shape, v.dtype) for v in large]
        + [pltpu.SemaphoreType.DMA((8,)), pltpu.SemaphoreType.DMA((8,))],
        name="hand_out",
    )(*large, small)


def body(
    stride,
    hidden_in,
    page_lengths,
    pad_mask,
    query_weight,
    query_bias,
    key_weight,
    value_weight,
    value_bias,
    output_weight,
    output_bias,
    first_gain,
    first_shift,
    inner_weight,
    inner_bias,
    outer_weight,
    outer_bias,
    second_gain,
    second_shift,
    out_grad,
):
    coarse = partial(own_part, stride=stride)
    fine = partial(fine_part, stride=stride)
    weights = (query_weight, key_weight, value_weight, output_weight, inner_weight, outer_weight)
    vectors = (
        query_bias, value_bias, output_bias, first_gain, first_shift, outer_bias, second_gain, second_shift, inner_bias,
    )
    parts = [coarse(v) for v in weights + vectors]
    *large, dsmall, _ = layer_call(stride, (*parts, pad_mask, hidden_in, out_grad, page_lengths))
    output, input_grad, *grads = hand_out(large, dsmall)
    dq, dk, dv, do, di, du, qbg, vbg, obg, g1g, s1g, ubg, g2g, s2g, ibg = [fine(v) for v in grads]
    return (
        output, input_grad, dq, qbg, dk, dv, vbg, do, obg, g1g, s1g, di, ibg, du, ubg, g2g, s2g,
    )


def solution(mesh):
    stride = mesh.shape["dp"] // GROUP
    row = P(("dp", "blk"))
    mat = P(("dp", "blk"), None)
    tok = P("dp", "blk", None)
    in_specs = (
        tok, P("dp"), P("dp", "blk"), mat, row, mat, mat, row, mat, row, row, row, mat, row, mat, row, row, row, tok,
    )
    out_specs = (
        tok, tok, mat, row, mat, mat, row, mat, row, row, row, mat, row, mat, row, row, row,
    )
    return jax.shard_map(
        partial(body, stride), mesh=mesh, in_specs=in_specs, out_specs=out_specs, check_vma=False
    )
```

```python
from functools import partial

import jax
import jax.numpy as jnp
from jax import lax
from jax.experimental import pallas as pl
from jax.experimental.pallas import tpu as pltpu
from jax.sharding import PartitionSpec as P

HEADS = 12
NEG_FILL = -1000000000.0
EPSILON = 1e-05

NZ, NX, NC, NY = 4, 2, 2, 2
GROUP = NZ * NX * NC
CHUNKS = 6
ROWS, COLS = 96, 384
LATE = 5
FINE_G, COARSE = (0, 1), (2, 3, 4)
G_STEPS = NZ * len(FINE_G) + len(COARSE) + 1
G_ALONG = len(COARSE) + (NZ - 1) * (len(FINE_G) + 1)
WIDTH = 768
CUTS_G = (64, 80, 48, 48, 64, 80)
CUTS_S = (32, 48, 32, 48, 48, 80)
FINE = (4, 5)
S_STEPS = FINE[0] + NZ * len(FINE)
BF, F32 = jnp.bfloat16, jnp.float32
VMEM_LIMIT = 63 * 2**20

FORWARD = (
    "own 5", "own 1", "vector_z", "z 0", "z 1", "turn 5 0", "own 0", "page", "turn 1 0", "plane 0 1",
    "vector_x", "z 2", "plane 0 3", "plane 0 2", "plane 1 1", "plane 1 2", "turn 0 1", "turn 0 0", "z 3",
    "plane 1 3", "turn 1 1", "page_wait", "turn 0 3", "vector_y", "turn 1 2", "turn 0 2", "turn 1 3", "z 4",
    "plane_all 2", "vector_c", "cross 0", "vector_wait", "cross 1", "prepare", "arrive 0", "late_z", "arrive 1",
    "plane_all 3", "unpack 0", "queries_keys", "turn 2", "unpack 1", "values", "attend 0", "attend 1",
    "attend 2", "plane_all 4", "attend 3", "attend 4", "turn 3", "cross 2", "attend 5", "after_attention",
    "arrive 2", "unpack 2", "feed 0", "turn 4", "grad", "feed 1", "late_arrive 0", "cross 3", "feed 2",
    "feed 3", "arrive 3", "unpack 3", "feed_on 4", "late_cross 1", "cross 4", "late_cross 2", "late_cross 3",
    "feed_on 5", "feed_on 6", "feed_on 7", "arrive 4", "outer_left", "outer_right 0", "late_arrive 1",
    "late_arrive 3", "outer_right 1", "late_arrive 2", "outer_right 2", "grad_wait", "cotangent",
    "outer_right 3",
)
BACKWARD = (
    "out", "outer_second 2", "outer_second 1", "outer_first 0", "early_start 2", "start_first 0",
    "outer_first 1", "inner_back 0", "outer_second 3", "early_start 1", "outer_first 2", "outer_first 3",
    "early_core 2", "core_first", "start_first 2", "inner_back 1", "start_first 1", "outer_second 0",
    "inner_back 2", "inner_back 3", "core_rest", "early_start 3", "inner_grad 0", "early_start 0",
    "early_core 1", "diagonal 1", "inner_grad 1", "early_core 0", "early_core 3", "start 2", "inner_grad 2",
    "inner_grad 3", "hidden_back 0", "start 3", "core 2", "hidden_back 1", "hidden_back 2", "first_back",
    "core 3", "diagonal 2", "context_back", "attend_back 0", "attend_back 1", "attend_back 2", "plane 1",
    "output_grad", "early_plane", "diagonal 3", "attend_back 3", "attend_back 4", "attend_back 5", "value_grad",
    "start 4", "early_diagonal", "key_grad", "query_grad", "sums", "plane 3", "start 5", "core 4",
    "gather_vectors", "diagonal 4 1", "vector", "plane 2", "finish 1", "diagonal 4 2", "core 5", "input_back 0",
    "diagonal 4 3", "plane 4 2", "vector_core", "input_back 1", "plane 4 1", "diagonal 5 1", "diagonal 5 2",
    "diagonal 5 3", "diagonal 4 0", "finish 3", "diagonal 5 0", "input_back 2", "plane 4 3", "finish 0",
    "vector_x", "grad", "plane 5 1", "plane 5 2", "finish 2", "plane 5 3", "plane 5 0", "vector_y", "plane 4 0",
    "finish 4", "finish 5", "vector_finish",
)


def rem(a, b):
    return lax.rem(a, b)


class Place:
    def __init__(self, stride):
        dp = lax.axis_index("dp")
        self.y = lax.axis_index("blk")
        index = dp // stride
        self.low = dp - index * stride
        self.stride = stride
        self.z = index // (NX * NC)
        self.x = (index // NC) % NX
        self.c = index % NC
        self.ox, self.oy, self.oc = 1 - self.x, 1 - self.y, 1 - self.c

    def dev(self, z, x, c, y):
        return ((z * (NX * NC) + x * NC + c) * self.stride + self.low, y)

    def above(self, k):
        return rem(self.z + k, NZ)

    def below(self, k):
        return rem(self.z + NZ - k, NZ)

    def to_z(self, k):
        return self.dev(self.above(k), self.x, self.c, self.y)

    @property
    def to_x(self):
        return self.dev(self.z, self.ox, self.c, self.y)

    @property
    def to_y(self):
        return self.dev(self.z, self.x, self.c, self.oy)

    @property
    def to_c(self):
        return self.dev(self.z, self.x, self.oc, self.y)

    def hail(self):
        partners = [self.to_z(k) for k in range(1, NZ)] + [self.to_x, self.to_y, self.to_c]
        for who in partners:
            pl.semaphore_signal(
                pltpu.get_barrier_semaphore(), inc=1, device_id=who, device_id_type=pl.DeviceIdType.MESH
            )

    def meet(self):
        pl.semaphore_wait(pltpu.get_barrier_semaphore(), NZ + 2)


def remote(src, dst, sems, index, who, group=None):
    send, recv = sems
    return pltpu.make_async_remote_copy(
        src_ref=src,
        dst_ref=dst,
        send_sem=send.at[index if group is None else group],
        recv_sem=recv.at[index],
        device_id=who,
        device_id_type=pl.DeviceIdType.MESH,
    )


def loop(count, body):
    def step(i, carry):
        body(i)
        return carry

    lax.fori_loop(0, count, step, 0)


def cut(rows):
    return pl.ds(0, rows), pl.ds(rows, ROWS - rows)


class Gather:
    def __init__(self, at, blocks, zs, p1, p2, cs):
        self.at, self.g = at, blocks
        self.zs, self.p1, self.p2, self.cs = zs, p1, p2, cs

    def z_copy(self, ch, k, mine=True):
        at = self.at
        z = at.z if mine else at.below(k)
        ref = self.g.at[ch, z, at.x, at.c, at.y]
        return remote(ref, ref, self.zs, self.along(ch, k), at.to_z(k), (ch,))

    def along(self, ch, k):
        if ch in COARSE:
            return (ch - COARSE[0],)
        return (len(COARSE) + (NZ - 1) * (FINE_G + (LATE,)).index(ch) + k - 1,)

    def some(self, ch, k):
        if ch in COARSE:
            return slice(None), NZ * len(FINE_G) + COARSE.index(ch)
        if ch == LATE:
            return pl.ds(self.at.z, 1), NZ * len(FINE_G) + len(COARSE)
        return pl.ds(self.at.below(k), 1), NZ * FINE_G.index(ch) + k

    def p1_copies(self, ch, k, mine=True):
        at = self.at
        z, index = self.some(ch, k)
        x, y = (at.x, at.y) if mine else (at.ox, at.oy)
        over_x = self.g.at[ch, z, x, at.c, at.y]
        over_y = self.g.at[ch, z, at.x, at.c, y]
        return (
            remote(over_x, over_x, self.p1, (index, 0), at.to_x, (ch,)),
            remote(over_y, over_y, self.p1, (index, 1), at.to_y, (ch,)),
        )

    def p2_copies(self, ch, k):
        at = self.at
        z, _ = self.some(ch, k)
        head, tail = cut(CUTS_G[ch])
        over_x = self.g.at[ch, z, at.x, at.c, at.oy, head]
        over_y = self.g.at[ch, z, at.ox, at.c, at.y, tail]
        return (
            remote(over_x, over_x, self.p2, (ch,), at.to_x),
            remote(over_y, over_y, self.p2, (ch,), at.to_y),
        )

    def c_copy(self, ch, mine=True):
        at = self.at
        ref = self.g.at[ch, :, :, at.c if mine else at.oc]
        return remote(ref, ref, self.cs, (ch,), at.to_c)

    def start_z(self, ch):
        for k in range(1, NZ):
            self.z_copy(ch, k).start()

    def start_own(self, ch):
        for copy in self.p1_copies(ch, 0):
            copy.start()

    def plane(self, ch, k):
        self.z_copy(ch, k, False).wait_recv()
        for copy in self.p1_copies(ch, k):
            copy.start()

    def plane_all(self, ch):
        self.got(self.g.at[ch, 0:3, 0, 0, 0], self.zs[1].at[self.along(ch, 1)])
        for copy in self.p1_copies(ch, 0):
            copy.start()

    def turn(self, ch, k=0):
        from_x, from_y = self.p1_copies(ch, k, False)
        over_x, over_y = self.p2_copies(ch, k)
        from_y.wait_recv()
        over_x.start()
        from_x.wait_recv()
        over_y.start()

    def cross(self, ch):
        self.got(self.g.at[ch, :, 0, 0, 0], self.p2[1].at[ch])
        self.c_copy(ch).start()

    def arrive(self, ch):
        self.c_copy(ch, False).wait_recv()


    def late_copy(self, k, mine=True):
        at = self.at
        ref = self.g.at[LATE, at.z if mine else at.below(k), :, at.c]
        return remote(ref, ref, self.zs, self.along(LATE, k), at.to_z(k), (LATE,))

    def late_core(self, k, mine=True):
        at = self.at
        ref = self.g.at[LATE, at.below(k), :, at.c if mine else at.oc]
        return remote(ref, ref, self.cs, (LATE + k,), at.to_c)

    def late_z(self):
        self.got(self.g.at[LATE, 0:1, 0, 0, 0], self.p2[1].at[LATE])
        for k in range(1, NZ):
            self.late_copy(k).start()
        self.late_core(0).start()

    def late_cross(self, k):
        self.late_copy(k, False).wait_recv()
        self.late_core(k).start()

    def late_arrive(self, k):
        self.late_core(k, False).wait_recv()

    def all_of(self, ref, sem):
        return pltpu.make_async_remote_copy(
            src_ref=ref, dst_ref=ref, send_sem=sem, recv_sem=sem, device_id=self.at.to_c,
            device_id_type=pl.DeviceIdType.MESH,
        )

    def sent(self, ref, sem):
        self.all_of(ref, sem).wait_send()

    def got(self, ref, sem):
        self.all_of(ref, sem).wait_recv()

    def drain(self, ch):
        self.sent(self.g.at[ch, 0:3, 0, 0, 0], self.zs[0].at[ch])
        self.sent(self.g.at[ch, :, :, 0, 0], self.p1[0].at[ch])
        self.sent(self.g.at[ch, :, 0, 0, 0], self.p2[0].at[ch])
        self.c_copy(ch).wait_send()

    def late_drain(self):
        self.sent(self.g.at[LATE, 0:3, :, 0], self.zs[0].at[LATE])
        self.sent(self.g.at[LATE, 0:1, :, 0, 0], self.p1[0].at[LATE])
        self.sent(self.g.at[LATE, 0:1, 0, 0, 0], self.p2[0].at[LATE])
        for k in range(NZ):
            self.late_core(k).wait_send()


def fold(wide):
    return jnp.concatenate([wide[:, :COLS], wide[:, COLS:]], axis=0)


def pack_weights(refs, put):
    q, k, v, o, inner, outer = refs
    units = [r[...].astype(F32) for r in (q, k, v, o)]
    wide = inner[...].astype(F32)
    units += [wide[:, WIDTH * i : WIDTH * (i + 1)] for i in range(4)]
    for ch in range(4):
        put(ch, jnp.concatenate([fold(units[2 * ch]), fold(units[2 * ch + 1])], axis=0).astype(BF))
    tall = outer[...]
    put(4, tall[:, :COLS])
    put(5, tall[:, COLS:])


def unpack_weights(g, ch, w):
    def one(pair):
        z, x, c = pair // (NX * NC), (pair // NC) % NX, pair % NC
        a = g[ch, z, x, c, 0].astype(F32)
        b = g[ch, z, x, c, 1].astype(F32)
        for unit in range(2):
            base = 48 * unit
            left = jnp.concatenate([a[base : base + 24], b[base : base + 24]], axis=0)
            right = jnp.concatenate([a[base + 24 : base + 48], b[base + 24 : base + 48]], axis=0)
            at = WIDTH * (2 * ch + unit)
            rows = pl.ds(pl.multiple_of(48 * pair, 48), 48)
            w[rows, at : at + COLS] = left.astype(BF)
            w[rows, at + COLS : at + WIDTH] = right.astype(BF)

    loop(GROUP, one)


def spread(gv, vec, ib):
    owners = GROUP * NY
    parts = gv[...].astype(F32).reshape(owners, 16, 128)
    across = lax.broadcasted_iota(jnp.int32, (128, WIDTH), 1)
    lane = lax.broadcasted_iota(jnp.int32, (128, WIDTH), 0)
    device = lax.broadcasted_iota(jnp.int32, (owners, 8, WIDTH), 0)
    col = lax.broadcasted_iota(jnp.int32, (owners, 8, WIDTH), 2)

    def placed(flat, size, start):
        pick = (rem(across + start, size) == lane).astype(F32).astype(BF)
        wide = jnp.dot(flat, pick, preferred_element_type=F32).reshape(owners, 8, WIDTH)
        first = device * size - start
        return jnp.sum(jnp.where((col >= first) & (col < first + size), wide, 0.0), axis=0)

    vec[...] = placed(parts[:, 0:8].reshape(owners * 8, 128).astype(BF), 24, 0)
    flat = parts[:, 8:16].reshape(owners * 8, 128).astype(BF)
    for i in range(4):
        total = placed(flat, 96, WIDTH * i)[0:1]
        ib[:, WIDTH * i : WIDTH * (i + 1)] = jnp.broadcast_to(total, (8, WIDTH))


class Scatter:
    def __init__(self, at, s, r1, rd, rx, ry, rz, early, earlier, sent, got, cs, p2, p1, zs):
        self.at, self.s = at, s
        self.early, self.sent, self.got = early, sent, got
        self.erd, self.erx, self.ery = earlier
        self.r1, self.rd, self.rx, self.ry, self.rz = r1, rd, rx, ry, rz
        self.cs, self.p2, self.p1, self.zs = cs, p2, p1, zs

    def slot(self, ch):
        return 1 if ch == CHUNKS - 1 else ch

    def c_copy(self, ch):
        at = self.at
        return remote(self.s.at[ch, :, :, at.oc], self.r1.at[self.slot(ch)], self.cs, (ch,), at.to_c)

    def some(self, ch, k):
        if k is None:
            return slice(None), ch
        return pl.ds(self.at.above(k), 1), FINE[0] + NZ * FINE.index(ch) + k

    def p2_copies(self, ch, k=None):
        at = self.at
        some, index = self.some(ch, k)
        head, tail = cut(CUTS_S[ch])
        corner = self.s.at[ch, some, at.ox, at.c, at.oy]
        return (
            remote(corner.at[:, head], self.rd.at[ch - 1, some, head], self.p2, (index, 0), at.to_x, (ch,)),
            remote(corner.at[:, tail], self.rd.at[ch - 1, some, tail], self.p2, (index, 1), at.to_y, (ch,)),
        )

    def p1_copies(self, ch, k=None):
        at = self.at
        some, index = self.some(ch, k)
        return (
            remote(self.s.at[ch, some, at.ox, at.c, at.y], self.rx.at[ch - 1, some], self.p1, (index,), at.to_x, (ch,)),
            remote(self.s.at[ch, some, at.x, at.c, at.oy], self.ry.at[ch - 1, some], self.p1, (index,), at.to_y, (ch,)),
        )

    def z_copy(self, ch, k):
        at = self.at
        return remote(
            self.s.at[ch, at.above(k), at.x, at.c, at.y], self.rz.at[ch - 1, k - 1], self.zs, (ch,), at.to_z(k)
        )

    def first_copies(self):
        at, s, r1 = self.at, self.s, self.r1
        pieces = (
            (s.at[1, :, at.ox, at.oc, at.oy], r1.at[1, :, at.ox, at.oy]),
            (s.at[1, :, at.ox, at.oc, at.y], r1.at[1, :, at.ox, at.y]),
            (s.at[1, :, at.x, at.oc], r1.at[1, :, at.x]),
        )
        return [remote(src, dst, self.cs, (index,), at.to_c) for (src, dst), index in zip(pieces, (1, CHUNKS, CHUNKS + 1))]

    def start(self, ch):
        self.c_copy(ch).start()

    def start_first(self, piece):
        self.first_copies()[piece].start()

    def add_core(self, ch, x, y):
        def one(z):
            total = self.s[ch, z, x, self.at.c, y].astype(F32) + self.r1[self.slot(ch), z, x, y].astype(F32)
            self.s[ch, z, x, self.at.c, y] = total.astype(BF)

        loop(NZ, one)

    def core(self, ch):
        at = self.at
        self.c_copy(ch).wait_recv()
        self.add_core(ch, at.ox, at.oy)
        for k in (1, 2, 3, 0) if ch in FINE else (None,):
            for copy in self.p2_copies(ch, k):
                copy.start()
        self.add_core(ch, at.ox, at.y)
        self.add_core(ch, at.x, at.oy)
        self.add_core(ch, at.x, at.y)

    def core_first(self):
        self.first_copies()[0].wait_recv()
        self.add_core(1, self.at.ox, self.at.oy)
        for copy in self.p2_copies(1):
            copy.start()

    def core_rest(self):
        at = self.at
        for copy in self.first_copies()[1:]:
            copy.wait_recv()
        self.add_core(1, at.ox, at.y)
        self.add_core(1, at.x, at.oy)
        self.add_core(1, at.x, at.y)

    def over(self, k, work):
        if k is None:
            loop(NZ, work)
        else:
            work(self.at.above(k))

    def diagonal(self, ch, k=None):
        at = self.at
        over_x, over_y = self.p2_copies(ch, k)
        to_x, to_y = self.p1_copies(ch, k)
        head, tail = cut(CUTS_S[ch])
        over_x.wait_recv()

        def first(z):
            total = self.s[ch, z, at.x, at.c, at.oy, head].astype(F32) + self.rd[ch - 1, z, head].astype(F32)
            self.s[ch, z, at.x, at.c, at.oy, head] = total.astype(BF)

        self.over(k, first)
        to_y.start()
        over_y.wait_recv()

        def second(z):
            total = self.s[ch, z, at.ox, at.c, at.y, tail].astype(F32) + self.rd[ch - 1, z, tail].astype(F32)
            self.s[ch, z, at.ox, at.c, at.y, tail] = total.astype(BF)

        self.over(k, second)
        to_x.start()

    def plane(self, ch, k=None):
        at = self.at
        some = slice(None) if k is None else slice(0, 1)
        self.got(self.s.at[ch, some, :, 0, 0], self.p1[1].at[self.some(ch, k)[1]])

        def one(z):
            total = self.s[ch, z, at.x, at.c, at.y].astype(F32) + self.rx[ch - 1, z].astype(F32)
            total = total + self.ry[ch - 1, z].astype(F32)
            self.s[ch, z, at.x, at.c, at.y] = total.astype(BF)

        self.over(k, one)
        for j in range(1, NZ) if k is None else (k,) if k else ():
            self.z_copy(ch, j).start()

    def finish(self, ch):
        at = self.at
        self.got(self.s.at[ch, 0:3, 0, 0, 0], self.zs[1].at[ch])
        total = self.s[ch, at.z, at.x, at.c, at.y].astype(F32)
        for k in range(NZ - 1):
            total = total + self.rz[ch - 1, k].astype(F32)
        return total

    def drain(self, ch):
        for copy in self.first_copies() if ch == 1 else (self.c_copy(ch),):
            copy.wait_send()
        self.sent(self.s.at[ch, :, 0, 0, 0], self.p2[0].at[ch])
        self.sent(self.s.at[ch, :, :, 0, 0], self.p1[0].at[ch])
        self.sent(self.s.at[ch, 0:3, 0, 0, 0], self.zs[0].at[ch])


    def early_z(self):
        at = self.at
        return [
            remote(self.s.at[0, at.above(k), :, at.c], self.early.at[k - 1], self.zs, (0,), at.to_z(k))
            for k in range(1, NZ)
        ]

    def early_p2(self):
        at = self.at
        head, tail = cut(CUTS_S[0])
        return (
            remote(self.s.at[0, at.z, at.ox, at.c, at.oy, head], self.erd.at[head], self.p2, (0, 0), at.to_x, (0,)),
            remote(self.s.at[0, at.z, at.ox, at.c, at.oy, tail], self.erd.at[tail], self.p2, (0, 1), at.to_y, (0,)),
        )

    def early_p1(self):
        at = self.at
        return (
            remote(self.s.at[0, at.z, at.ox, at.c, at.y], self.erx, self.p1, (0,), at.to_x),
            remote(self.s.at[0, at.z, at.x, at.c, at.oy], self.ery, self.p1, (0,), at.to_y),
        )

    def early_copy(self, k):
        at = self.at
        z = at.above(k)
        index = CHUNKS + 1 + k if k else 0
        return remote(self.s.at[0, z, :, at.oc], self.r1.at[0, z], self.cs, (index,), at.to_c)

    def early_start(self, k):
        self.early_copy(k).start()

    def early_core(self, k):
        at = self.at
        self.early_copy(k).wait_recv()
        z = at.above(k)

        def one(i):
            x, y = i // NY, rem(i, NY)
            total = self.s[0, z, x, at.c, y].astype(F32) + self.r1[0, z, x, y].astype(F32)
            self.s[0, z, x, at.c, y] = total.astype(BF)

        loop(NX * NY, one)
        if k:
            self.early_z()[k - 1].start()

    def early_plane(self):
        at = self.at
        self.got(self.s.at[0, 0:3, :, 0], self.zs[1].at[0])

        def one(i):
            x, y = i // NY, rem(i, NY)
            total = self.s[0, at.z, x, at.c, y].astype(F32)
            for k in range(NZ - 1):
                total = total + self.early[k, x, y].astype(F32)
            self.s[0, at.z, x, at.c, y] = total.astype(BF)

        loop(NX * NY, one)
        for copy in self.early_p2():
            copy.start()

    def early_diagonal(self):
        at = self.at
        over_x, over_y = self.early_p2()
        to_x, to_y = self.early_p1()
        head, tail = cut(CUTS_S[0])
        over_x.wait_recv()
        total = self.s[0, at.z, at.x, at.c, at.oy, head].astype(F32) + self.erd[head].astype(F32)
        self.s[0, at.z, at.x, at.c, at.oy, head] = total.astype(BF)
        to_y.start()
        over_y.wait_recv()
        total = self.s[0, at.z, at.ox, at.c, at.y, tail].astype(F32) + self.erd[tail].astype(F32)
        self.s[0, at.z, at.ox, at.c, at.y, tail] = total.astype(BF)
        to_x.start()

    def early_finish(self):
        at = self.at
        self.got(self.s.at[0, 0:1, :, 0, 0], self.p1[1].at[0])
        total = self.s[0, at.z, at.x, at.c, at.y].astype(F32) + self.erx[...].astype(F32)
        return total + self.ery[...].astype(F32)

    def early_drain(self):
        for k in range(NZ):
            self.early_copy(k).wait_send()
        self.sent(self.s.at[0, 0:1, 0, 0, 0], self.p2[0].at[0])
        self.sent(self.s.at[0, 0:1, :, 0, 0], self.p1[0].at[0])
        self.sent(self.s.at[0, 0:3, :, 0], self.zs[0].at[0])


def unfold(total, unit):
    base = 48 * unit
    return jnp.concatenate([total[base : base + 24], total[base + 24 : base + 48]], axis=1)


class VectorScatter:
    def __init__(self, at, s, rc, rx, ry, rz, sems):
        self.at, self.s = at, s
        self.rc, self.rx, self.ry, self.rz, self.sems = rc, rx, ry, rz, sems
        at = self.at
        self.cc = remote(s.at[:, :, at.oc], rc, sems, 0, at.to_c)
        self.xx = remote(s.at[:, at.ox, at.c], rx, sems, 1, at.to_x)
        self.yy = remote(s.at[:, at.x, at.c, at.oy], ry, sems, 2, at.to_y)
        self.zz = [
            remote(s.at[at.above(k), at.x, at.c, at.y], rz.at[k - 1], sems, 2 + k, at.to_z(k)) for k in range(1, NZ)
        ]

    def start(self):
        self.cc.start()

    def core(self):
        self.cc.wait_recv()
        self.s[:, :, self.at.c] = self.s[:, :, self.at.c] + self.rc[...]
        self.xx.start()

    def over_x(self):
        at = self.at
        self.xx.wait_recv()
        self.s[:, at.x, at.c] = self.s[:, at.x, at.c] + self.rx[...]
        self.yy.start()

    def over_y(self):
        at = self.at
        self.yy.wait_recv()
        self.s[:, at.x, at.c, at.y] = self.s[:, at.x, at.c, at.y] + self.ry[...]
        for copy in self.zz:
            copy.start()

    def finish(self):
        at = self.at
        for copy in self.zz:
            copy.wait_recv()
        return self.s[at.z, at.x, at.c, at.y] + self.rz[0] + self.rz[1] + self.rz[2]

    def drain(self):
        for copy in [self.cc, self.xx, self.yy] + self.zz:
            copy.wait_send()


def own_part(value, stride):
    if stride == 1:
        return value
    whole = lax.all_gather(value, ("dp", "blk"), axis=0, tiled=True)
    rows = whole.shape[0] // (GROUP * NY)
    index = (lax.axis_index("dp") // stride) * NY + lax.axis_index("blk")
    return lax.dynamic_slice_in_dim(whole, index * rows, rows, axis=0)


def fine_part(value, stride):
    if stride == 1:
        return value
    index = (lax.axis_index("dp") // stride) * NY + lax.axis_index("blk")
    rows = value.shape[0]
    whole = jnp.zeros((rows * GROUP * NY,) + value.shape[1:], value.dtype)
    whole = lax.dynamic_update_slice_in_dim(whole, value, index * rows, axis=0)
    return lax.psum_scatter(whole, ("dp", "blk"), scatter_dimension=0, tiled=True)


def product(left, right):
    return jnp.dot(left, right, preferred_element_type=F32)


def product_left(left, right):
    return lax.dot_general(left, right, (((0,), (0,)), ((), ())), preferred_element_type=F32)


def product_right(left, right):
    return lax.dot_general(left, right, (((1,), (1,)), ((), ())), preferred_element_type=F32)


def tile(i, size):
    return pl.ds(pl.multiple_of(i * size, size), size)


def mean(values):
    return jnp.mean(values, axis=-1, keepdims=True)


def column(values):
    return jnp.sum(values, axis=0, keepdims=True)


def gather_vectors(vg, ibg, sv):
    owners = GROUP * NY
    across = lax.broadcasted_iota(jnp.int32, (WIDTH, 128), 0)
    lane = lax.broadcasted_iota(jnp.int32, (WIDTH, 128), 1)

    def pieces(wide, size, start):
        pick = ((rem(across + start, size) == lane) & (lane < size)).astype(F32).astype(BF)
        high = wide.astype(BF)
        rest = (wide - high.astype(F32)).astype(BF)
        return product(high, pick) + product(rest, pick)

    def owned(shape, size, start):
        first = lax.broadcasted_iota(jnp.int32, shape, 0) * size - start
        col = lax.broadcasted_iota(jnp.int32, shape, len(shape) - 1)
        return (col >= first) & (col < first + size)

    wide = jnp.where(owned((owners, 8, WIDTH), 24, 0), vg[...][None], 0.0)
    total = pieces(wide.reshape(owners * 8, WIDTH), 24, 0)
    sv[:, :, :, :, 0:8] = total.reshape(NZ, NX, NC, NY, 8, 128)
    total = jnp.zeros((owners, 128), F32)
    for i in range(4):
        part = ibg[0:1, WIDTH * i : WIDTH * (i + 1)]
        wide = jnp.where(owned((owners, WIDTH), 96, WIDTH * i), part, 0.0)
        total = total + pieces(wide, 96, WIDTH * i)
    total = jnp.broadcast_to(total[:, None, :], (owners, 8, 128))
    sv[:, :, :, :, 8:16] = total.reshape(NZ, NX, NC, NY, 8, 128)


def play(schedule, steps, loops):
    at = 0
    while at < len(schedule):
        name, *numbers = schedule[at].split()
        numbers = [int(n) for n in numbers]
        if name not in loops:
            steps[name](*numbers)
            at += 1
            continue
        turns = [i for i, entry in enumerate(schedule) if entry.split()[0] == name]
        between = [schedule[i + 1 : j] for i, j in zip(turns, turns[1:])]

        def turn(i):
            loops[name](i)
            for index, entries in enumerate(between):
                if entries:
                    pl.when(i == index)(partial(play, entries, steps, {}))

        loop(len(turns), turn)
        at = turns[-1] + 1


QB, VB, OB, G1, S1, UB, G2, S2 = range(8)


def layer_kernel(
    stride,
    q, k, v, o, inner, outer, qb, vb, ob, g1, s1, ub, g2, s2, inner_bias, pad, hidden, grad, lengths,
    out, igrad, dq, dk, dv, do, di, du, dsmall, saved,
    g, gv, wd, u, page, cot, dead, mask, small, hid, qkv, outp, xt, hidt, ctxt, actt,
    n1, acc1, acc2, bias, vec, ib, vg, ibg,
    sv, r1, rd, rx, ry, rz, early, erd, erx, ery, vc, vx, vy, vz,
    zs, zr, p1s, p1r, p2s, p2r, cs, cr, vs, vr, es, er,
    csr, q2r, q1r, zsr, wr, loads, saves, stores,
):
    at = Place(stride)
    gather = Gather(at, g, (zs, zr), (p1s, p1r), (p2s, p2r), (cs, cr))
    scatter = Scatter(
        at, g, r1, rd, rx, ry, rz, early, (erd, erx, ery), gather.sent, gather.got, (cs, csr), (p2s, q2r), (p1s, q1r), (zs, zsr)
    )
    vector = VectorScatter(at, sv, vc, vx, vy, vz, (vs, wr))

    def put(ch, value):
        g[ch, at.z, at.x, at.c, at.y] = value

    at.hail()
    pack_weights((q, k, v, o, inner, outer), put)
    small[...] = jnp.zeros_like(small)
    for i, ref in enumerate((qb, vb, ob, g1, s1, ub, g2, s2, inner_bias)):
        small[i : i + 1, 0 : ref.shape[-1]] = ref[...].astype(F32).reshape(1, ref.shape[-1])
    gv[at.z, at.x, at.c, at.y] = small[...].astype(BF)
    position = lax.broadcasted_iota(jnp.int32, (8, 256), 1) + at.y * 256
    for i in range(2):
        live = (position < lengths[i]) & (jnp.broadcast_to(pad[i : i + 1], (8, 256)) == 1)
        mask[i] = jnp.where(live, 0.0, NEG_FILL)
    own = pl.ds(pl.multiple_of(at.y * 256, 256), 256)
    theirs = pl.ds(pl.multiple_of(at.oy * 256, 256), 256)
    local = [
        pltpu.make_async_copy(hidden.at[at.y], page.at[own], loads.at[0]),
        pltpu.make_async_copy(grad.at[at.y], cot.at[own], loads.at[1]),
    ]
    for copy in local:
        copy.start()
    at.meet()

    ve, ee = (vs, vr), (es, er)
    page_in = remote(hidden.at[at.oy], page.at[own], ee, 0, at.to_y)
    mask_in = remote(mask.at[at.oy], dead.at[at.y], ee, 1, at.to_y)
    grad_in = remote(grad.at[at.oy], cot.at[own], ee, 2, at.to_y)
    out_over = remote(outp.at[theirs], out.at[at.y], ee, 3, at.to_y)
    grad_over = remote(cot.at[theirs], igrad.at[at.y], ee, 4, at.to_y)
    swaps = [page_in, mask_in, grad_in, out_over, grad_over]
    mine = gv.at[at.z, at.x, at.c, at.y]
    line = gv.at[:, at.x, at.c, at.y]
    pairs = gv.at[:, :, at.c, at.y]
    core = gv.at[:, :, at.c]
    vzs = [remote(mine, mine, ve, kk - 1, at.to_z(kk)) for kk in range(1, NZ)]
    vxs = remote(line, line, ve, 3, at.to_x)
    vys = remote(pairs, pairs, ve, 4, at.to_y)
    vcs = remote(core, core, ve, 5, at.to_c)

    def vector_z():
        for copy in vzs:
            copy.start()

    def vector_x():
        for copy in vzs:
            copy.wait_recv()
        vxs.start()

    def vector_y():
        vxs.wait_recv()
        vys.start()

    def vector_c():
        vys.wait_recv()
        vcs.start()

    def page_start():
        page_in.start()
        mask_in.start()

    def page_wait():
        for copy in local:
            copy.wait()
        page_in.wait_recv()
        mask_in.wait_recv()

    def turn(i):
        xt[tile(i, 256), :] = page[:, tile(i, 256)].T

    def prepare():
        dead[at.y] = mask[at.y]
        loop(3, turn)
        for half in range(2):
            bias[256 * half : 256 * half + 256] = jnp.broadcast_to(dead[half, 0:1].T, (256, 128))
        spread(gv, vec, ib)

    def queries(i):
        cols = tile(i, 256)
        value = product(page[...], wd[:, cols]) + vec[QB : QB + 1, cols]
        qkv[:, cols] = (value.astype(BF).astype(F32) * 0.125).astype(BF)

    def keys(i):
        cols = tile(i + 3, 256)
        qkv[:, cols] = product(page[...], wd[:, cols]).astype(BF)

    def vals(i):
        cols = tile(i + 6, 256)
        value = product(page[...], wd[:, cols]) + vec[VB : VB + 1, tile(i, 256)]
        qkv[:, cols] = value.astype(BF)

    def queries_keys():
        loop(3, queries)
        loop(3, keys)

    lane = lax.broadcasted_iota(jnp.int32, (512, 128), 1)
    sides = (lane < 64, lane >= 64)

    def side(value, which):
        return jnp.where(sides[which], value.astype(F32), 0.0).astype(BF)

    def save(pair):
        cols = tile(pair, 1024)
        return pltpu.make_async_copy(u.at[:, cols], saved.at[:, cols], saves.at[0])

    def attend(pair):
        at_q, at_k, at_v = tile(pair, 128), tile(pair + 6, 128), tile(pair + 12, 128)
        k2, v2 = qkv[:, at_k], qkv[:, at_v]
        total = jnp.zeros((128, 512), F32)
        for a in range(2):
            ka, va = side(k2, a), side(v2, a)
            for h in range(2):
                q2 = qkv[256 * h : 256 * h + 256, at_q]
                s = product_right(ka, q2) + jnp.concatenate([bias[...], bias[...]], axis=1)
                e = jnp.exp(s - jnp.max(s, axis=0, keepdims=True))
                p = e * (1.0 / jnp.sum(e, axis=0, keepdims=True))
                cols = pl.ds(pl.multiple_of(1024 * pair + 512 * a + 256 * h, 256), 256)
                u[:, cols] = p.astype(BF)
            cols = pl.ds(pl.multiple_of(1024 * pair + 512 * a, 512), 512)
            total = total + product_left(va, u[:, cols])
        ctxt[tile(pair, 128), :] = total.astype(BF)
        outp[:, tile(pair, 128)] = total.T.astype(BF)
        save(pair).start()

    def attended(i):
        cols = tile(i, 256)
        value = product(outp[...], wd[:, tile(i + 9, 256)]) + vec[OB : OB + 1, cols]
        acc1[:, cols] = page[:, cols].astype(F32) + value

    def first_norm(i):
        rows = tile(i, 64)
        joined = acc1[rows, :]
        center = joined - mean(joined)
        inverse = lax.rsqrt(mean(center * center) + EPSILON)
        normed = center * inverse
        n1[rows, :] = normed
        bias[rows, 64:128] = jnp.broadcast_to(inverse, (64, 64))
        hid[rows, :] = (normed * vec[G1 : G1 + 1] + vec[S1 : S1 + 1]).astype(BF)

    def turn_hidden(i):
        hidt[tile(i, 256), :] = hid[:, tile(i, 256)].T

    def after_attention():
        loop(3, attended)
        loop(8, first_norm)
        loop(3, turn_hidden)
        pltpu.make_async_copy(u, saved, saves.at[0]).wait()

    def feed(i):
        cols = tile(i, 384)
        weight = wd[:, pl.ds(pl.multiple_of(4 * WIDTH + 384 * i, 384), 384)]
        acc1[:, 0:384] = product(hid[...], weight) + ib[0:1, cols]

        def one(r):
            rows = tile(r, 64)
            value = acc1[rows, 0:384]
            cdf = 0.5 + 0.5 * lax.erf(value * 0.7071067811865476)
            density = 0.3989422804014327 * jnp.exp(-0.5 * value * value)
            u[rows, cols] = (value * cdf).astype(BF)
            u[rows, pl.ds(pl.multiple_of(3072 + 384 * i, 384), 384)] = (cdf + value * density).astype(BF)

        loop(8, one)
        actt[i // NX, rem(i, NX)] = u[:, cols].T.reshape(NC, NY, ROWS, 512)

    def outer_left():
        acc1[:, 0:COLS] = product(u[:, 0:3072], g[4].reshape(8 * COLS, COLS))

    def outer_right(step):
        z = at.below(step)
        value = product(u[:, tile(z, 768)], g[LATE, z].reshape(2 * COLS, COLS))
        acc1[:, COLS:] = value if step == 0 else acc1[:, COLS:] + value

    def cotangent():
        vg[...] = jnp.zeros_like(vg)

        def one(i):
            rows = tile(i, 64)
            dy = cot[rows, :].astype(F32)
            vg[S2 : S2 + 1] += column(dy)
            bias[rows, 0:64] = jnp.broadcast_to(mean(dy * vec[G2 : G2 + 1]), (64, 64))

        loop(8, one)

    def second_norm(i):
        gain = vec[G2 : G2 + 1]
        sums = [jnp.zeros((1, WIDTH), F32)] * 2
        for part in range(2):
            rows = tile(2 * i + part, 64)
            second = hid[rows, :].astype(F32) + (acc1[rows, :] + vec[UB : UB + 1])
            center = second - mean(second)
            inverse = lax.rsqrt(mean(center * center) + EPSILON)
            normed = center * inverse
            outp[rows, :] = (normed * gain + vec[S2 : S2 + 1]).astype(BF)
            dy = cot[rows, :].astype(F32)
            product_normed = dy * normed
            back = inverse * (dy * gain - bias[rows, 0:1] - normed * mean(product_normed * gain))
            acc2[rows, :] = back
            low = back.astype(BF)
            page[rows, :] = low
            sums = [sums[0] + column(product_normed), sums[1] + column(low.astype(F32))]
        vg[G2 : G2 + 1] += sums[0]
        vg[UB : UB + 1] += sums[1]

    play(
        FORWARD,
        {
            "z": gather.start_z,
            "own": gather.start_own,
            "plane": gather.plane,
            "turn": gather.turn,
            "cross": gather.cross,
            "arrive": gather.arrive,
            "late_z": gather.late_z,
            "late_cross": gather.late_cross,
            "late_arrive": gather.late_arrive,
            "plane_all": gather.plane_all,
            "cotangent": cotangent,
            "vector_z": vector_z,
            "vector_x": vector_x,
            "vector_y": vector_y,
            "vector_c": vector_c,
            "vector_wait": vcs.wait_recv,
            "page": page_start,
            "page_wait": page_wait,
            "grad": grad_in.start,
            "grad_wait": grad_in.wait_recv,
            "prepare": prepare,
            "unpack": lambda ch: unpack_weights(g, ch, wd),
            "queries_keys": queries_keys,
            "values": lambda: loop(3, vals),
            "after_attention": after_attention,
            "outer_left": outer_left,
            "outer_right": outer_right,
        },
        {"attend": attend, "feed": feed, "feed_on": lambda i: feed(i + 4)},
    )
    loop(4, second_norm)

    low = page
    keep = pltpu.make_async_copy(outp.at[own], out.at[at.y], loads.at[0])
    for ch in range(LATE):
        gather.drain(ch)
    gather.late_drain()

    for copy in vzs + [vxs, vys, vcs]:
        copy.wait_send()

    def out_start():
        out_over.start()
        keep.start()

    def outer_first(step):
        x, y = ((at.ox, at.oy), (at.ox, at.y), (at.x, at.oy), (at.x, at.y))[step]
        value = product(actt[:, x, :, y].reshape(2 * COLS, 512), low[:, 0:COLS]).astype(BF)
        g[1, :, x, :, y] = value.reshape(NZ, NC, ROWS, COLS)

    def outer_second(k):
        z = at.above(k)
        value = product(actt[z].reshape(2 * COLS, 512), low[:, COLS:]).astype(BF)
        g[0, z] = value.reshape(NX, NC, NY, ROWS, COLS)

    def load(part):
        cols = pl.ds(3072 * part, 3072)
        return pltpu.make_async_copy(saved.at[:, cols], u.at[:, cols], loads.at[1])

    load(0).start()

    def inner_back(i):
        weight = [g[4 + half, i].reshape(2 * COLS, COLS) for half in range(2)]
        value = product_right(low[...], jnp.concatenate(weight, axis=1))
        cols = pl.ds(pl.multiple_of(3072 + 768 * i, 768), 768)
        value = (value * u[:, cols].astype(F32)).astype(BF)
        u[:, cols] = value
        total = column(value.astype(F32))
        ibg[:, tile(i, 768)] = jnp.broadcast_to(total, (8, 768))

    def weight_grad(slot, unit, left, right):
        def one(i):
            value = product(left[tile(i, 384), :], right)
            value = value.reshape(16, 24, WIDTH)
            value = jnp.concatenate([value[:, :, :COLS], value[:, :, COLS:]], axis=1).astype(BF)
            g[slot, pl.ds(2 * i, 2), :, :, :, 48 * unit : 48 * unit + 48, :] = value.reshape(
                2, NX, NC, NY, 48, COLS
            )

        loop(2, one)

    def inner_grad(unit):
        right = u[:, 3072 + WIDTH * unit : 3072 + WIDTH * (unit + 1)]
        weight_grad(2 + unit // 2, unit % 2, hidt, right)

    def hidden_back(i):
        cols = tile(i, 256)
        acc2[:, cols] = acc2[:, cols] + product_right(u[:, 3072:6144], wd[cols, 4 * WIDTH :])

    def first_back(i):
        rows = tile(i, 64)
        up = acc2[rows, :]
        normed = n1[rows, :]
        vg[G1 : G1 + 1] += column(up * normed)
        vg[S1 : S1 + 1] += column(up)
        scaled = up * vec[G1 : G1 + 1]
        inverse = bias[rows, 64:65]
        back = inverse * (scaled - mean(scaled) - normed * mean(scaled * normed))
        acc2[rows, :] = back
        short = back.astype(BF)
        low[rows, :] = short
        vg[OB : OB + 1] += column(short.astype(F32))

    def context_back(i):
        cols = tile(i, 256)
        hid[:, cols] = product_right(low[...], wd[cols, 3 * WIDTH : 4 * WIDTH]).astype(BF)

    dst = hidt.at[pl.ds(0, 512), :]

    def attend_back(pair):
        at_q, at_k, at_v = tile(pair, 128), tile(pair + 6, 128), tile(pair + 12, 128)
        q2, k2, v2, c2 = qkv[:, at_q], qkv[:, at_k], qkv[:, at_v], hid[:, at_q]
        dqt = jnp.zeros((128, 512), F32)
        dk2 = jnp.zeros((512, 128), F32)
        dv2 = jnp.zeros((512, 128), F32)
        for a in range(2):
            va = side(v2, a)
            for h in range(2):
                cols = pl.ds(pl.multiple_of(1024 * pair + 512 * a + 256 * h, 256), 256)
                p = u[:, cols].astype(F32)
                d = product_right(va, c2[256 * h : 256 * h + 256])
                delta = jnp.sum(p * d, axis=0, keepdims=True)
                dst[:, 256 * h : 256 * h + 256] = (p * (d - delta)).astype(BF)
            cols = pl.ds(pl.multiple_of(1024 * pair + 512 * a, 512), 512)
            dv2 = dv2 + product(u[:, cols], side(c2, a))
            dk2 = dk2 + product(dst[...], side(q2, a))
            dqt = dqt + product_left(side(k2, a), dst[...])
        qkv[:, at_q] = (dqt.T * 0.125).astype(BF)
        qkv[:, at_k] = dk2.astype(BF)
        qkv[:, at_v] = dv2.astype(BF)

    def sums(i):
        rows = tile(i, 64)
        vg[QB : QB + 1] += column(qkv[rows, 0:WIDTH].astype(F32))
        vg[VB : VB + 1] += column(qkv[rows, 2 * WIDTH : 3 * WIDTH].astype(F32))

    def input_back(i):
        cols = tile(i, 256)
        value = acc2[:, cols] + product_right(qkv[...], wd[cols, 0 : 3 * WIDTH])
        cot[:, cols] = value.astype(BF)

    keep_in = pltpu.make_async_copy(cot.at[own], igrad.at[at.y], loads.at[1])

    def grad_start():
        grad_over.start()
        keep_in.start()

    def result(index):
        if index < 2:
            rows, cols = pl.ds(0, ROWS), pl.ds(COLS * (1 - index), COLS)
            target = du.at[:, cols]
        else:
            rows, cols = pl.ds(ROWS + 24 * (index - 2), 24), pl.ds(0, WIDTH)
            target = di.at[:, pl.ds(WIDTH * (index - 2), WIDTH)] if index < 6 else (dv, do, dq, dk)[index - 6]
        place = acc1.at[rows, cols]
        return place, pltpu.make_async_copy(place, target, stores.at[0])

    def store(index, value):
        place, copy = result(index)
        place[...] = value
        copy.start()

    def finish(n):
        total = scatter.finish(n) if n else scatter.early_finish()
        if n < 2:
            store(n, total)
        else:
            store(2 * n - 2, unfold(total, 0))
            store(2 * n - 1, unfold(total, 1))

    def vector_finish():
        dsmall[...] = vector.finish()

    def context_grad():
        load(1).start()
        loop(3, context_back)
        load(1).wait()

    def output_grad():
        weight_grad(4, 1, ctxt, low[...])

    def first_grad():
        loop(8, first_back)
        load(0).wait()

    play(
        BACKWARD,
        {
            "start": scatter.start,
            "core": scatter.core,
            "diagonal": scatter.diagonal,
            "plane": scatter.plane,
            "finish": finish,
            "early_start": scatter.early_start,
            "early_core": scatter.early_core,
            "early_plane": scatter.early_plane,
            "early_diagonal": scatter.early_diagonal,
            "vector": vector.start,
            "vector_core": vector.core,
            "vector_x": vector.over_x,
            "vector_y": vector.over_y,
            "vector_finish": vector_finish,
            "out": out_start,
            "grad": grad_start,
            "start_first": scatter.start_first,
            "core_first": scatter.core_first,
            "core_rest": scatter.core_rest,
            "outer_first": outer_first,
            "outer_second": outer_second,
            "inner_grad": inner_grad,
            "first_back": first_grad,
            "output_grad": output_grad,
            "context_back": context_grad,
            "value_grad": lambda: weight_grad(4, 0, xt, qkv[:, 2 * WIDTH : 3 * WIDTH]),
            "query_grad": lambda: weight_grad(5, 0, xt, qkv[:, 0:WIDTH]),
            "key_grad": lambda: weight_grad(5, 1, xt, qkv[:, WIDTH : 2 * WIDTH]),
            "sums": lambda: loop(8, sums),
            "gather_vectors": lambda: gather_vectors(vg, ibg, sv),
        },
        {
            "inner_back": inner_back,
            "hidden_back": hidden_back,
            "attend_back": attend_back,
            "input_back": input_back,
        },
    )
    keep.wait()
    keep_in.wait()
    stored = acc1.at[pl.ds(0, 3 * ROWS)]
    pltpu.make_async_copy(stored, stored, stores.at[0]).wait()
    out_over.wait_recv()
    grad_over.wait_recv()
    for n in range(1, CHUNKS):
        scatter.drain(n)
    scatter.early_drain()
    vector.drain()
    for copy in swaps:
        copy.wait_send()


def layer_call(stride, args):
    vmem = pl.BlockSpec(memory_space=pltpu.VMEM)
    hbm = pl.BlockSpec(memory_space=pl.ANY)
    dma = pltpu.SemaphoreType.DMA

    def shape(*dims, kind=F32):
        return jax.ShapeDtypeStruct(dims, kind)

    tokens = [shape(2, 256, WIDTH, kind=BF)] * 2
    grads = [shape(24, WIDTH)] * 4 + [shape(24, 4 * WIDTH), shape(96, WIDTH), shape(16, 128)]

    def low(*dims):
        return pltpu.VMEM(dims, BF)

    def full(*dims):
        return pltpu.VMEM(dims, F32)

    def pair(*dims):
        return [dma(dims), dma(dims)]

    return pl.pallas_call(
        partial(layer_kernel, stride),
        out_shape=tuple(tokens + grads + [shape(512, 12 * 512, kind=BF)]),
        in_specs=[vmem] * 16 + [hbm, hbm, pl.BlockSpec(memory_space=pltpu.SMEM)],
        out_specs=tuple([hbm] * 8 + [vmem, hbm]),
        scratch_shapes=[
            low(CHUNKS, NZ, NX, NC, NY, ROWS, COLS),
            low(NZ, NX, NC, NY, 16, 128),
            low(WIDTH, 8 * WIDTH),
            low(512, 12 * 512),
            low(512, WIDTH),
            low(512, WIDTH),
            full(2, 8, 256),
            full(2, 8, 256),
            full(16, 128),
            low(512, WIDTH),
            low(512, 3 * WIDTH),
            low(512, WIDTH),
            low(WIDTH, 512),
            low(WIDTH, 512),
            low(WIDTH, 512),
            low(NZ, NX, NC, NY, ROWS, 512),
            full(512, WIDTH),
            full(512, WIDTH),
            full(512, WIDTH),
            full(512, 128),
            full(8, WIDTH),
            full(8, 4 * WIDTH),
            full(8, WIDTH),
            full(8, 4 * WIDTH),
            full(NZ, NX, NC, NY, 16, 128),
            low(CHUNKS - 1, NZ, NX, NY, ROWS, COLS),
            low(CHUNKS - 1, NZ, ROWS, COLS),
            low(CHUNKS - 1, NZ, ROWS, COLS),
            low(CHUNKS - 1, NZ, ROWS, COLS),
            low(CHUNKS - 1, NZ - 1, ROWS, COLS),
            low(NZ - 1, NX, NY, ROWS, COLS),
            low(ROWS, COLS),
            low(ROWS, COLS),
            low(ROWS, COLS),
            full(NZ, NX, NY, 16, 128),
            full(NZ, NY, 16, 128),
            full(NZ, 16, 128),
            full(NZ - 1, 16, 128),
            dma((CHUNKS,)), dma((G_ALONG,)),
            dma((CHUNKS,)), dma((G_STEPS, 2)),
            *pair(CHUNKS),
            dma((CHUNKS + NZ + 1,)), dma((LATE + NZ,)),
            *pair(6),
            *pair(5),
            dma((CHUNKS + NZ + 1,)),
            dma((S_STEPS, 2)),
            dma((S_STEPS,)),
            dma((CHUNKS,)),
            dma((6,)),
            dma((2,)),
            dma((1,)),
            dma((1,)),
        ],
        compiler_params=pltpu.CompilerParams(
            collective_id=0, has_side_effects=True, vmem_limit_bytes=VMEM_LIMIT
        ),
        name="layer",
    )(*args)


def hand_out_kernel(*refs):
    large, small, outs, vectors = refs[:8], refs[8], refs[9:17], refs[17:26]
    held, into, back = refs[26:34], refs[34], refs[35]
    loads = [pltpu.make_async_copy(a, b, into.at[i]) for i, (a, b) in enumerate(zip(large, held))]
    stores = [pltpu.make_async_copy(a, b, back.at[i]) for i, (a, b) in enumerate(zip(held, outs))]
    for copy in loads:
        copy.start()
    for i, ref in enumerate(vectors):
        ref[...] = small[i, : ref.shape[0]]
    for load, store in zip(loads, stores):
        load.wait()
        store.start()
    for store in stores:
        store.wait()


def hand_out(large, small):
    vmem = pl.BlockSpec(memory_space=pltpu.VMEM)
    hbm = pl.BlockSpec(memory_space=pl.ANY)
    vectors = [jax.ShapeDtypeStruct((24,), F32)] * 8 + [jax.ShapeDtypeStruct((96,), F32)]
    return pl.pallas_call(
        hand_out_kernel,
        out_shape=tuple([jax.ShapeDtypeStruct(v.shape, v.dtype) for v in large] + vectors),
        in_specs=[hbm] * 8 + [vmem],
        out_specs=tuple([hbm] * 8 + [vmem] * 9),
        scratch_shapes=[pltpu.VMEM(v.shape, v.dtype) for v in large]
        + [pltpu.SemaphoreType.DMA((8,)), pltpu.SemaphoreType.DMA((8,))],
        name="hand_out",
    )(*large, small)


def body(
    stride,
    hidden_in,
    page_lengths,
    pad_mask,
    query_weight,
    query_bias,
    key_weight,
    value_weight,
    value_bias,
    output_weight,
    output_bias,
    first_gain,
    first_shift,
    inner_weight,
    inner_bias,
    outer_weight,
    outer_bias,
    second_gain,
    second_shift,
    out_grad,
):
    coarse = partial(own_part, stride=stride)
    fine = partial(fine_part, stride=stride)
    weights = (query_weight, key_weight, value_weight, output_weight, inner_weight, outer_weight)
    vectors = (
        query_bias, value_bias, output_bias, first_gain, first_shift, outer_bias, second_gain, second_shift, inner_bias,
    )
    parts = [coarse(v) for v in weights + vectors]
    *large, dsmall, _ = layer_call(stride, (*parts, pad_mask, hidden_in, out_grad, page_lengths))
    output, input_grad, *grads = hand_out(large, dsmall)
    dq, dk, dv, do, di, du, qbg, vbg, obg, g1g, s1g, ubg, g2g, s2g, ibg = [fine(v) for v in grads]
    return (
        output, input_grad, dq, qbg, dk, dv, vbg, do, obg, g1g, s1g, di, ibg, du, ubg, g2g, s2g,
    )


def solution(mesh):
    stride = mesh.shape["dp"] // GROUP
    row = P(("dp", "blk"))
    mat = P(("dp", "blk"), None)
    tok = P("dp", "blk", None)
    in_specs = (
        tok, P("dp"), P("dp", "blk"), mat, row, mat, mat, row, mat, row, row, row, mat, row, mat, row, row, row, tok,
    )
    out_specs = (
        tok, tok, mat, row, mat, mat, row, mat, row, row, row, mat, row, mat, row, row, row,
    )
    return jax.shard_map(
        partial(body, stride), mesh=mesh, in_specs=in_specs, out_specs=out_specs, check_vma=False
    )
```

```python
from functools import partial

import jax
import jax.numpy as jnp
from jax import lax
from jax.experimental import pallas as pl
from jax.experimental.pallas import tpu as pltpu
from jax.sharding import PartitionSpec as P

HEADS = 12
NEG_FILL = -1000000000.0
EPSILON = 1e-05

NZ, NX, NC, NY = 4, 2, 2, 2
GROUP = NZ * NX * NC
CHUNKS = 6
ROWS, COLS = 96, 384
LATE = 5
FINE_G, COARSE = (0, 1), (2, 3, 4)
G_STEPS = NZ * len(FINE_G) + len(COARSE) + 1
G_ALONG = len(COARSE) + (NZ - 1) * (len(FINE_G) + 1)
WIDTH = 768
CUTS_G = (64, 80, 48, 48, 64, 80)
CUTS_S = (32, 80, 64, 48, 48, 64)
FINE = (4, 5)
S_STEPS = FINE[0] + NZ * len(FINE)
BF, F32 = jnp.bfloat16, jnp.float32
VMEM_LIMIT = 63 * 2**20

FORWARD = (
    "own 5", "own 1", "vector_z", "z 0", "z 1", "turn 5 0", "own 0", "page", "turn 1 0", "plane 0 1",
    "vector_x", "z 2", "plane 0 3", "plane 0 2", "plane 1 1", "plane 1 2", "turn 0 1", "turn 0 0", "z 3",
    "plane 1 3", "turn 1 1", "page_wait", "turn 0 3", "vector_y", "turn 1 2", "turn 0 2", "turn 1 3", "z 4",
    "plane_all 2", "vector_c", "cross 0", "vector_wait", "cross 1", "prepare", "arrive 0", "late_z", "arrive 1",
    "plane_all 3", "unpack 0", "queries_keys", "turn 2", "unpack 1", "values", "attend 0", "attend 1",
    "attend 2", "plane_all 4", "attend 3", "attend 4", "turn 3", "cross 2", "attend 5", "after_attention",
    "arrive 2", "unpack 2", "feed 0", "turn 4", "grad", "feed 1", "late_arrive 0", "cross 3", "feed 2",
    "feed 3", "arrive 3", "unpack 3", "feed_on 4", "late_cross 1", "cross 4", "late_cross 2", "late_cross 3",
    "feed_on 5", "feed_on 6", "feed_on 7", "arrive 4", "outer_left", "outer_right 0", "late_arrive 1",
    "late_arrive 3", "outer_right 1", "late_arrive 2", "outer_right 2", "grad_wait", "cotangent",
    "outer_right 3",
)
BACKWARD = (
    "out", "outer_second 3", "outer_second 1", "outer_first 0", "start_first 0", "outer_first 1",
    "outer_first 2", "outer_second 2", "early_start 2", "inner_back 0", "core_first", "early_start 1",
    "early_core 2", "start_first 1", "outer_first 3", "start_first 2", "outer_second 0", "early_start 0",
    "inner_back 1", "inner_back 2", "inner_back 3", "early_start 3", "core_rest", "inner_grad 0", "diagonal 1",
    "early_core 3", "inner_grad 1", "early_core 1", "inner_grad 2", "early_core 0", "start 2", "inner_grad 3",
    "hidden_back 0", "hidden_back 1", "start 3", "core 2", "hidden_back 2", "first_back", "core 3",
    "context_back", "diagonal 2", "attend_back 0", "attend_back 1", "attend_back 2", "output_grad", "plane 1",
    "early_plane", "diagonal 3", "attend_back 3", "attend_back 4", "attend_back 5", "early_diagonal",
    "value_grad", "start 4", "key_grad", "sums", "query_grad", "plane 3", "start 5", "core 4", "gather_vectors",
    "diagonal 4 1", "diagonal 4 2", "finish 1", "plane 2", "vector", "input_back 0", "core 5", "plane 4 2",
    "finish 0", "diagonal 4 3", "vector_core", "plane 4 1", "diagonal 5 1", "input_back 1", "input_back 2",
    "diagonal 4 0", "finish 3", "diagonal 5 2", "diagonal 5 3", "vector_x", "plane 4 3", "diagonal 5 0",
    "plane 5 1", "grad", "plane 4 0", "plane 5 2", "plane 5 3", "finish 4", "plane 5 0", "vector_y", "finish 2",
    "vector_finish", "finish 5",
)


def rem(a, b):
    return lax.rem(a, b)


class Place:
    def __init__(self, stride):
        dp = lax.axis_index("dp")
        self.y = lax.axis_index("blk")
        index = dp // stride
        self.low = dp - index * stride
        self.stride = stride
        self.z = index // (NX * NC)
        self.x = (index // NC) % NX
        self.c = index % NC
        self.ox, self.oy, self.oc = 1 - self.x, 1 - self.y, 1 - self.c

    def dev(self, z, x, c, y):
        return ((z * (NX * NC) + x * NC + c) * self.stride + self.low, y)

    def above(self, k):
        return rem(self.z + k, NZ)

    def below(self, k):
        return rem(self.z + NZ - k, NZ)

    def to_z(self, k):
        return self.dev(self.above(k), self.x, self.c, self.y)

    @property
    def to_x(self):
        return self.dev(self.z, self.ox, self.c, self.y)

    @property
    def to_y(self):
        return self.dev(self.z, self.x, self.c, self.oy)

    @property
    def to_c(self):
        return self.dev(self.z, self.x, self.oc, self.y)

    def hail(self):
        partners = [self.to_z(k) for k in range(1, NZ)] + [self.to_x, self.to_y, self.to_c]
        for who in partners:
            pl.semaphore_signal(
                pltpu.get_barrier_semaphore(), inc=1, device_id=who, device_id_type=pl.DeviceIdType.MESH
            )

    def meet(self):
        pl.semaphore_wait(pltpu.get_barrier_semaphore(), NZ + 2)


def remote(src, dst, sems, index, who, group=None):
    send, recv = sems
    return pltpu.make_async_remote_copy(
        src_ref=src,
        dst_ref=dst,
        send_sem=send.at[index if group is None else group],
        recv_sem=recv.at[index],
        device_id=who,
        device_id_type=pl.DeviceIdType.MESH,
    )


def loop(count, body):
    def step(i, carry):
        body(i)
        return carry

    lax.fori_loop(0, count, step, 0)


def cut(rows):
    return pl.ds(0, rows), pl.ds(rows, ROWS - rows)


class Gather:
    def __init__(self, at, blocks, zs, p1, p2, cs):
        self.at, self.g = at, blocks
        self.zs, self.p1, self.p2, self.cs = zs, p1, p2, cs

    def z_copy(self, ch, k, mine=True):
        at = self.at
        z = at.z if mine else at.below(k)
        ref = self.g.at[ch, z, at.x, at.c, at.y]
        return remote(ref, ref, self.zs, self.along(ch, k), at.to_z(k), (ch,))

    def along(self, ch, k):
        if ch in COARSE:
            return (ch - COARSE[0],)
        return (len(COARSE) + (NZ - 1) * (FINE_G + (LATE,)).index(ch) + k - 1,)

    def some(self, ch, k):
        if ch in COARSE:
            return slice(None), NZ * len(FINE_G) + COARSE.index(ch)
        if ch == LATE:
            return pl.ds(self.at.z, 1), NZ * len(FINE_G) + len(COARSE)
        return pl.ds(self.at.below(k), 1), NZ * FINE_G.index(ch) + k

    def p1_copies(self, ch, k, mine=True):
        at = self.at
        z, index = self.some(ch, k)
        x, y = (at.x, at.y) if mine else (at.ox, at.oy)
        over_x = self.g.at[ch, z, x, at.c, at.y]
        over_y = self.g.at[ch, z, at.x, at.c, y]
        return (
            remote(over_x, over_x, self.p1, (index, 0), at.to_x, (ch,)),
            remote(over_y, over_y, self.p1, (index, 1), at.to_y, (ch,)),
        )

    def p2_copies(self, ch, k):
        at = self.at
        z, _ = self.some(ch, k)
        head, tail = cut(CUTS_G[ch])
        over_x = self.g.at[ch, z, at.x, at.c, at.oy, head]
        over_y = self.g.at[ch, z, at.ox, at.c, at.y, tail]
        return (
            remote(over_x, over_x, self.p2, (ch,), at.to_x),
            remote(over_y, over_y, self.p2, (ch,), at.to_y),
        )

    def c_copy(self, ch, mine=True):
        at = self.at
        ref = self.g.at[ch, :, :, at.c if mine else at.oc]
        return remote(ref, ref, self.cs, (ch,), at.to_c)

    def start_z(self, ch):
        for k in range(1, NZ):
            self.z_copy(ch, k).start()

    def start_own(self, ch):
        for copy in self.p1_copies(ch, 0):
            copy.start()

    def plane(self, ch, k):
        self.z_copy(ch, k, False).wait_recv()
        for copy in self.p1_copies(ch, k):
            copy.start()

    def plane_all(self, ch):
        self.got(self.g.at[ch, 0:3, 0, 0, 0], self.zs[1].at[self.along(ch, 1)])
        for copy in self.p1_copies(ch, 0):
            copy.start()

    def turn(self, ch, k=0):
        from_x, from_y = self.p1_copies(ch, k, False)
        over_x, over_y = self.p2_copies(ch, k)
        from_y.wait_recv()
        over_x.start()
        from_x.wait_recv()
        over_y.start()

    def cross(self, ch):
        self.got(self.g.at[ch, :, 0, 0, 0], self.p2[1].at[ch])
        self.c_copy(ch).start()

    def arrive(self, ch):
        self.c_copy(ch, False).wait_recv()


    def late_copy(self, k, mine=True):
        at = self.at
        ref = self.g.at[LATE, at.z if mine else at.below(k), :, at.c]
        return remote(ref, ref, self.zs, self.along(LATE, k), at.to_z(k), (LATE,))

    def late_core(self, k, mine=True):
        at = self.at
        ref = self.g.at[LATE, at.below(k), :, at.c if mine else at.oc]
        return remote(ref, ref, self.cs, (LATE + k,), at.to_c)

    def late_z(self):
        self.got(self.g.at[LATE, 0:1, 0, 0, 0], self.p2[1].at[LATE])
        for k in range(1, NZ):
            self.late_copy(k).start()
        self.late_core(0).start()

    def late_cross(self, k):
        self.late_copy(k, False).wait_recv()
        self.late_core(k).start()

    def late_arrive(self, k):
        self.late_core(k, False).wait_recv()

    def all_of(self, ref, sem):
        return pltpu.make_async_remote_copy(
            src_ref=ref, dst_ref=ref, send_sem=sem, recv_sem=sem, device_id=self.at.to_c,
            device_id_type=pl.DeviceIdType.MESH,
        )

    def sent(self, ref, sem):
        self.all_of(ref, sem).wait_send()

    def got(self, ref, sem):
        self.all_of(ref, sem).wait_recv()

    def drain(self, ch):
        self.sent(self.g.at[ch, 0:3, 0, 0, 0], self.zs[0].at[ch])
        self.sent(self.g.at[ch, :, :, 0, 0], self.p1[0].at[ch])
        self.sent(self.g.at[ch, :, 0, 0, 0], self.p2[0].at[ch])
        self.c_copy(ch).wait_send()

    def late_drain(self):
        self.sent(self.g.at[LATE, 0:3, :, 0], self.zs[0].at[LATE])
        self.sent(self.g.at[LATE, 0:1, :, 0, 0], self.p1[0].at[LATE])
        self.sent(self.g.at[LATE, 0:1, 0, 0, 0], self.p2[0].at[LATE])
        for k in range(NZ):
            self.late_core(k).wait_send()


def fold(wide):
    return jnp.concatenate([wide[:, :COLS], wide[:, COLS:]], axis=0)


def pack_weights(refs, put):
    q, k, v, o, inner, outer = refs
    units = [r[...].astype(F32) for r in (q, k, v, o)]
    wide = inner[...].astype(F32)
    units += [wide[:, WIDTH * i : WIDTH * (i + 1)] for i in range(4)]
    for ch in range(4):
        put(ch, jnp.concatenate([fold(units[2 * ch]), fold(units[2 * ch + 1])], axis=0).astype(BF))
    tall = outer[...]
    put(4, tall[:, :COLS])
    put(5, tall[:, COLS:])


def unpack_weights(g, ch, w):
    def one(pair):
        z, x, c = pair // (NX * NC), (pair // NC) % NX, pair % NC
        a = g[ch, z, x, c, 0].astype(F32)
        b = g[ch, z, x, c, 1].astype(F32)
        for unit in range(2):
            base = 48 * unit
            left = jnp.concatenate([a[base : base + 24], b[base : base + 24]], axis=0)
            right = jnp.concatenate([a[base + 24 : base + 48], b[base + 24 : base + 48]], axis=0)
            at = WIDTH * (2 * ch + unit)
            rows = pl.ds(pl.multiple_of(48 * pair, 48), 48)
            w[rows, at : at + COLS] = left.astype(BF)
            w[rows, at + COLS : at + WIDTH] = right.astype(BF)

    loop(GROUP, one)


def spread(gv, vec, ib):
    owners = GROUP * NY
    parts = gv[...].astype(F32).reshape(owners, 16, 128)
    across = lax.broadcasted_iota(jnp.int32, (128, WIDTH), 1)
    lane = lax.broadcasted_iota(jnp.int32, (128, WIDTH), 0)
    device = lax.broadcasted_iota(jnp.int32, (owners, 8, WIDTH), 0)
    col = lax.broadcasted_iota(jnp.int32, (owners, 8, WIDTH), 2)

    def placed(flat, size, start):
        pick = (rem(across + start, size) == lane).astype(F32).astype(BF)
        wide = jnp.dot(flat, pick, preferred_element_type=F32).reshape(owners, 8, WIDTH)
        first = device * size - start
        return jnp.sum(jnp.where((col >= first) & (col < first + size), wide, 0.0), axis=0)

    vec[...] = placed(parts[:, 0:8].reshape(owners * 8, 128).astype(BF), 24, 0)
    flat = parts[:, 8:16].reshape(owners * 8, 128).astype(BF)
    for i in range(4):
        total = placed(flat, 96, WIDTH * i)[0:1]
        ib[:, WIDTH * i : WIDTH * (i + 1)] = jnp.broadcast_to(total, (8, WIDTH))


class Scatter:
    def __init__(self, at, s, r1, rd, rx, ry, rz, early, earlier, sent, got, cs, p2, p1, zs):
        self.at, self.s = at, s
        self.early, self.sent, self.got = early, sent, got
        self.erd, self.erx, self.ery = earlier
        self.r1, self.rd, self.rx, self.ry, self.rz = r1, rd, rx, ry, rz
        self.cs, self.p2, self.p1, self.zs = cs, p2, p1, zs

    def slot(self, ch):
        return 1 if ch == CHUNKS - 1 else ch

    def c_copy(self, ch):
        at = self.at
        return remote(self.s.at[ch, :, :, at.oc], self.r1.at[self.slot(ch)], self.cs, (ch,), at.to_c)

    def some(self, ch, k):
        if k is None:
            return slice(None), ch
        return pl.ds(self.at.above(k), 1), FINE[0] + NZ * FINE.index(ch) + k

    def p2_copies(self, ch, k=None):
        at = self.at
        some, index = self.some(ch, k)
        head, tail = cut(CUTS_S[ch])
        corner = self.s.at[ch, some, at.ox, at.c, at.oy]
        return (
            remote(corner.at[:, head], self.rd.at[ch - 1, some, head], self.p2, (index, 0), at.to_x, (ch,)),
            remote(corner.at[:, tail], self.rd.at[ch - 1, some, tail], self.p2, (index, 1), at.to_y, (ch,)),
        )

    def p1_copies(self, ch, k=None):
        at = self.at
        some, index = self.some(ch, k)
        return (
            remote(self.s.at[ch, some, at.ox, at.c, at.y], self.rx.at[ch - 1, some], self.p1, (index,), at.to_x, (ch,)),
            remote(self.s.at[ch, some, at.x, at.c, at.oy], self.ry.at[ch - 1, some], self.p1, (index,), at.to_y, (ch,)),
        )

    def z_copy(self, ch, k):
        at = self.at
        return remote(
            self.s.at[ch, at.above(k), at.x, at.c, at.y], self.rz.at[ch - 1, k - 1], self.zs, (ch,), at.to_z(k)
        )

    def first_copies(self):
        at, s, r1 = self.at, self.s, self.r1
        pieces = (
            (s.at[1, :, at.ox, at.oc, at.oy], r1.at[1, :, at.ox, at.oy]),
            (s.at[1, :, at.ox, at.oc, at.y], r1.at[1, :, at.ox, at.y]),
            (s.at[1, :, at.x, at.oc], r1.at[1, :, at.x]),
        )
        return [remote(src, dst, self.cs, (index,), at.to_c) for (src, dst), index in zip(pieces, (1, CHUNKS, CHUNKS + 1))]

    def start(self, ch):
        self.c_copy(ch).start()

    def start_first(self, piece):
        self.first_copies()[piece].start()

    def add_core(self, ch, x, y):
        def one(z):
            total = self.s[ch, z, x, self.at.c, y].astype(F32) + self.r1[self.slot(ch), z, x, y].astype(F32)
            self.s[ch, z, x, self.at.c, y] = total.astype(BF)

        loop(NZ, one)

    def core(self, ch):
        at = self.at
        self.c_copy(ch).wait_recv()
        self.add_core(ch, at.ox, at.oy)
        for k in (1, 2, 3, 0) if ch in FINE else (None,):
            for copy in self.p2_copies(ch, k):
                copy.start()
        self.add_core(ch, at.ox, at.y)
        self.add_core(ch, at.x, at.oy)
        self.add_core(ch, at.x, at.y)

    def core_first(self):
        self.first_copies()[0].wait_recv()
        self.add_core(1, self.at.ox, self.at.oy)
        for copy in self.p2_copies(1):
            copy.start()

    def core_rest(self):
        at = self.at
        for copy in self.first_copies()[1:]:
            copy.wait_recv()
        self.add_core(1, at.ox, at.y)
        self.add_core(1, at.x, at.oy)
        self.add_core(1, at.x, at.y)

    def over(self, k, work):
        if k is None:
            loop(NZ, work)
        else:
            work(self.at.above(k))

    def diagonal(self, ch, k=None):
        at = self.at
        over_x, over_y = self.p2_copies(ch, k)
        to_x, to_y = self.p1_copies(ch, k)
        head, tail = cut(CUTS_S[ch])
        over_x.wait_recv()

        def first(z):
            total = self.s[ch, z, at.x, at.c, at.oy, head].astype(F32) + self.rd[ch - 1, z, head].astype(F32)
            self.s[ch, z, at.x, at.c, at.oy, head] = total.astype(BF)

        self.over(k, first)
        to_y.start()
        over_y.wait_recv()

        def second(z):
            total = self.s[ch, z, at.ox, at.c, at.y, tail].astype(F32) + self.rd[ch - 1, z, tail].astype(F32)
            self.s[ch, z, at.ox, at.c, at.y, tail] = total.astype(BF)

        self.over(k, second)
        to_x.start()

    def plane(self, ch, k=None):
        at = self.at
        some = slice(None) if k is None else slice(0, 1)
        self.got(self.s.at[ch, some, :, 0, 0], self.p1[1].at[self.some(ch, k)[1]])

        def one(z):
            total = self.s[ch, z, at.x, at.c, at.y].astype(F32) + self.rx[ch - 1, z].astype(F32)
            total = total + self.ry[ch - 1, z].astype(F32)
            self.s[ch, z, at.x, at.c, at.y] = total.astype(BF)

        self.over(k, one)
        for j in range(1, NZ) if k is None else (k,) if k else ():
            self.z_copy(ch, j).start()

    def finish(self, ch):
        at = self.at
        self.got(self.s.at[ch, 0:3, 0, 0, 0], self.zs[1].at[ch])
        total = self.s[ch, at.z, at.x, at.c, at.y].astype(F32)
        for k in range(NZ - 1):
            total = total + self.rz[ch - 1, k].astype(F32)
        return total

    def drain(self, ch):
        for copy in self.first_copies() if ch == 1 else (self.c_copy(ch),):
            copy.wait_send()
        self.sent(self.s.at[ch, :, 0, 0, 0], self.p2[0].at[ch])
        self.sent(self.s.at[ch, :, :, 0, 0], self.p1[0].at[ch])
        self.sent(self.s.at[ch, 0:3, 0, 0, 0], self.zs[0].at[ch])


    def early_z(self):
        at = self.at
        return [
            remote(self.s.at[0, at.above(k), :, at.c], self.early.at[k - 1], self.zs, (0,), at.to_z(k))
            for k in range(1, NZ)
        ]

    def early_p2(self):
        at = self.at
        head, tail = cut(CUTS_S[0])
        return (
            remote(self.s.at[0, at.z, at.ox, at.c, at.oy, head], self.erd.at[head], self.p2, (0, 0), at.to_x, (0,)),
            remote(self.s.at[0, at.z, at.ox, at.c, at.oy, tail], self.erd.at[tail], self.p2, (0, 1), at.to_y, (0,)),
        )

    def early_p1(self):
        at = self.at
        return (
            remote(self.s.at[0, at.z, at.ox, at.c, at.y], self.erx, self.p1, (0,), at.to_x),
            remote(self.s.at[0, at.z, at.x, at.c, at.oy], self.ery, self.p1, (0,), at.to_y),
        )

    def early_copy(self, k):
        at = self.at
        z = at.above(k)
        index = CHUNKS + 1 + k if k else 0
        return remote(self.s.at[0, z, :, at.oc], self.r1.at[0, z], self.cs, (index,), at.to_c)

    def early_start(self, k):
        self.early_copy(k).start()

    def early_core(self, k):
        at = self.at
        self.early_copy(k).wait_recv()
        z = at.above(k)

        def one(i):
            x, y = i // NY, rem(i, NY)
            total = self.s[0, z, x, at.c, y].astype(F32) + self.r1[0, z, x, y].astype(F32)
            self.s[0, z, x, at.c, y] = total.astype(BF)

        loop(NX * NY, one)
        if k:
            self.early_z()[k - 1].start()

    def early_plane(self):
        at = self.at
        self.got(self.s.at[0, 0:3, :, 0], self.zs[1].at[0])

        def one(i):
            x, y = i // NY, rem(i, NY)
            total = self.s[0, at.z, x, at.c, y].astype(F32)
            for k in range(NZ - 1):
                total = total + self.early[k, x, y].astype(F32)
            self.s[0, at.z, x, at.c, y] = total.astype(BF)

        loop(NX * NY, one)
        for copy in self.early_p2():
            copy.start()

    def early_diagonal(self):
        at = self.at
        over_x, over_y = self.early_p2()
        to_x, to_y = self.early_p1()
        head, tail = cut(CUTS_S[0])
        over_x.wait_recv()
        total = self.s[0, at.z, at.x, at.c, at.oy, head].astype(F32) + self.erd[head].astype(F32)
        self.s[0, at.z, at.x, at.c, at.oy, head] = total.astype(BF)
        to_y.start()
        over_y.wait_recv()
        total = self.s[0, at.z, at.ox, at.c, at.y, tail].astype(F32) + self.erd[tail].astype(F32)
        self.s[0, at.z, at.ox, at.c, at.y, tail] = total.astype(BF)
        to_x.start()

    def early_finish(self):
        at = self.at
        self.got(self.s.at[0, 0:1, :, 0, 0], self.p1[1].at[0])
        total = self.s[0, at.z, at.x, at.c, at.y].astype(F32) + self.erx[...].astype(F32)
        return total + self.ery[...].astype(F32)

    def early_drain(self):
        for k in range(NZ):
            self.early_copy(k).wait_send()
        self.sent(self.s.at[0, 0:1, 0, 0, 0], self.p2[0].at[0])
        self.sent(self.s.at[0, 0:1, :, 0, 0], self.p1[0].at[0])
        self.sent(self.s.at[0, 0:3, :, 0], self.zs[0].at[0])


def unfold(total, unit):
    base = 48 * unit
    return jnp.concatenate([total[base : base + 24], total[base + 24 : base + 48]], axis=1)


class VectorScatter:
    def __init__(self, at, s, rc, rx, ry, rz, sems):
        self.at, self.s = at, s
        self.rc, self.rx, self.ry, self.rz, self.sems = rc, rx, ry, rz, sems
        at = self.at
        self.cc = remote(s.at[:, :, at.oc], rc, sems, 0, at.to_c)
        self.xx = remote(s.at[:, at.ox, at.c], rx, sems, 1, at.to_x)
        self.yy = remote(s.at[:, at.x, at.c, at.oy], ry, sems, 2, at.to_y)
        self.zz = [
            remote(s.at[at.above(k), at.x, at.c, at.y], rz.at[k - 1], sems, 2 + k, at.to_z(k)) for k in range(1, NZ)
        ]

    def start(self):
        self.cc.start()

    def core(self):
        self.cc.wait_recv()
        self.s[:, :, self.at.c] = self.s[:, :, self.at.c] + self.rc[...]
        self.xx.start()

    def over_x(self):
        at = self.at
        self.xx.wait_recv()
        self.s[:, at.x, at.c] = self.s[:, at.x, at.c] + self.rx[...]
        self.yy.start()

    def over_y(self):
        at = self.at
        self.yy.wait_recv()
        self.s[:, at.x, at.c, at.y] = self.s[:, at.x, at.c, at.y] + self.ry[...]
        for copy in self.zz:
            copy.start()

    def finish(self):
        at = self.at
        for copy in self.zz:
            copy.wait_recv()
        return self.s[at.z, at.x, at.c, at.y] + self.rz[0] + self.rz[1] + self.rz[2]

    def drain(self):
        for copy in [self.cc, self.xx, self.yy] + self.zz:
            copy.wait_send()


def own_part(value, stride):
    if stride == 1:
        return value
    whole = lax.all_gather(value, ("dp", "blk"), axis=0, tiled=True)
    rows = whole.shape[0] // (GROUP * NY)
    index = (lax.axis_index("dp") // stride) * NY + lax.axis_index("blk")
    return lax.dynamic_slice_in_dim(whole, index * rows, rows, axis=0)


def fine_part(value, stride):
    if stride == 1:
        return value
    index = (lax.axis_index("dp") // stride) * NY + lax.axis_index("blk")
    rows = value.shape[0]
    whole = jnp.zeros((rows * GROUP * NY,) + value.shape[1:], value.dtype)
    whole = lax.dynamic_update_slice_in_dim(whole, value, index * rows, axis=0)
    return lax.psum_scatter(whole, ("dp", "blk"), scatter_dimension=0, tiled=True)


def product(left, right):
    return jnp.dot(left, right, preferred_element_type=F32)


def product_left(left, right):
    return lax.dot_general(left, right, (((0,), (0,)), ((), ())), preferred_element_type=F32)


def product_right(left, right):
    return lax.dot_general(left, right, (((1,), (1,)), ((), ())), preferred_element_type=F32)


def tile(i, size):
    return pl.ds(pl.multiple_of(i * size, size), size)


def mean(values):
    return jnp.mean(values, axis=-1, keepdims=True)


def column(values):
    return jnp.sum(values, axis=0, keepdims=True)


def gather_vectors(vg, ibg, sv):
    owners = GROUP * NY
    across = lax.broadcasted_iota(jnp.int32, (WIDTH, 128), 0)
    lane = lax.broadcasted_iota(jnp.int32, (WIDTH, 128), 1)

    def pieces(wide, size, start):
        pick = ((rem(across + start, size) == lane) & (lane < size)).astype(F32).astype(BF)
        high = wide.astype(BF)
        rest = (wide - high.astype(F32)).astype(BF)
        return product(high, pick) + product(rest, pick)

    def owned(shape, size, start):
        first = lax.broadcasted_iota(jnp.int32, shape, 0) * size - start
        col = lax.broadcasted_iota(jnp.int32, shape, len(shape) - 1)
        return (col >= first) & (col < first + size)

    wide = jnp.where(owned((owners, 8, WIDTH), 24, 0), vg[...][None], 0.0)
    total = pieces(wide.reshape(owners * 8, WIDTH), 24, 0)
    sv[:, :, :, :, 0:8] = total.reshape(NZ, NX, NC, NY, 8, 128)
    total = jnp.zeros((owners, 128), F32)
    for i in range(4):
        part = ibg[0:1, WIDTH * i : WIDTH * (i + 1)]
        wide = jnp.where(owned((owners, WIDTH), 96, WIDTH * i), part, 0.0)
        total = total + pieces(wide, 96, WIDTH * i)
    total = jnp.broadcast_to(total[:, None, :], (owners, 8, 128))
    sv[:, :, :, :, 8:16] = total.reshape(NZ, NX, NC, NY, 8, 128)


def play(schedule, steps, loops):
    at = 0
    while at < len(schedule):
        name, *numbers = schedule[at].split()
        numbers = [int(n) for n in numbers]
        if name not in loops:
            steps[name](*numbers)
            at += 1
            continue
        turns = [i for i, entry in enumerate(schedule) if entry.split()[0] == name]
        between = [schedule[i + 1 : j] for i, j in zip(turns, turns[1:])]

        def turn(i):
            loops[name](i)
            for index, entries in enumerate(between):
                if entries:
                    pl.when(i == index)(partial(play, entries, steps, {}))

        loop(len(turns), turn)
        at = turns[-1] + 1


QB, VB, OB, G1, S1, UB, G2, S2 = range(8)


def layer_kernel(
    stride,
    q, k, v, o, inner, outer, qb, vb, ob, g1, s1, ub, g2, s2, inner_bias, pad, hidden, grad, lengths,
    out, igrad, dq, dk, dv, do, di, du, dsmall, saved,
    g, gv, wd, u, page, cot, dead, mask, small, hid, qkv, outp, xt, hidt, ctxt, actt,
    n1, acc1, acc2, bias, vec, ib, vg, ibg,
    sv, r1, rd, rx, ry, rz, early, erd, erx, ery, vc, vx, vy, vz,
    zs, zr, p1s, p1r, p2s, p2r, cs, cr, vs, vr, es, er,
    csr, q2r, q1r, zsr, wr, loads, saves, stores,
):
    at = Place(stride)
    gather = Gather(at, g, (zs, zr), (p1s, p1r), (p2s, p2r), (cs, cr))
    scatter = Scatter(
        at, g, r1, rd, rx, ry, rz, early, (erd, erx, ery), gather.sent, gather.got, (cs, csr), (p2s, q2r), (p1s, q1r), (zs, zsr)
    )
    vector = VectorScatter(at, sv, vc, vx, vy, vz, (vs, wr))

    def put(ch, value):
        g[ch, at.z, at.x, at.c, at.y] = value

    at.hail()
    pack_weights((q, k, v, o, inner, outer), put)
    small[...] = jnp.zeros_like(small)
    for i, ref in enumerate((qb, vb, ob, g1, s1, ub, g2, s2, inner_bias)):
        small[i : i + 1, 0 : ref.shape[-1]] = ref[...].astype(F32).reshape(1, ref.shape[-1])
    gv[at.z, at.x, at.c, at.y] = small[...].astype(BF)
    position = lax.broadcasted_iota(jnp.int32, (8, 256), 1) + at.y * 256
    for i in range(2):
        live = (position < lengths[i]) & (jnp.broadcast_to(pad[i : i + 1], (8, 256)) == 1)
        mask[i] = jnp.where(live, 0.0, NEG_FILL)
    own = pl.ds(pl.multiple_of(at.y * 256, 256), 256)
    theirs = pl.ds(pl.multiple_of(at.oy * 256, 256), 256)
    local = [
        pltpu.make_async_copy(hidden.at[at.y], page.at[own], loads.at[0]),
        pltpu.make_async_copy(grad.at[at.y], cot.at[own], loads.at[1]),
    ]
    for copy in local:
        copy.start()
    at.meet()

    ve, ee = (vs, vr), (es, er)
    page_in = remote(hidden.at[at.oy], page.at[own], ee, 0, at.to_y)
    mask_in = remote(mask.at[at.oy], dead.at[at.y], ee, 1, at.to_y)
    grad_in = remote(grad.at[at.oy], cot.at[own], ee, 2, at.to_y)
    out_over = remote(outp.at[theirs], out.at[at.y], ee, 3, at.to_y)
    grad_over = remote(cot.at[theirs], igrad.at[at.y], ee, 4, at.to_y)
    swaps = [page_in, mask_in, grad_in, out_over, grad_over]
    mine = gv.at[at.z, at.x, at.c, at.y]
    line = gv.at[:, at.x, at.c, at.y]
    pairs = gv.at[:, :, at.c, at.y]
    core = gv.at[:, :, at.c]
    vzs = [remote(mine, mine, ve, kk - 1, at.to_z(kk)) for kk in range(1, NZ)]
    vxs = remote(line, line, ve, 3, at.to_x)
    vys = remote(pairs, pairs, ve, 4, at.to_y)
    vcs = remote(core, core, ve, 5, at.to_c)

    def vector_z():
        for copy in vzs:
            copy.start()

    def vector_x():
        for copy in vzs:
            copy.wait_recv()
        vxs.start()

    def vector_y():
        vxs.wait_recv()
        vys.start()

    def vector_c():
        vys.wait_recv()
        vcs.start()

    def page_start():
        page_in.start()
        mask_in.start()

    def page_wait():
        for copy in local:
            copy.wait()
        page_in.wait_recv()
        mask_in.wait_recv()

    def turn(i):
        xt[tile(i, 256), :] = page[:, tile(i, 256)].T

    def prepare():
        dead[at.y] = mask[at.y]
        loop(3, turn)
        for half in range(2):
            bias[256 * half : 256 * half + 256] = jnp.broadcast_to(dead[half, 0:1].T, (256, 128))
        spread(gv, vec, ib)

    def queries(i):
        cols = tile(i, 256)
        value = product(page[...], wd[:, cols]) + vec[QB : QB + 1, cols]
        qkv[:, cols] = (value.astype(BF).astype(F32) * 0.125).astype(BF)

    def keys(i):
        cols = tile(i + 3, 256)
        qkv[:, cols] = product(page[...], wd[:, cols]).astype(BF)

    def vals(i):
        cols = tile(i + 6, 256)
        value = product(page[...], wd[:, cols]) + vec[VB : VB + 1, tile(i, 256)]
        qkv[:, cols] = value.astype(BF)

    def queries_keys():
        loop(3, queries)
        loop(3, keys)

    lane = lax.broadcasted_iota(jnp.int32, (512, 128), 1)
    sides = (lane < 64, lane >= 64)

    def side(value, which):
        return jnp.where(sides[which], value.astype(F32), 0.0).astype(BF)

    def save(pair):
        cols = tile(pair, 1024)
        return pltpu.make_async_copy(u.at[:, cols], saved.at[:, cols], saves.at[0])

    def attend(pair):
        at_q, at_k, at_v = tile(pair, 128), tile(pair + 6, 128), tile(pair + 12, 128)
        k2, v2 = qkv[:, at_k], qkv[:, at_v]
        total = jnp.zeros((128, 512), F32)
        for a in range(2):
            ka, va = side(k2, a), side(v2, a)
            for h in range(2):
                q2 = qkv[256 * h : 256 * h + 256, at_q]
                s = product_right(ka, q2) + jnp.concatenate([bias[...], bias[...]], axis=1)
                e = jnp.exp(s - jnp.max(s, axis=0, keepdims=True))
                p = e * (1.0 / jnp.sum(e, axis=0, keepdims=True))
                cols = pl.ds(pl.multiple_of(1024 * pair + 512 * a + 256 * h, 256), 256)
                u[:, cols] = p.astype(BF)
            cols = pl.ds(pl.multiple_of(1024 * pair + 512 * a, 512), 512)
            total = total + product_left(va, u[:, cols])
        ctxt[tile(pair, 128), :] = total.astype(BF)
        outp[:, tile(pair, 128)] = total.T.astype(BF)
        save(pair).start()

    def attended(i):
        cols = tile(i, 256)
        value = product(outp[...], wd[:, tile(i + 9, 256)]) + vec[OB : OB + 1, cols]
        acc1[:, cols] = page[:, cols].astype(F32) + value

    def first_norm(i):
        rows = tile(i, 64)
        joined = acc1[rows, :]
        center = joined - mean(joined)
        inverse = lax.rsqrt(mean(center * center) + EPSILON)
        normed = center * inverse
        n1[rows, :] = normed
        bias[rows, 64:128] = jnp.broadcast_to(inverse, (64, 64))
        hid[rows, :] = (normed * vec[G1 : G1 + 1] + vec[S1 : S1 + 1]).astype(BF)

    def turn_hidden(i):
        hidt[tile(i, 256), :] = hid[:, tile(i, 256)].T

    def after_attention():
        loop(3, attended)
        loop(8, first_norm)
        loop(3, turn_hidden)
        pltpu.make_async_copy(u, saved, saves.at[0]).wait()

    def feed(i):
        cols = tile(i, 384)
        weight = wd[:, pl.ds(pl.multiple_of(4 * WIDTH + 384 * i, 384), 384)]
        acc1[:, 0:384] = product(hid[...], weight) + ib[0:1, cols]

        def one(r):
            rows = tile(r, 64)
            value = acc1[rows, 0:384]
            cdf = 0.5 + 0.5 * lax.erf(value * 0.7071067811865476)
            density = 0.3989422804014327 * jnp.exp(-0.5 * value * value)
            u[rows, cols] = (value * cdf).astype(BF)
            u[rows, pl.ds(pl.multiple_of(3072 + 384 * i, 384), 384)] = (cdf + value * density).astype(BF)

        loop(8, one)
        actt[i // NX, rem(i, NX)] = u[:, cols].T.reshape(NC, NY, ROWS, 512)

    def outer_left():
        acc1[:, 0:COLS] = product(u[:, 0:3072], g[4].reshape(8 * COLS, COLS))

    def outer_right(step):
        z = at.below(step)
        value = product(u[:, tile(z, 768)], g[LATE, z].reshape(2 * COLS, COLS))
        acc1[:, COLS:] = value if step == 0 else acc1[:, COLS:] + value

    def cotangent():
        vg[...] = jnp.zeros_like(vg)

        def one(i):
            rows = tile(i, 64)
            dy = cot[rows, :].astype(F32)
            vg[S2 : S2 + 1] += column(dy)
            bias[rows, 0:64] = jnp.broadcast_to(mean(dy * vec[G2 : G2 + 1]), (64, 64))

        loop(8, one)

    def second_norm(i):
        gain = vec[G2 : G2 + 1]
        sums = [jnp.zeros((1, WIDTH), F32)] * 2
        for part in range(2):
            rows = tile(2 * i + part, 64)
            second = hid[rows, :].astype(F32) + (acc1[rows, :] + vec[UB : UB + 1])
            center = second - mean(second)
            inverse = lax.rsqrt(mean(center * center) + EPSILON)
            normed = center * inverse
            outp[rows, :] = (normed * gain + vec[S2 : S2 + 1]).astype(BF)
            dy = cot[rows, :].astype(F32)
            product_normed = dy * normed
            back = inverse * (dy * gain - bias[rows, 0:1] - normed * mean(product_normed * gain))
            acc2[rows, :] = back
            low = back.astype(BF)
            page[rows, :] = low
            sums = [sums[0] + column(product_normed), sums[1] + column(low.astype(F32))]
        vg[G2 : G2 + 1] += sums[0]
        vg[UB : UB + 1] += sums[1]

    play(
        FORWARD,
        {
            "z": gather.start_z,
            "own": gather.start_own,
            "plane": gather.plane,
            "turn": gather.turn,
            "cross": gather.cross,
            "arrive": gather.arrive,
            "late_z": gather.late_z,
            "late_cross": gather.late_cross,
            "late_arrive": gather.late_arrive,
            "plane_all": gather.plane_all,
            "cotangent": cotangent,
            "vector_z": vector_z,
            "vector_x": vector_x,
            "vector_y": vector_y,
            "vector_c": vector_c,
            "vector_wait": vcs.wait_recv,
            "page": page_start,
            "page_wait": page_wait,
            "grad": grad_in.start,
            "grad_wait": grad_in.wait_recv,
            "prepare": prepare,
            "unpack": lambda ch: unpack_weights(g, ch, wd),
            "queries_keys": queries_keys,
            "values": lambda: loop(3, vals),
            "after_attention": after_attention,
            "outer_left": outer_left,
            "outer_right": outer_right,
        },
        {"attend": attend, "feed": feed, "feed_on": lambda i: feed(i + 4)},
    )
    loop(4, second_norm)

    low = page
    keep = pltpu.make_async_copy(outp.at[own], out.at[at.y], loads.at[0])
    for ch in range(LATE):
        gather.drain(ch)
    gather.late_drain()

    for copy in vzs + [vxs, vys, vcs]:
        copy.wait_send()

    def out_start():
        out_over.start()
        keep.start()

    def outer_first(step):
        x, y = ((at.ox, at.oy), (at.ox, at.y), (at.x, at.oy), (at.x, at.y))[step]
        value = product(actt[:, x, :, y].reshape(2 * COLS, 512), low[:, 0:COLS]).astype(BF)
        g[1, :, x, :, y] = value.reshape(NZ, NC, ROWS, COLS)

    def outer_second(k):
        z = at.above(k)
        value = product(actt[z].reshape(2 * COLS, 512), low[:, COLS:]).astype(BF)
        g[0, z] = value.reshape(NX, NC, NY, ROWS, COLS)

    def load(part):
        cols = pl.ds(3072 * part, 3072)
        return pltpu.make_async_copy(saved.at[:, cols], u.at[:, cols], loads.at[1])

    load(0).start()

    def inner_back(i):
        weight = [g[4 + half, i].reshape(2 * COLS, COLS) for half in range(2)]
        value = product_right(low[...], jnp.concatenate(weight, axis=1))
        cols = pl.ds(pl.multiple_of(3072 + 768 * i, 768), 768)
        value = (value * u[:, cols].astype(F32)).astype(BF)
        u[:, cols] = value
        total = column(value.astype(F32))
        ibg[:, tile(i, 768)] = jnp.broadcast_to(total, (8, 768))

    def weight_grad(slot, unit, left, right):
        def one(i):
            value = product(left[tile(i, 384), :], right)
            value = value.reshape(16, 24, WIDTH)
            value = jnp.concatenate([value[:, :, :COLS], value[:, :, COLS:]], axis=1).astype(BF)
            g[slot, pl.ds(2 * i, 2), :, :, :, 48 * unit : 48 * unit + 48, :] = value.reshape(
                2, NX, NC, NY, 48, COLS
            )

        loop(2, one)

    def inner_grad(unit):
        right = u[:, 3072 + WIDTH * unit : 3072 + WIDTH * (unit + 1)]
        weight_grad(2 + unit // 2, unit % 2, hidt, right)

    def hidden_back(i):
        cols = tile(i, 256)
        acc2[:, cols] = acc2[:, cols] + product_right(u[:, 3072:6144], wd[cols, 4 * WIDTH :])

    def first_back(i):
        rows = tile(i, 64)
        up = acc2[rows, :]
        normed = n1[rows, :]
        vg[G1 : G1 + 1] += column(up * normed)
        vg[S1 : S1 + 1] += column(up)
        scaled = up * vec[G1 : G1 + 1]
        inverse = bias[rows, 64:65]
        back = inverse * (scaled - mean(scaled) - normed * mean(scaled * normed))
        acc2[rows, :] = back
        short = back.astype(BF)
        low[rows, :] = short
        vg[OB : OB + 1] += column(short.astype(F32))

    def context_back(i):
        cols = tile(i, 256)
        hid[:, cols] = product_right(low[...], wd[cols, 3 * WIDTH : 4 * WIDTH]).astype(BF)

    dst = hidt.at[pl.ds(0, 512), :]

    def attend_back(pair):
        at_q, at_k, at_v = tile(pair, 128), tile(pair + 6, 128), tile(pair + 12, 128)
        q2, k2, v2, c2 = qkv[:, at_q], qkv[:, at_k], qkv[:, at_v], hid[:, at_q]
        dqt = jnp.zeros((128, 512), F32)
        dk2 = jnp.zeros((512, 128), F32)
        dv2 = jnp.zeros((512, 128), F32)
        for a in range(2):
            va = side(v2, a)
            for h in range(2):
                cols = pl.ds(pl.multiple_of(1024 * pair + 512 * a + 256 * h, 256), 256)
                p = u[:, cols].astype(F32)
                d = product_right(va, c2[256 * h : 256 * h + 256])
                delta = jnp.sum(p * d, axis=0, keepdims=True)
                dst[:, 256 * h : 256 * h + 256] = (p * (d - delta)).astype(BF)
            cols = pl.ds(pl.multiple_of(1024 * pair + 512 * a, 512), 512)
            dv2 = dv2 + product(u[:, cols], side(c2, a))
            dk2 = dk2 + product(dst[...], side(q2, a))
            dqt = dqt + product_left(side(k2, a), dst[...])
        qkv[:, at_q] = (dqt.T * 0.125).astype(BF)
        qkv[:, at_k] = dk2.astype(BF)
        qkv[:, at_v] = dv2.astype(BF)

    def sums(i):
        rows = tile(i, 64)
        vg[QB : QB + 1] += column(qkv[rows, 0:WIDTH].astype(F32))
        vg[VB : VB + 1] += column(qkv[rows, 2 * WIDTH : 3 * WIDTH].astype(F32))

    def input_back(i):
        cols = tile(i, 256)
        value = acc2[:, cols] + product_right(qkv[...], wd[cols, 0 : 3 * WIDTH])
        cot[:, cols] = value.astype(BF)

    keep_in = pltpu.make_async_copy(cot.at[own], igrad.at[at.y], loads.at[1])

    def grad_start():
        grad_over.start()
        keep_in.start()

    def result(index):
        if index < 2:
            rows, cols = pl.ds(0, ROWS), pl.ds(COLS * (1 - index), COLS)
            target = du.at[:, cols]
        else:
            rows, cols = pl.ds(ROWS + 24 * (index - 2), 24), pl.ds(0, WIDTH)
            target = di.at[:, pl.ds(WIDTH * (index - 2), WIDTH)] if index < 6 else (dv, do, dq, dk)[index - 6]
        place = acc1.at[rows, cols]
        return place, pltpu.make_async_copy(place, target, stores.at[0])

    def store(index, value):
        place, copy = result(index)
        place[...] = value
        copy.start()

    def finish(n):
        total = scatter.finish(n) if n else scatter.early_finish()
        if n < 2:
            store(n, total)
        else:
            store(2 * n - 2, unfold(total, 0))
            store(2 * n - 1, unfold(total, 1))

    def vector_finish():
        dsmall[...] = vector.finish()

    def context_grad():
        load(1).start()
        loop(3, context_back)
        load(1).wait()

    def output_grad():
        weight_grad(4, 1, ctxt, low[...])

    def first_grad():
        loop(8, first_back)
        load(0).wait()

    play(
        BACKWARD,
        {
            "start": scatter.start,
            "core": scatter.core,
            "diagonal": scatter.diagonal,
            "plane": scatter.plane,
            "finish": finish,
            "early_start": scatter.early_start,
            "early_core": scatter.early_core,
            "early_plane": scatter.early_plane,
            "early_diagonal": scatter.early_diagonal,
            "vector": vector.start,
            "vector_core": vector.core,
            "vector_x": vector.over_x,
            "vector_y": vector.over_y,
            "vector_finish": vector_finish,
            "out": out_start,
            "grad": grad_start,
            "start_first": scatter.start_first,
            "core_first": scatter.core_first,
            "core_rest": scatter.core_rest,
            "outer_first": outer_first,
            "outer_second": outer_second,
            "inner_grad": inner_grad,
            "first_back": first_grad,
            "output_grad": output_grad,
            "context_back": context_grad,
            "value_grad": lambda: weight_grad(4, 0, xt, qkv[:, 2 * WIDTH : 3 * WIDTH]),
            "query_grad": lambda: weight_grad(5, 0, xt, qkv[:, 0:WIDTH]),
            "key_grad": lambda: weight_grad(5, 1, xt, qkv[:, WIDTH : 2 * WIDTH]),
            "sums": lambda: loop(8, sums),
            "gather_vectors": lambda: gather_vectors(vg, ibg, sv),
        },
        {
            "inner_back": inner_back,
            "hidden_back": hidden_back,
            "attend_back": attend_back,
            "input_back": input_back,
        },
    )
    keep.wait()
    keep_in.wait()
    stored = acc1.at[pl.ds(0, 3 * ROWS)]
    pltpu.make_async_copy(stored, stored, stores.at[0]).wait()
    out_over.wait_recv()
    grad_over.wait_recv()
    for n in range(1, CHUNKS):
        scatter.drain(n)
    scatter.early_drain()
    vector.drain()
    for copy in swaps:
        copy.wait_send()


def layer_call(stride, args):
    vmem = pl.BlockSpec(memory_space=pltpu.VMEM)
    hbm = pl.BlockSpec(memory_space=pl.ANY)
    dma = pltpu.SemaphoreType.DMA

    def shape(*dims, kind=F32):
        return jax.ShapeDtypeStruct(dims, kind)

    tokens = [shape(2, 256, WIDTH, kind=BF)] * 2
    grads = [shape(24, WIDTH)] * 4 + [shape(24, 4 * WIDTH), shape(96, WIDTH), shape(16, 128)]

    def low(*dims):
        return pltpu.VMEM(dims, BF)

    def full(*dims):
        return pltpu.VMEM(dims, F32)

    def pair(*dims):
        return [dma(dims), dma(dims)]

    return pl.pallas_call(
        partial(layer_kernel, stride),
        out_shape=tuple(tokens + grads + [shape(512, 12 * 512, kind=BF)]),
        in_specs=[vmem] * 16 + [hbm, hbm, pl.BlockSpec(memory_space=pltpu.SMEM)],
        out_specs=tuple([hbm] * 8 + [vmem, hbm]),
        scratch_shapes=[
            low(CHUNKS, NZ, NX, NC, NY, ROWS, COLS),
            low(NZ, NX, NC, NY, 16, 128),
            low(WIDTH, 8 * WIDTH),
            low(512, 12 * 512),
            low(512, WIDTH),
            low(512, WIDTH),
            full(2, 8, 256),
            full(2, 8, 256),
            full(16, 128),
            low(512, WIDTH),
            low(512, 3 * WIDTH),
            low(512, WIDTH),
            low(WIDTH, 512),
            low(WIDTH, 512),
            low(WIDTH, 512),
            low(NZ, NX, NC, NY, ROWS, 512),
            full(512, WIDTH),
            full(512, WIDTH),
            full(512, WIDTH),
            full(512, 128),
            full(8, WIDTH),
            full(8, 4 * WIDTH),
            full(8, WIDTH),
            full(8, 4 * WIDTH),
            full(NZ, NX, NC, NY, 16, 128),
            low(CHUNKS - 1, NZ, NX, NY, ROWS, COLS),
            low(CHUNKS - 1, NZ, ROWS, COLS),
            low(CHUNKS - 1, NZ, ROWS, COLS),
            low(CHUNKS - 1, NZ, ROWS, COLS),
            low(CHUNKS - 1, NZ - 1, ROWS, COLS),
            low(NZ - 1, NX, NY, ROWS, COLS),
            low(ROWS, COLS),
            low(ROWS, COLS),
            low(ROWS, COLS),
            full(NZ, NX, NY, 16, 128),
            full(NZ, NY, 16, 128),
            full(NZ, 16, 128),
            full(NZ - 1, 16, 128),
            dma((CHUNKS,)), dma((G_ALONG,)),
            dma((CHUNKS,)), dma((G_STEPS, 2)),
            *pair(CHUNKS),
            dma((CHUNKS + NZ + 1,)), dma((LATE + NZ,)),
            *pair(6),
            *pair(5),
            dma((CHUNKS + NZ + 1,)),
            dma((S_STEPS, 2)),
            dma((S_STEPS,)),
            dma((CHUNKS,)),
            dma((6,)),
            dma((2,)),
            dma((1,)),
            dma((1,)),
        ],
        compiler_params=pltpu.CompilerParams(
            collective_id=0, has_side_effects=True, vmem_limit_bytes=VMEM_LIMIT
        ),
        name="layer",
    )(*args)


def hand_out_kernel(*refs):
    large, small, outs, vectors = refs[:8], refs[8], refs[9:17], refs[17:26]
    held, into, back = refs[26:34], refs[34], refs[35]
    loads = [pltpu.make_async_copy(a, b, into.at[i]) for i, (a, b) in enumerate(zip(large, held))]
    stores = [pltpu.make_async_copy(a, b, back.at[i]) for i, (a, b) in enumerate(zip(held, outs))]
    for copy in loads:
        copy.start()
    for i, ref in enumerate(vectors):
        ref[...] = small[i, : ref.shape[0]]
    for load, store in zip(loads, stores):
        load.wait()
        store.start()
    for store in stores:
        store.wait()


def hand_out(large, small):
    vmem = pl.BlockSpec(memory_space=pltpu.VMEM)
    hbm = pl.BlockSpec(memory_space=pl.ANY)
    vectors = [jax.ShapeDtypeStruct((24,), F32)] * 8 + [jax.ShapeDtypeStruct((96,), F32)]
    return pl.pallas_call(
        hand_out_kernel,
        out_shape=tuple([jax.ShapeDtypeStruct(v.shape, v.dtype) for v in large] + vectors),
        in_specs=[hbm] * 8 + [vmem],
        out_specs=tuple([hbm] * 8 + [vmem] * 9),
        scratch_shapes=[pltpu.VMEM(v.shape, v.dtype) for v in large]
        + [pltpu.SemaphoreType.DMA((8,)), pltpu.SemaphoreType.DMA((8,))],
        name="hand_out",
    )(*large, small)


def body(
    stride,
    hidden_in,
    page_lengths,
    pad_mask,
    query_weight,
    query_bias,
    key_weight,
    value_weight,
    value_bias,
    output_weight,
    output_bias,
    first_gain,
    first_shift,
    inner_weight,
    inner_bias,
    outer_weight,
    outer_bias,
    second_gain,
    second_shift,
    out_grad,
):
    coarse = partial(own_part, stride=stride)
    fine = partial(fine_part, stride=stride)
    weights = (query_weight, key_weight, value_weight, output_weight, inner_weight, outer_weight)
    vectors = (
        query_bias, value_bias, output_bias, first_gain, first_shift, outer_bias, second_gain, second_shift, inner_bias,
    )
    parts = [coarse(v) for v in weights + vectors]
    *large, dsmall, _ = layer_call(stride, (*parts, pad_mask, hidden_in, out_grad, page_lengths))
    output, input_grad, *grads = hand_out(large, dsmall)
    dq, dk, dv, do, di, du, qbg, vbg, obg, g1g, s1g, ubg, g2g, s2g, ibg = [fine(v) for v in grads]
    return (
        output, input_grad, dq, qbg, dk, dv, vbg, do, obg, g1g, s1g, di, ibg, du, ubg, g2g, s2g,
    )


def solution(mesh):
    stride = mesh.shape["dp"] // GROUP
    row = P(("dp", "blk"))
    mat = P(("dp", "blk"), None)
    tok = P("dp", "blk", None)
    in_specs = (
        tok, P("dp"), P("dp", "blk"), mat, row, mat, mat, row, mat, row, row, row, mat, row, mat, row, row, row, tok,
    )
    out_specs = (
        tok, tok, mat, row, mat, mat, row, mat, row, row, row, mat, row, mat, row, row, row,
    )
    return jax.shard_map(
        partial(body, stride), mesh=mesh, in_specs=in_specs, out_specs=out_specs, check_vma=False
    )
```
